512 devices in a mesh: chan: 32 (over z_lo, y, core), spec: 16 (over z_hi, x).
Axes of the slice: x: 4, y: 8, z: 8 (z_hi: 4, z_lo: 2; z = z_hi * 2 + z_lo), core: 2. Of those that a mesh axis runs over, the one named last changes fastest.
Arguments:
- record: bfloat16 [4096, 32, 1152], P('chan', 'spec'), may hold values from -6 to 6
- offsets: int32 [32], P('spec'), may hold values from 0 to 128
- sources: int32 [16], replicated, may hold values from 0 to 4095
Outputs:
- lagged: bfloat16 [512, 16, 4096], P('spec', None, 'chan')
The draws below stay inside these ranges and needn't reach their ends.
All inputs are finite; a program needn't handle non-finite values.
Results may differ from the reference program's by a relative error of at most 0.017.
Values may be sent and summed in bfloat16 or wider, within the bound.
A program may use at most 64 MiB of HBM per device.

```python
import math
import jax
import jax.numpy as jnp
from jax import lax

SAMPLES = 1024
PAD = 128
NSRC = 16
SEGMENT = 1152
CHANNELS = 4096
WINDOWS = 32


def with_ends(entries, key, least, top_value):
    spot = [jax.random.randint(jax.random.fold_in(key, axis), (), 0, length) for axis, length in enumerate(entries.shape)]
    widest = entries.shape.index(max(entries.shape))
    neighbour = spot[:widest] + [(spot[widest] + 1) % entries.shape[widest]] + spot[widest + 1:]
    return entries.at[tuple(spot)].set(least).at[tuple(neighbour)].set(top_value)


def shard_levels(own_key, shape, shards, smallest, largest):
    def one(axis_at, parts):
        steps = jax.random.uniform(jax.random.fold_in(jax.random.fold_in(own_key, 6), axis_at), (parts,), jnp.float32, smallest / len(shards), largest / len(shards))
        return jnp.repeat(jnp.exp(steps), shape[axis_at] // parts).reshape((-1,) + (1,) * (len(shape) - axis_at - 1))

    level = one(*shards[0])
    for cut in shards[1:]:
        level = level * one(*cut)
    return level


def normal_values(stream_key, extent, spread, bound, split=(), held_as=jnp.bfloat16):
    loudness = shard_levels(stream_key, extent, split, -0.22, 0.18) if split else 1.0
    result = jax.random.normal(stream_key, extent, jnp.float32) * spread * loudness
    return jnp.minimum(jnp.maximum(result, -bound), bound).astype(held_as)


def setup_inputs(seed: int = 0) -> dict:
    arg_keys = jax.random.split(jax.random.key(seed), 4)
    record = normal_values(arg_keys[0], (CHANNELS, WINDOWS, SEGMENT), 1.0, 6.0, ((0, 32), (1, 16)))
    offsets = with_ends(jax.random.randint(arg_keys[1], (WINDOWS,), 0, PAD + 1), jax.random.fold_in(arg_keys[1], 1), 0, PAD).astype(jnp.int32)
    sources = with_ends(jax.random.randint(arg_keys[2], (NSRC,), 0, CHANNELS), jax.random.fold_in(arg_keys[2], 1), 0, CHANNELS - 1).astype(jnp.int32)
    return {"record": record, "offsets": offsets, "sources": sources}


WATER = 0.1

def whiten_rows(real_part, imag_part):
    half = real_part.shape[-1]
    magnitude = jnp.sqrt(real_part * real_part + imag_part * imag_part)
    first = jnp.arange(half) == 0
    amp_real = jnp.where(first, jnp.abs(real_part), magnitude)
    amp_imag = jnp.where(first, jnp.abs(imag_part), magnitude)
    total = lax.optimization_barrier(jnp.sum(jnp.where(first, 0.0, magnitude), axis=-1, keepdims=True))
    total = total + jnp.abs(real_part[:, :1]) + jnp.abs(imag_part[:, :1])
    level = WATER * (total / (half + 1) + 1e-06)
    white_real = (real_part / (amp_real + level)).astype(jnp.bfloat16)
    white_imag = (imag_part / (amp_imag + level)).astype(jnp.bfloat16)
    return (white_real, white_imag)

def window_spectra(rows, start):
    half = SAMPLES // 2
    trace = lax.dynamic_slice_in_dim(rows, start, SAMPLES, 1).astype(jnp.float32)
    trace = trace - lax.optimization_barrier(jnp.mean(trace, axis=1, keepdims=True))
    trace = trace * lax.rsqrt(lax.optimization_barrier(jnp.mean(trace * trace, axis=1, keepdims=True)) + 1e-06)
    normed = lax.optimization_barrier(trace.astype(jnp.bfloat16)).astype(jnp.float32)
    coeffs = jnp.fft.rfft(normed, axis=1)
    real_all = jnp.real(coeffs)
    imag_all = jnp.imag(coeffs)
    packed_real = real_all[:, :half]
    packed_imag = jnp.concatenate([real_all[:, half:half + 1], imag_all[:, 1:half]], axis=1)
    return whiten_rows(packed_real, packed_imag)

def pair_product(left, right):
    return jnp.einsum('sk,ck->ksc', left.astype(jnp.float32), right.astype(jnp.float32))

def correlate_window(src_real, src_imag, rec_real, rec_imag):
    half = src_real.shape[-1]
    both_real = pair_product(src_real, rec_real)
    both_imag = pair_product(src_imag, rec_imag)
    cross_a = pair_product(src_real, rec_imag)
    cross_b = pair_product(src_imag, rec_real)
    first = (jnp.arange(half) == 0)[:, None, None]
    real_sum = both_real + jnp.where(first, 0.0, both_imag)
    imag_sum = jnp.where(first, both_imag, cross_a - cross_b)
    return jnp.stack([real_sum, imag_sum], axis=0)

def reference(record, offsets, sources):
    half = SAMPLES // 2

    def one_window(index, cross):
        rows = lax.dynamic_index_in_dim(record, index, 1, keepdims=False)
        start = lax.dynamic_index_in_dim(offsets, index, 0, keepdims=False)
        white_real, white_imag = window_spectra(rows, start)
        src_real = white_real[sources]
        src_imag = white_imag[sources]
        return cross + correlate_window(src_real, src_imag, white_real, white_imag)
    initial = jnp.zeros((2, half, NSRC, CHANNELS), jnp.float32)
    cross = lax.fori_loop(0, WINDOWS, one_window, initial)
    zero_row = jnp.zeros_like(cross[0, :1])
    real_full = jnp.concatenate([cross[0], cross[1, :1]], axis=0)
    imag_full = jnp.concatenate([zero_row, cross[1, 1:], zero_row], axis=0)
    values = jnp.fft.irfft(lax.complex(real_full, imag_full), n=SAMPLES, axis=0)
    lag_index = (jnp.arange(half) - half // 2) % SAMPLES
    lagged = values[lag_index] * math.sqrt(SAMPLES / WINDOWS)
    return lagged.astype(jnp.bfloat16)
```

```python
import functools
import math

import jax
import jax.numpy as jnp
import numpy as np
from jax import lax
from jax.experimental import pallas as pl
from jax.experimental.pallas import tpu as pltpu
from jax.sharding import PartitionSpec as P

SAMPLES = 1024
HALF = SAMPLES // 2
PAD = 128
NSRC = 16
WATER = 0.1
NX = 4
ROWS = 128
WIN = 2
BLK = ROWS // NX
GROUPS = 32
PIECES = 32
F32 = jnp.float32
BF16 = jnp.bfloat16
MESH = pl.DeviceIdType.MESH


def forward_tables():
    rows = np.arange(SAMPLES)[:, None]
    cols = np.arange(SAMPLES)[None, :]
    freq = rows % HALF
    angle = 2.0 * np.pi / SAMPLES * (freq * cols % SAMPLES)
    alternating = 1.0 - 2.0 * (cols % 2)
    imag = np.where(freq == 0, alternating, -np.sin(angle))
    table = np.where(rows < HALF, np.cos(angle), imag)
    upper = table.astype(jnp.bfloat16)
    lower = (table - upper.astype(np.float64)).astype(jnp.bfloat16)
    return upper, lower


def inverse_table(windows):
    shifted = np.arange(HALF)[:, None] - HALF // 2
    freq = (np.arange(16)[:, None] + 16 * np.arange(GROUPS)[None, :]).reshape(1, -1)
    angle = 2.0 * np.pi / SAMPLES * (freq * shifted % SAMPLES)
    alternating = 1.0 - 2.0 * (shifted % 2)
    first = freq == 0
    real = np.where(first, 1.0, 2.0 * np.cos(angle))
    imag = np.where(first, alternating, -2.0 * np.sin(angle))
    table = np.concatenate([real, imag], axis=1) / math.sqrt(windows * SAMPLES)
    return table.astype(jnp.bfloat16)


def spread_table():
    table = np.zeros((4, BLK, 4, 4, BLK))
    for quarter in range(4):
        for copy in range(4):
            table[quarter, np.arange(BLK), quarter, copy, np.arange(BLK)] = 1.0
    return table.reshape(128, 512).astype(jnp.bfloat16)


def diagonal_mask():
    mask = np.zeros((16, 16, BLK))
    mask[np.arange(16), np.arange(16)] = 1.0
    return mask.reshape(16, 512).astype(jnp.bfloat16)


def dot_t(left, right):
    return lax.dot_general(left, right, (((1,), (1,)), ((), ())), preferred_element_type=F32)


def dot(left, right):
    return lax.dot_general(left, right, (((1,), (0,)), ((), ())), preferred_element_type=F32)


def block_transpose(parts):
    count = len(parts)
    lane = lax.broadcasted_iota(jnp.int32, parts[0].shape, 1)
    step = count // 2
    while step:
        width = step * 128 // count
        low = (lane // width) % 2 == 0
        done = list(parts)
        for i in range(count):
            if (i // step) % 2 == 0:
                a, b = parts[i], parts[i + step]
                done[i] = jnp.where(low, a, pltpu.roll(b, width, 1))
                done[i + step] = jnp.where(low, pltpu.roll(a, 128 - width, 1), b)
        parts = done
        step //= 2
    return parts


def kernel(
    nchan,
    nz,
    offsets,
    sources,
    record,
    upper,
    lower,
    inverse,
    spread,
    mask,
    out,
    traces,
    pieces,
    reduced,
    gathered_x,
    piece_out,
    picked,
    spectrum,
    outgoing,
    incoming,
    left,
    copies,
    cross,
    stacked,
    lags_out,
    lags_in,
    finished,
    last,
    reduce_send,
    reduce_recv,
    x_send,
    x_recv,
    chan_send,
    chan_recv,
    white_send,
    white_recv,
    z_send,
    z_recv,
    last_send,
    last_recv,
):
    chan = lax.axis_index("chan")
    spec = lax.axis_index("spec")
    me_x = lax.rem(spec, NX)
    me_z = spec // NX
    per = PIECES // nchan
    lag_rows = HALF // nz

    def at_x(other):
        return (chan, me_z * NX + other)

    def at_z(other):
        return (chan, other * NX + me_x)

    barrier = pltpu.get_barrier_semaphore()

    @pl.loop(1, nchan)
    def _(step):
        pl.semaphore_signal(
            barrier, inc=1, device_id=(lax.rem(chan + step, nchan), spec), device_id_type=MESH
        )

    @pl.loop(1, NX)
    def _(step):
        pl.semaphore_signal(
            barrier, inc=1, device_id=at_x(lax.rem(me_x + step, NX)), device_id_type=MESH
        )

    @pl.loop(1, nz)
    def _(step):
        pl.semaphore_signal(
            barrier, inc=1, device_id=at_z(lax.rem(me_z + step, nz)), device_id_type=MESH
        )

    lane = lax.broadcasted_iota(jnp.int32, (ROWS, 128), 1)
    for w in range(WIN):
        rows = record[w].astype(F32)
        head = jnp.where(lane < offsets[w], rows[:, SAMPLES:], rows[:, :PAD])
        rows = jnp.concatenate([head, rows[:, PAD:SAMPLES]], axis=1)
        rows = rows - jnp.mean(rows, axis=1, keepdims=True)
        rows = rows * lax.rsqrt(jnp.mean(rows * rows, axis=1, keepdims=True) + 1e-06)
        rows = rows.astype(BF16)
        for x in range(NX):
            traces[pl.ds(x * 64 + w * BLK, BLK), :] = rows[x * BLK : (x + 1) * BLK]

    row = lax.broadcasted_iota(jnp.int32, (32, 256), 0)
    col = lax.broadcasted_iota(jnp.int32, (32, 256), 1)
    wanted = jnp.zeros((32, 256), jnp.int32)
    for s in range(NSRC):
        wanted = jnp.where(row % NSRC == s, sources[s], wanted)
    channel = chan * ROWS + (col // 64) * BLK + col % BLK
    same = jnp.logical_and(wanted == channel, row // NSRC == (col // BLK) % 2)
    chosen = dot(jnp.where(same, 1.0, 0.0).astype(BF16), traces[...])
    for j in range(PIECES):
        r, l = j // 8, j % 8
        pieces[j] = chosen[8 * r : 8 * r + 8, 128 * l : 128 * l + 128]

    pl.semaphore_wait(barrier, nchan - 1 + NX - 1 + nz - 1)

    def reduce_copy(to, slot):
        return pltpu.make_async_remote_copy(
            src_ref=pieces.at[pl.ds(to * per, per)],
            dst_ref=reduced.at[slot],
            send_sem=reduce_send.at[to],
            recv_sem=reduce_recv.at[slot],
            device_id=(to, spec),
            device_id_type=MESH,
        )

    @pl.loop(1, nchan)
    def _(step):
        reduce_copy(lax.rem(chan + step, nchan), chan).start()

    reduced[chan] = pieces[pl.ds(chan * per, per)]

    spectrum[...] = dot_t(upper[...], traces[...])
    spectrum[...] += dot_t(lower[...], traces[...])

    @pl.loop(1, nchan)
    def _(step):
        reduce_copy(chan, lax.rem(chan + step, nchan)).wait_recv()

    total = reduced[0]
    for i in range(1, nchan):
        total = total + reduced[i]
    gathered_x[me_x] = total

    def x_copy(to, slot):
        return pltpu.make_async_remote_copy(
            src_ref=gathered_x.at[me_x],
            dst_ref=gathered_x.at[slot],
            send_sem=x_send.at[to],
            recv_sem=x_recv.at[slot],
            device_id=at_x(to),
            device_id_type=MESH,
        )

    for step in (2, 1, 3):
        x_copy(lax.rem(me_x + step, NX), me_x).start()

    chunk = 64
    first_row = lax.broadcasted_iota(jnp.int32, (chunk, 256), 0) == 0
    total = jnp.zeros((1, 256), F32)
    for k in range(0, HALF, chunk):
        re = spectrum[k : k + chunk]
        im = spectrum[HALF + k : HALF + k + chunk]
        size = jnp.sqrt(re * re + im * im)
        if k == 0:
            size = jnp.where(first_row, jnp.abs(re) + jnp.abs(im), size)
        total = total + jnp.sum(size, axis=0, keepdims=True)
    level = WATER * (total / (HALF + 1) + 1e-06)
    low = lax.broadcasted_iota(jnp.int32, (chunk, 128), 1) < 64
    for k in range(0, HALF, chunk):
        re = spectrum[k : k + chunk]
        im = spectrum[HALF + k : HALF + k + chunk]
        size = jnp.sqrt(re * re + im * im)
        if k == 0:
            re = re / (jnp.where(first_row, jnp.abs(re), size) + level)
            im = im / (jnp.where(first_row, jnp.abs(im), size) + level)
        else:
            scale = 1.0 / (size + level)
            re = re * scale
            im = im * scale
        for pair in range(2):
            a = re[:, 128 * pair : 128 * pair + 128]
            b = im[:, 128 * pair : 128 * pair + 128]
            even = jnp.where(low, a, pltpu.roll(b, 64, 1))
            odd = jnp.where(low, pltpu.roll(a, 64, 1), b)
            outgoing[2 * pair, k : k + chunk] = even.astype(BF16)
            outgoing[2 * pair + 1, k : k + chunk] = odd.astype(BF16)

    def white_copy(to, slot):
        return pltpu.make_async_remote_copy(
            src_ref=outgoing.at[to],
            dst_ref=incoming.at[slot],
            send_sem=white_send.at[to],
            recv_sem=white_recv.at[slot],
            device_id=at_x(to),
            device_id_type=MESH,
        )

    for step in (2, 1, 3):
        white_copy(lax.rem(me_x + step, NX), me_x).start()
    incoming[me_x] = outgoing[me_x]

    for step in (2, 1, 3):
        x_copy(me_x, lax.rem(me_x + step, NX)).wait_recv()
    for j in range(per):
        tall = jnp.concatenate([gathered_x[x, j] for x in range(NX)], axis=0)
        piece_out[j] = tall.astype(BF16)

    def chan_copy(to, slot):
        return pltpu.make_async_remote_copy(
            src_ref=piece_out,
            dst_ref=picked.at[pl.ds(slot * per, per)],
            send_sem=chan_send.at[to],
            recv_sem=chan_recv.at[slot],
            device_id=(to, spec),
            device_id_type=MESH,
        )

    @pl.loop(1, nchan)
    def _(step):
        chan_copy(lax.rem(chan + step, nchan), chan).start()

    picked[pl.ds(chan * per, per)] = piece_out[...]

    def widen(x):
        copies[x] = dot(incoming[x], spread[...]).astype(BF16)

    @pl.loop(1, nchan)
    def _(step):
        chan_copy(chan, lax.rem(chan + step, nchan)).wait_recv()

    rows = [
        jnp.concatenate([picked[8 * r + l] for l in range(8)], axis=1) for r in range(4)
    ]
    rows = jnp.concatenate(rows, axis=0)
    both = dot_t(rows, upper[...]) + dot_t(rows, lower[...])
    re = both[:, :HALF]
    im = both[:, HALF:]
    size = jnp.sqrt(re * re + im * im)
    first = lax.broadcasted_iota(jnp.int32, (ROWS, HALF), 1) == 0
    total = jnp.sum(
        jnp.where(first, jnp.abs(re) + jnp.abs(im), size), axis=1, keepdims=True
    )
    level = WATER * (total / (HALF + 1) + 1e-06)
    re = re / (jnp.where(first, jnp.abs(re), size) + level)
    im = im / (jnp.where(first, jnp.abs(im), size) + level)
    parts = []
    for x in range(NX):
        for w in range(WIN):
            tiles = []
            for half in (re, im):
                for big in range(4):
                    for high in range(2):
                        at = 8 * (w * 8 + high * 4 + x)
                        tiles.append(half[at : at + 8, 128 * big : 128 * big + 128])
            parts.append(jnp.concatenate(tiles, axis=0))
    parts = block_transpose(parts)
    for small in range(8):
        a_re = parts[small][:64]
        a_im = parts[small][64:]
        re_b0, re_b1, im_b0, im_b1 = a_re, a_im, -a_im, a_re
        if small == 0:
            shape = (64, 128)
            zero_bin = jnp.logical_and(
                lax.broadcasted_iota(jnp.int32, shape, 0) < 16,
                lax.broadcasted_iota(jnp.int32, shape, 1) % 16 == 0,
            )
            re_b1 = jnp.where(zero_bin, 0.0, re_b1)
            im_b0 = jnp.where(zero_bin, 0.0, im_b0)
            im_b1 = jnp.where(zero_bin, a_im, im_b1)
        left[small, 0, 0] = re_b0.astype(BF16)
        left[small, 0, 1] = re_b1.astype(BF16)
        left[small, 1, 0] = im_b0.astype(BF16)
        left[small, 1, 1] = im_b1.astype(BF16)

    for step in (2, 1, 3):
        white_copy(me_x, lax.rem(me_x + step, NX)).wait_recv()
    for x in range(NX):
        widen(x)

    @pl.loop(0, 8)
    def _(small):
        for big in range(4):
            group = big * 8 + small
            at = pl.ds(pl.multiple_of(group * 16, 16), 16)
            slabs = []
            for p in range(2):
                for x in range(NX):
                    for w in range(WIN):
                        quarter = p * 2 + w
                        tile = copies[x, at, quarter * 128 : quarter * 128 + 128]
                        slabs.append(
                            jnp.concatenate([tile] * 4, axis=1) * mask[...]
                        )
            right = jnp.concatenate(slabs, axis=0)
            rows_left = jnp.concatenate(
                [
                    jnp.concatenate(
                        [left[small, part, p, big * 16 : big * 16 + 16, :] for p in range(2)],
                        axis=1,
                    )
                    for part in range(2)
                ],
                axis=0,
            )
            result = dot(rows_left, right)
            for h in range(4):
                cross[h, pl.ds(group, 32, stride=32), :] = result[:, 128 * h : 128 * h + 128]

    for part in range(2):
        for quad in range(4):
            for h in range(4):
                parts = [
                    cross[h, pl.ds((part * 16 + quad * 4 + i) * 32, 32), :] for i in range(4)
                ]
                parts = block_transpose(parts)
                for j in range(4):
                    at = (part * 16 + h * 4 + j) * 32
                    stacked[at : at + 32, 128 * quad : 128 * quad + 128] = parts[j].astype(BF16)

    def z_copy(step, to, slot):
        return pltpu.make_async_remote_copy(
            src_ref=lags_out.at[step],
            dst_ref=lags_in.at[slot],
            send_sem=z_send.at[step],
            recv_sem=z_recv.at[slot],
            device_id=at_z(to),
            device_id_type=MESH,
        )

    def lag_block(to):
        at = pl.ds(pl.multiple_of(to * lag_rows, lag_rows), lag_rows)
        return dot(inverse[at, :], stacked[...])

    z_steps = sorted(range(1, nz), key=lambda step: -min(step, nz - step))
    for step in z_steps:
        to = lax.rem(me_z + step, nz)
        lags_out[step] = lag_block(to).astype(BF16)
        z_copy(step, to, me_z).start()
    total = lag_block(me_z)
    for step in z_steps[::-1]:
        slot = lax.rem(me_z + step, nz)
        z_copy(step, me_z, slot).wait_recv()
        total = total + lags_in[slot].astype(F32)
    finished[...] = total.astype(BF16)

    own = lag_rows // NX

    def last_copy(to, slot):
        at = pl.ds(pl.multiple_of(to * own, own), own)
        return pltpu.make_async_remote_copy(
            src_ref=finished.at[at],
            dst_ref=last.at[slot],
            send_sem=last_send.at[to],
            recv_sem=last_recv.at[slot],
            device_id=at_x(to),
            device_id_type=MESH,
        )

    for step in (2, 1, 3):
        last_copy(lax.rem(me_x + step, NX), me_x).start()
    last[me_x] = finished[pl.ds(pl.multiple_of(me_x * own, own), own), :]
    for step in (1, 3, 2):
        last_copy(me_x, lax.rem(me_x + step, NX)).wait_recv()
    for quad in range(4):
        parts = [
            last[x, :, 128 * quad : 128 * quad + 128].astype(F32) for x in range(NX)
        ]
        parts = block_transpose(parts)
        for j in range(4):
            s = quad * 4 + j
            out[:, 128 * s : 128 * s + 128] = parts[j].astype(BF16)

    @pl.loop(1, nchan)
    def _(step):
        to = lax.rem(chan + step, nchan)
        reduce_copy(to, chan).wait_send()
        chan_copy(to, chan).wait_send()

    for step in (1, 2, 3):
        to = lax.rem(me_x + step, NX)
        x_copy(to, me_x).wait_send()
        white_copy(to, me_x).wait_send()
        last_copy(to, me_x).wait_send()
    for step in z_steps:
        z_copy(step, lax.rem(me_z + step, nz), me_z).wait_send()


def local(nchan, nz, record, offsets, sources):
    lag_rows = HALF // nz
    own = lag_rows // NX
    per = PIECES // nchan
    upper, lower = forward_tables()
    inverse = inverse_table(nz * NX * WIN)
    vmem = pl.BlockSpec(memory_space=pltpu.VMEM)
    smem = pl.BlockSpec(memory_space=pltpu.SMEM)
    dma = pltpu.SemaphoreType.DMA
    flat = pl.pallas_call(
        functools.partial(kernel, nchan, nz),
        out_shape=jax.ShapeDtypeStruct((own, NSRC * ROWS), BF16),
        in_specs=[smem, smem] + [vmem] * 6,
        out_specs=vmem,
        scratch_shapes=[
            pltpu.VMEM((256, SAMPLES), BF16),
            pltpu.VMEM((PIECES, 8, 128), F32),
            pltpu.VMEM((nchan, per, 8, 128), F32),
            pltpu.VMEM((NX, per, 8, 128), F32),
            pltpu.VMEM((per, 32, 128), BF16),
            pltpu.VMEM((PIECES, 32, 128), BF16),
            pltpu.VMEM((SAMPLES, 256), F32),
            pltpu.VMEM((NX, HALF, 128), BF16),
            pltpu.VMEM((NX, HALF, 128), BF16),
            pltpu.VMEM((8, 2, 2, 64, 128), BF16),
            pltpu.VMEM((NX, HALF, 512), BF16),
            pltpu.VMEM((4, SAMPLES, 128), F32),
            pltpu.VMEM((SAMPLES, 512), BF16),
            pltpu.VMEM((nz, lag_rows, 512), BF16),
            pltpu.VMEM((nz, lag_rows, 512), BF16),
            pltpu.VMEM((lag_rows, 512), BF16),
            pltpu.VMEM((NX, own, 512), BF16),
            dma((nchan,)),
            dma((nchan,)),
            dma((NX,)),
            dma((NX,)),
            dma((nchan,)),
            dma((nchan,)),
            dma((NX,)),
            dma((NX,)),
            dma((nz,)),
            dma((nz,)),
            dma((NX,)),
            dma((NX,)),
        ],
        compiler_params=pltpu.CompilerParams(
            collective_id=0, has_side_effects=True, vmem_limit_bytes=48 * 1024 * 1024
        ),
        cost_estimate=pl.CostEstimate(
            flops=3 * 10**9, bytes_accessed=7 * 10**6, transcendentals=10**6
        ),
    )(
        offsets,
        sources,
        jnp.transpose(record, (1, 0, 2)),
        jnp.asarray(upper),
        jnp.asarray(lower),
        jnp.asarray(inverse),
        jnp.asarray(spread_table()),
        jnp.asarray(diagonal_mask()),
    )
    return flat.reshape(own, NSRC, ROWS)


def solution(mesh):
    nchan = mesh.shape["chan"]
    nz = mesh.shape["spec"] // NX
    in_specs = (P("chan", "spec", None), P("spec"), P())
    out_specs = P("spec", None, "chan")
    return jax.shard_map(
        functools.partial(local, nchan, nz),
        mesh=mesh,
        in_specs=in_specs,
        out_specs=out_specs,
        check_vma=False,
    )
```

```python
import functools
import math

import jax
import jax.numpy as jnp
import numpy as np
from jax import lax
from jax.experimental import pallas as pl
from jax.experimental.pallas import tpu as pltpu
from jax.sharding import PartitionSpec as P

SAMPLES = 1024
HALF = SAMPLES // 2
PAD = 128
NSRC = 16
WATER = 0.1
NX = 4
ROWS = 128
WIN = 2
BLK = ROWS // NX
GROUPS = 32
LANES = SAMPLES // 128
F32 = jnp.float32
BF16 = jnp.bfloat16
MESH = pl.DeviceIdType.MESH


def forward_tables():
    rows = np.arange(SAMPLES)[:, None]
    cols = np.arange(SAMPLES)[None, :]
    freq = rows % HALF
    angle = 2.0 * np.pi / SAMPLES * (freq * cols % SAMPLES)
    alternating = 1.0 - 2.0 * (cols % 2)
    imag = np.where(freq == 0, alternating, -np.sin(angle))
    table = np.where(rows < HALF, np.cos(angle), imag)
    upper = table.astype(jnp.bfloat16)
    lower = (table - upper.astype(np.float64)).astype(jnp.bfloat16)
    return upper, lower


def inverse_table(windows):
    shifted = np.arange(HALF)[:, None] - HALF // 2
    freq = (np.arange(16)[:, None] + 16 * np.arange(GROUPS)[None, :]).reshape(1, -1)
    angle = 2.0 * np.pi / SAMPLES * (freq * shifted % SAMPLES)
    alternating = 1.0 - 2.0 * (shifted % 2)
    first = freq == 0
    real = np.where(first, 1.0, 2.0 * np.cos(angle))
    imag = np.where(first, alternating, -2.0 * np.sin(angle))
    table = np.concatenate([real, imag], axis=1) / math.sqrt(windows * SAMPLES)
    return table.astype(jnp.bfloat16)


def split_chan(nchan):
    nlow = 2 if nchan >= 8 else 1
    return nlow, nchan // (2 * nlow)


def dot_t(left, right):
    return lax.dot_general(left, right, (((1,), (1,)), ((), ())), preferred_element_type=F32)


def dot(left, right):
    return lax.dot_general(left, right, (((1,), (0,)), ((), ())), preferred_element_type=F32)


def block_transpose(parts):
    count = len(parts)
    lane = lax.broadcasted_iota(jnp.int32, parts[0].shape, 1)
    step = count // 2
    while step:
        width = step * 128 // count
        low = (lane // width) % 2 == 0
        done = list(parts)
        for i in range(count):
            if (i // step) % 2 == 0:
                a, b = parts[i], parts[i + step]
                done[i] = jnp.where(low, a, pltpu.roll(b, width, 1))
                done[i + step] = jnp.where(low, pltpu.roll(a, 128 - width, 1), b)
        parts = done
        step //= 2
    return parts


def kernel(
    nchan,
    nz,
    offsets_hbm,
    sources_hbm,
    record,
    upper_hbm,
    lower_hbm,
    inverse_hbm,
    out,
    offsets,
    sources,
    upper,
    lower,
    inverse,
    traces,
    pieces,
    reduced,
    gathered,
    piece_out,
    picked,
    spectrum,
    outgoing,
    incoming,
    left,
    copies,
    cross,
    stacked,
    lags_out,
    lags_in,
    finished,
    last,
    load_sem,
    reduce_send,
    reduce_recv,
    side_send,
    side_recv,
    y_send,
    y_recv,
    core_send,
    core_recv,
    white_send,
    white_recv,
    z_send,
    z_recv,
    last_send,
    last_recv,
):
    nlow, ny = split_chan(nchan)
    per = LANES // ny
    lag_rows = HALF // nz
    plane = 2 * ny
    side = nlow * NX
    chan = lax.axis_index("chan")
    spec = lax.axis_index("spec")
    me_x = lax.rem(spec, NX)
    me_z = spec // NX
    me_low = chan // plane
    me_plane = lax.rem(chan, plane)
    me_y = me_plane // 2
    me_core = lax.rem(chan, 2)
    me_side = me_low * NX + me_x

    def at_plane(other):
        return (me_low * plane + other, spec)

    def at_side(other):
        return (other // NX * plane + me_plane, me_z * NX + lax.rem(other, NX))

    def at_x(other):
        return (chan, me_z * NX + other)

    def at_z(other):
        return (chan, other * NX + me_x)

    loads = [
        pltpu.make_async_copy(source, target, load_sem.at[i])
        for i, (source, target) in enumerate(
            [
                (offsets_hbm, offsets),
                (sources_hbm, sources),
                (upper_hbm, upper),
                (lower_hbm, lower),
                (inverse_hbm, inverse),
            ]
        )
    ]
    for load in loads:
        load.start()

    barrier = pltpu.get_barrier_semaphore()

    @pl.loop(1, plane)
    def _(step):
        pl.semaphore_signal(
            barrier, inc=1, device_id=at_plane(lax.rem(me_plane + step, plane)), device_id_type=MESH
        )

    @pl.loop(1, side)
    def _(step):
        pl.semaphore_signal(
            barrier, inc=1, device_id=at_side(lax.rem(me_side + step, side)), device_id_type=MESH
        )

    @pl.loop(1, nz)
    def _(step):
        pl.semaphore_signal(
            barrier, inc=1, device_id=at_z(lax.rem(me_z + step, nz)), device_id_type=MESH
        )

    loads[0].wait()
    loads[1].wait()

    lane = lax.broadcasted_iota(jnp.int32, (ROWS, 128), 1)
    for w in range(WIN):
        rows = record[w].astype(F32)
        head = jnp.where(lane < offsets[w], rows[:, SAMPLES:], rows[:, :PAD])
        rows = jnp.concatenate([head, rows[:, PAD:SAMPLES]], axis=1)
        rows = rows - jnp.mean(rows, axis=1, keepdims=True)
        rows = rows * lax.rsqrt(jnp.mean(rows * rows, axis=1, keepdims=True) + 1e-06)
        rows = rows.astype(BF16)
        for x in range(NX):
            traces[pl.ds(x * 64 + w * BLK, BLK), :] = rows[x * BLK : (x + 1) * BLK]

    row = lax.broadcasted_iota(jnp.int32, (32, 256), 0)
    col = lax.broadcasted_iota(jnp.int32, (32, 256), 1)
    wanted = jnp.zeros((32, 256), jnp.int32)
    for s in range(NSRC):
        wanted = jnp.where(row % NSRC == s, sources[s], wanted)
    channel = chan * ROWS + (col // 64) * BLK + col % BLK
    same = jnp.logical_and(wanted == channel, row // NSRC == (col // BLK) % 2)
    chosen = dot(jnp.where(same, 1.0, 0.0).astype(BF16), traces[...])
    chosen = chosen.astype(BF16)
    for w in range(WIN):
        for l in range(LANES):
            pieces[w, l] = chosen[NSRC * w : NSRC * w + NSRC, 128 * l : 128 * l + 128]

    pl.semaphore_wait(barrier, plane - 1 + side - 1 + nz - 1)

    def reduce_copy(to, slot):
        return pltpu.make_async_remote_copy(
            src_ref=pieces.at[lax.rem(to, 2), pl.ds(to // 2 * per, per)],
            dst_ref=reduced.at[slot],
            send_sem=reduce_send.at[to],
            recv_sem=reduce_recv.at[slot],
            device_id=at_plane(to),
            device_id_type=MESH,
        )

    @pl.loop(1, plane)
    def _(step):
        reduce_copy(lax.rem(me_plane + step, plane), me_plane).start()

    reduced[me_plane] = pieces[me_core, pl.ds(me_y * per, per)]
    loads[2].wait()
    loads[3].wait()

    spectrum[...] = dot_t(upper[...], traces[...])
    spectrum[...] += dot_t(lower[...], traces[...])

    @pl.loop(1, plane)
    def _(step):
        reduce_copy(me_plane, lax.rem(me_plane + step, plane)).wait_recv()

    total = reduced[0].astype(F32)
    for i in range(1, plane):
        total = total + reduced[i].astype(F32)
    gathered[me_side] = total.astype(BF16)

    def side_copy(to, slot):
        return pltpu.make_async_remote_copy(
            src_ref=gathered.at[me_side],
            dst_ref=gathered.at[slot],
            send_sem=side_send.at[to],
            recv_sem=side_recv.at[slot],
            device_id=at_side(to),
            device_id_type=MESH,
        )

    @pl.loop(1, side)
    def _(step):
        side_copy(lax.rem(me_side + step, side), me_side).start()

    chunk = 64
    first_row = lax.broadcasted_iota(jnp.int32, (chunk, 256), 0) == 0
    total = jnp.zeros((1, 256), F32)
    for k in range(0, HALF, chunk):
        re = spectrum[k : k + chunk]
        im = spectrum[HALF + k : HALF + k + chunk]
        size = jnp.sqrt(re * re + im * im)
        if k == 0:
            size = jnp.where(first_row, jnp.abs(re) + jnp.abs(im), size)
        total = total + jnp.sum(size, axis=0, keepdims=True)
    level = WATER * (total / (HALF + 1) + 1e-06)
    low = lax.broadcasted_iota(jnp.int32, (chunk, 128), 1) < 64
    for k in range(0, HALF, chunk):
        re = spectrum[k : k + chunk]
        im = spectrum[HALF + k : HALF + k + chunk]
        size = jnp.sqrt(re * re + im * im)
        if k == 0:
            re = re / (jnp.where(first_row, jnp.abs(re), size) + level)
            im = im / (jnp.where(first_row, jnp.abs(im), size) + level)
        else:
            scale = 1.0 / (size + level)
            re = re * scale
            im = im * scale
        for pair in range(2):
            a = re[:, 128 * pair : 128 * pair + 128]
            b = im[:, 128 * pair : 128 * pair + 128]
            even = jnp.where(low, a, pltpu.roll(b, 64, 1))
            odd = jnp.where(low, pltpu.roll(a, 64, 1), b)
            outgoing[2 * pair, k : k + chunk] = even.astype(BF16)
            outgoing[2 * pair + 1, k : k + chunk] = odd.astype(BF16)

    def white_copy(to, slot):
        return pltpu.make_async_remote_copy(
            src_ref=outgoing.at[to],
            dst_ref=incoming.at[slot],
            send_sem=white_send.at[to],
            recv_sem=white_recv.at[slot],
            device_id=at_x(to),
            device_id_type=MESH,
        )

    for step in (2, 1, 3):
        white_copy(lax.rem(me_x + step, NX), me_x).start()
    incoming[me_x] = outgoing[me_x]

    @pl.loop(1, side)
    def _(step):
        side_copy(me_side, lax.rem(me_side + step, side)).wait_recv()

    for l in range(per):
        for x in range(NX):
            total = gathered[x, l].astype(F32)
            for low_z in range(1, nlow):
                total = total + gathered[low_z * NX + x, l].astype(F32)
            piece_out[l, NSRC * x : NSRC * x + NSRC] = total.astype(BF16)

    def y_copy(to, slot):
        return pltpu.make_async_remote_copy(
            src_ref=piece_out,
            dst_ref=picked.at[me_core, pl.ds(slot * per, per)],
            send_sem=y_send.at[to],
            recv_sem=y_recv.at[slot],
            device_id=at_plane(to * 2 + me_core),
            device_id_type=MESH,
        )

    def core_copy(core, slot):
        at = picked.at[core, pl.ds(slot * per, per)]
        return pltpu.make_async_remote_copy(
            src_ref=at,
            dst_ref=at,
            send_sem=core_send.at[slot],
            recv_sem=core_recv.at[slot],
            device_id=at_plane(me_y * 2 + 1 - me_core),
            device_id_type=MESH,
        )

    @pl.loop(1, ny)
    def _(step):
        y_copy(lax.rem(me_y + step, ny), me_y).start()

    picked[me_core, pl.ds(me_y * per, per)] = piece_out[...]
    core_copy(me_core, me_y).start()

    @pl.loop(1, ny)
    def _(step):
        slot = lax.rem(me_y + step, ny)
        y_copy(me_y, slot).wait_recv()
        core_copy(me_core, slot).start()

    r = lax.broadcasted_iota(jnp.int32, (128, 512), 0)
    c = lax.broadcasted_iota(jnp.int32, (128, 512), 1)
    match = jnp.logical_and(r // BLK == c // 128, r % BLK == c % BLK)
    spread = jnp.where(match, 1.0, 0.0).astype(BF16)
    r = lax.broadcasted_iota(jnp.int32, (16, 512), 0)
    c = lax.broadcasted_iota(jnp.int32, (16, 512), 1)
    mask = jnp.where(r == c // BLK, 1.0, 0.0).astype(BF16)

    def widen(x):
        copies[x] = dot(incoming[x], spread).astype(BF16)

    @pl.loop(0, ny)
    def _(slot):
        core_copy(1 - me_core, slot).wait_recv()

    rows = [
        jnp.concatenate([picked[w, l] for l in range(LANES)], axis=1) for w in range(WIN)
    ]
    rows = jnp.concatenate(rows, axis=0)
    both = dot_t(rows, upper[...]) + dot_t(rows, lower[...])
    re = both[:, :HALF]
    im = both[:, HALF:]
    size = jnp.sqrt(re * re + im * im)
    first = lax.broadcasted_iota(jnp.int32, (ROWS, HALF), 1) == 0
    total = jnp.sum(
        jnp.where(first, jnp.abs(re) + jnp.abs(im), size), axis=1, keepdims=True
    )
    level = WATER * (total / (HALF + 1) + 1e-06)
    re = re / (jnp.where(first, jnp.abs(re), size) + level)
    im = im / (jnp.where(first, jnp.abs(im), size) + level)
    parts = []
    for x in range(NX):
        for w in range(WIN):
            tiles = []
            for half in (re, im):
                for big in range(4):
                    at = NSRC * (w * NX + x)
                    tiles.append(half[at : at + NSRC, 128 * big : 128 * big + 128])
            parts.append(jnp.concatenate(tiles, axis=0))
    parts = block_transpose(parts)
    for small in range(8):
        a_re = parts[small][:64]
        a_im = parts[small][64:]
        re_b0, re_b1, im_b0, im_b1 = a_re, a_im, -a_im, a_re
        if small == 0:
            shape = (64, 128)
            zero_bin = jnp.logical_and(
                lax.broadcasted_iota(jnp.int32, shape, 0) < 16,
                lax.broadcasted_iota(jnp.int32, shape, 1) % 16 == 0,
            )
            re_b1 = jnp.where(zero_bin, 0.0, re_b1)
            im_b0 = jnp.where(zero_bin, 0.0, im_b0)
            im_b1 = jnp.where(zero_bin, a_im, im_b1)
        left[small, 0, 0] = re_b0.astype(BF16)
        left[small, 0, 1] = re_b1.astype(BF16)
        left[small, 1, 0] = im_b0.astype(BF16)
        left[small, 1, 1] = im_b1.astype(BF16)

    for step in (2, 1, 3):
        white_copy(me_x, lax.rem(me_x + step, NX)).wait_recv()
    for x in range(NX):
        widen(x)

    @pl.loop(0, 8)
    def _(small):
        for big in range(4):
            group = big * 8 + small
            at = pl.ds(pl.multiple_of(group * 16, 16), 16)
            slabs = []
            for p in range(2):
                for x in range(NX):
                    for w in range(WIN):
                        quarter = p * 2 + w
                        tile = copies[x, at, quarter * 128 : quarter * 128 + 128]
                        slabs.append(
                            jnp.concatenate([tile] * 4, axis=1) * mask
                        )
            right = jnp.concatenate(slabs, axis=0)
            rows_left = jnp.concatenate(
                [
                    jnp.concatenate(
                        [left[small, part, p, big * 16 : big * 16 + 16, :] for p in range(2)],
                        axis=1,
                    )
                    for part in range(2)
                ],
                axis=0,
            )
            result = dot(rows_left, right)
            for h in range(4):
                cross[h, pl.ds(group, 32, stride=32), :] = result[:, 128 * h : 128 * h + 128]

    for part in range(2):
        for quad in range(4):
            for h in range(4):
                parts = [
                    cross[h, pl.ds((part * 16 + quad * 4 + i) * 32, 32), :] for i in range(4)
                ]
                parts = block_transpose(parts)
                for j in range(4):
                    at = (part * 16 + h * 4 + j) * 32
                    stacked[at : at + 32, 128 * quad : 128 * quad + 128] = parts[j].astype(BF16)

    loads[4].wait()

    def z_copy(step, to, slot):
        return pltpu.make_async_remote_copy(
            src_ref=lags_out.at[step],
            dst_ref=lags_in.at[slot],
            send_sem=z_send.at[step],
            recv_sem=z_recv.at[slot],
            device_id=at_z(to),
            device_id_type=MESH,
        )

    def lag_block(to):
        at = pl.ds(pl.multiple_of(to * lag_rows, lag_rows), lag_rows)
        return dot(inverse[at, :], stacked[...])

    z_steps = sorted(range(1, nz), key=lambda step: -min(step, nz - step))
    for step in z_steps:
        to = lax.rem(me_z + step, nz)
        lags_out[step] = lag_block(to).astype(BF16)
        z_copy(step, to, me_z).start()
    total = lag_block(me_z)
    for step in z_steps[::-1]:
        slot = lax.rem(me_z + step, nz)
        z_copy(step, me_z, slot).wait_recv()
        total = total + lags_in[slot].astype(F32)
    finished[...] = total.astype(BF16)

    own = lag_rows // NX

    def last_copy(to, slot):
        at = pl.ds(pl.multiple_of(to * own, own), own)
        return pltpu.make_async_remote_copy(
            src_ref=finished.at[at],
            dst_ref=last.at[slot],
            send_sem=last_send.at[to],
            recv_sem=last_recv.at[slot],
            device_id=at_x(to),
            device_id_type=MESH,
        )

    for step in (2, 1, 3):
        last_copy(lax.rem(me_x + step, NX), me_x).start()
    last[me_x] = finished[pl.ds(pl.multiple_of(me_x * own, own), own), :]
    for step in (1, 3, 2):
        last_copy(me_x, lax.rem(me_x + step, NX)).wait_recv()
    for quad in range(4):
        parts = [
            last[x, :, 128 * quad : 128 * quad + 128].astype(F32) for x in range(NX)
        ]
        parts = block_transpose(parts)
        for j in range(4):
            s = quad * 4 + j
            out[:, 128 * s : 128 * s + 128] = parts[j].astype(BF16)

    @pl.loop(1, plane)
    def _(step):
        reduce_copy(lax.rem(me_plane + step, plane), me_plane).wait_send()

    @pl.loop(1, side)
    def _(step):
        side_copy(lax.rem(me_side + step, side), me_side).wait_send()

    @pl.loop(1, ny)
    def _(step):
        y_copy(lax.rem(me_y + step, ny), me_y).wait_send()

    @pl.loop(0, ny)
    def _(slot):
        core_copy(me_core, slot).wait_send()

    for step in (1, 2, 3):
        to = lax.rem(me_x + step, NX)
        white_copy(to, me_x).wait_send()
        last_copy(to, me_x).wait_send()
    for step in z_steps:
        z_copy(step, lax.rem(me_z + step, nz), me_z).wait_send()


def local(nchan, nz, record, offsets, sources):
    lag_rows = HALF // nz
    own = lag_rows // NX
    nlow, ny = split_chan(nchan)
    per = LANES // ny
    upper, lower = forward_tables()
    inverse = inverse_table(nz * NX * WIN)
    vmem = pl.BlockSpec(memory_space=pltpu.VMEM)
    hbm = pl.BlockSpec(memory_space=pltpu.HBM)
    dma = pltpu.SemaphoreType.DMA
    flat = pl.pallas_call(
        functools.partial(kernel, nchan, nz),
        out_shape=jax.ShapeDtypeStruct((own, NSRC * ROWS), BF16),
        in_specs=[hbm, hbm, vmem, hbm, hbm, hbm],
        out_specs=vmem,
        scratch_shapes=[
            pltpu.SMEM((WIN,), jnp.int32),
            pltpu.SMEM((NSRC,), jnp.int32),
            pltpu.VMEM((SAMPLES, SAMPLES), BF16),
            pltpu.VMEM((SAMPLES, SAMPLES), BF16),
            pltpu.VMEM((HALF, SAMPLES), BF16),
            pltpu.VMEM((256, SAMPLES), BF16),
            pltpu.VMEM((WIN, LANES, NSRC, 128), BF16),
            pltpu.VMEM((2 * ny, per, NSRC, 128), BF16),
            pltpu.VMEM((nlow * NX, per, NSRC, 128), BF16),
            pltpu.VMEM((per, NX * NSRC, 128), BF16),
            pltpu.VMEM((WIN, LANES, NX * NSRC, 128), BF16),
            pltpu.VMEM((SAMPLES, 256), F32),
            pltpu.VMEM((NX, HALF, 128), BF16),
            pltpu.VMEM((NX, HALF, 128), BF16),
            pltpu.VMEM((8, 2, 2, 64, 128), BF16),
            pltpu.VMEM((NX, HALF, 512), BF16),
            pltpu.VMEM((4, SAMPLES, 128), F32),
            pltpu.VMEM((SAMPLES, 512), BF16),
            pltpu.VMEM((nz, lag_rows, 512), BF16),
            pltpu.VMEM((nz, lag_rows, 512), BF16),
            pltpu.VMEM((lag_rows, 512), BF16),
            pltpu.VMEM((NX, own, 512), BF16),
            dma((5,)),
            dma((2 * ny,)),
            dma((2 * ny,)),
            dma((nlow * NX,)),
            dma((nlow * NX,)),
            dma((ny,)),
            dma((ny,)),
            dma((ny,)),
            dma((ny,)),
            dma((NX,)),
            dma((NX,)),
            dma((nz,)),
            dma((nz,)),
            dma((NX,)),
            dma((NX,)),
        ],
        compiler_params=pltpu.CompilerParams(
            collective_id=0, has_side_effects=True, vmem_limit_bytes=48 * 1024 * 1024
        ),
        cost_estimate=pl.CostEstimate(
            flops=3 * 10**9, bytes_accessed=7 * 10**6, transcendentals=10**6
        ),
    )(
        offsets,
        sources,
        jnp.transpose(record, (1, 0, 2)),
        jnp.asarray(upper),
        jnp.asarray(lower),
        jnp.asarray(inverse),
    )
    return flat.reshape(own, NSRC, ROWS)


def solution(mesh):
    nchan = mesh.shape["chan"]
    nz = mesh.shape["spec"] // NX
    in_specs = (P("chan", "spec", None), P("spec"), P())
    out_specs = P("spec", None, "chan")
    return jax.shard_map(
        functools.partial(local, nchan, nz),
        mesh=mesh,
        in_specs=in_specs,
        out_specs=out_specs,
        check_vma=False,
    )
```

```python
import functools
import math

import jax
import jax.numpy as jnp
import numpy as np
from jax import lax
from jax.experimental import pallas as pl
from jax.experimental.pallas import tpu as pltpu
from jax.sharding import PartitionSpec as P

SAMPLES = 1024
HALF = SAMPLES // 2
PAD = 128
NSRC = 16
WATER = 0.1
NX = 4
ROWS = 128
WIN = 2
BLK = ROWS // NX
GROUPS = 32
LANES = SAMPLES // 128
NZ = 4
CHUNKS = 2
WIDE = NSRC * BLK // CHUNKS
F32 = jnp.float32
BF16 = jnp.bfloat16
MESH = pl.DeviceIdType.MESH


def forward_tables():
    rows = np.arange(SAMPLES)[:, None]
    cols = np.arange(SAMPLES)[None, :]
    freq = rows % HALF
    angle = 2.0 * np.pi / SAMPLES * (freq * cols % SAMPLES)
    alternating = 1.0 - 2.0 * (cols % 2)
    imag = np.where(freq == 0, alternating, -np.sin(angle))
    table = np.where(rows < HALF, np.cos(angle), imag)
    upper = table.astype(jnp.bfloat16)
    lower = (table - upper.astype(np.float64)).astype(jnp.bfloat16)
    return upper, lower


def inverse_table(windows):
    shifted = np.arange(HALF)[:, None] - HALF // 2
    freq = (np.arange(16)[:, None] + 16 * np.arange(GROUPS)[None, :]).reshape(1, -1)
    angle = 2.0 * np.pi / SAMPLES * (freq * shifted % SAMPLES)
    alternating = 1.0 - 2.0 * (shifted % 2)
    first = freq == 0
    real = np.where(first, 1.0, 2.0 * np.cos(angle))
    imag = np.where(first, alternating, -2.0 * np.sin(angle))
    table = np.concatenate([real, imag], axis=1) / math.sqrt(windows * SAMPLES)
    return table.astype(jnp.bfloat16)


def split_chan(nchan):
    nlow = 2 if nchan >= 8 else 1
    return nlow, nchan // (2 * nlow)


def dot_t(left, right):
    return lax.dot_general(left, right, (((1,), (1,)), ((), ())), preferred_element_type=F32)


def dot(left, right):
    return lax.dot_general(left, right, (((1,), (0,)), ((), ())), preferred_element_type=F32)


def block_transpose(parts):
    count = len(parts)
    width = 128 // count
    lane = lax.broadcasted_iota(jnp.int32, parts[0].shape, 1)
    masks = [lane // width == i for i in range(count - 1)]

    def pick(choices):
        result = choices[-1]
        for mask, choice in zip(masks, choices):
            result = jnp.where(mask, choice, result)
        return result

    turned = []
    for d in range(count):
        part = pick([parts[(i - d) % count] for i in range(count)])
        turned.append(pltpu.roll(part, 128 - width * d, 1) if d else part)
    return [pick([turned[(j - i) % count] for i in range(count)]) for j in range(count)]


def kernel(
    nchan,
    numbers_hbm,
    record,
    tables_hbm,
    out,
    numbers,
    upper,
    lower,
    inverse,
    traces,
    pieces,
    reduced,
    gathered,
    piece_out,
    picked,
    spectrum,
    outgoing,
    incoming,
    left,
    copies,
    right,
    cross,
    stacked,
    lags_out,
    mixed,
    kept,
    lags_in,
    finished,
    last,
    load_sem,
    reduce_send,
    reduce_recv,
    side_send,
    side_recv,
    y_send,
    y_recv,
    core_send,
    core_recv,
    white_send,
    white_recv,
    z_send,
    z_recv,
    last_send,
    last_recv,
):
    nlow, ny = split_chan(nchan)
    per = LANES // ny
    plane = 2 * ny
    side = nlow * NX
    chan = lax.axis_index("chan")
    spec = lax.axis_index("spec")
    me_x = lax.rem(spec, NX)
    me_z = spec // NX
    me_low = chan // plane
    me_plane = lax.rem(chan, plane)
    me_y = me_plane // 2
    me_core = lax.rem(chan, 2)
    me_side = me_low * NX + me_x

    def at_plane(other):
        return (me_low * plane + other, spec)

    def at_side(other):
        return (other // NX * plane + me_plane, me_z * NX + lax.rem(other, NX))

    def at_x(other):
        return (chan, me_z * NX + other)

    def at_z(other):
        return (chan, other * NX + me_x)

    loads = [
        pltpu.make_async_copy(source, target, load_sem.at[i])
        for i, (source, target) in enumerate(
            [
                (numbers_hbm, numbers),
                (tables_hbm.at[pl.ds(0, SAMPLES)], upper),
                (tables_hbm.at[pl.ds(SAMPLES, SAMPLES)], lower),
                (tables_hbm.at[pl.ds(2 * SAMPLES, HALF)], inverse),
            ]
        )
    ]
    for load in loads:
        load.start()

    barrier = pltpu.get_barrier_semaphore()

    @pl.loop(1, plane)
    def _(step):
        pl.semaphore_signal(
            barrier, inc=1, device_id=at_plane(lax.rem(me_plane + step, plane)), device_id_type=MESH
        )

    @pl.loop(1, side)
    def _(step):
        pl.semaphore_signal(
            barrier, inc=1, device_id=at_side(lax.rem(me_side + step, side)), device_id_type=MESH
        )

    for step in (1, NZ - 1):
        pl.semaphore_signal(
            barrier, inc=1, device_id=at_z(lax.rem(me_z + step, NZ)), device_id_type=MESH
        )

    loads[0].wait()

    lane = lax.broadcasted_iota(jnp.int32, (ROWS, 128), 1)
    for w in range(WIN):
        rows = record[w].astype(F32)
        head = jnp.where(lane < numbers[w], rows[:, SAMPLES:], rows[:, :PAD])
        rows = jnp.concatenate([head, rows[:, PAD:SAMPLES]], axis=1)
        rows = rows - jnp.mean(rows, axis=1, keepdims=True)
        rows = rows * lax.rsqrt(jnp.mean(rows * rows, axis=1, keepdims=True) + 1e-06)
        rows = rows.astype(BF16)
        for x in range(NX):
            traces[pl.ds(x * 64 + w * BLK, BLK), :] = rows[x * BLK : (x + 1) * BLK]

    row = lax.broadcasted_iota(jnp.int32, (32, 256), 0)
    col = lax.broadcasted_iota(jnp.int32, (32, 256), 1)
    wanted = jnp.zeros((32, 256), jnp.int32)
    for s in range(NSRC):
        wanted = jnp.where(row % NSRC == s, numbers[WIN + s], wanted)
    channel = chan * ROWS + (col // 64) * BLK + col % BLK
    same = jnp.logical_and(wanted == channel, row // NSRC == (col // BLK) % 2)
    chosen = dot(jnp.where(same, 1.0, 0.0).astype(BF16), traces[...])
    chosen = chosen.astype(BF16)
    for w in range(WIN):
        for l in range(LANES):
            pieces[w, l] = chosen[NSRC * w : NSRC * w + NSRC, 128 * l : 128 * l + 128]

    pl.semaphore_wait(barrier, plane - 1 + side - 1 + 2)

    def reduce_copy(to, slot):
        return pltpu.make_async_remote_copy(
            src_ref=pieces.at[lax.rem(to, 2), pl.ds(to // 2 * per, per)],
            dst_ref=reduced.at[slot],
            send_sem=reduce_send.at[to],
            recv_sem=reduce_recv.at[slot],
            device_id=at_plane(to),
            device_id_type=MESH,
        )

    @pl.loop(1, plane)
    def _(step):
        reduce_copy(lax.rem(me_plane + step, plane), me_plane).start()

    reduced[me_plane] = pieces[me_core, pl.ds(me_y * per, per)]
    loads[1].wait()
    loads[2].wait()

    spectrum[...] = dot_t(upper[...], traces[...])
    spectrum[...] += dot_t(lower[...], traces[...])

    chunk = 64
    first_row = lax.broadcasted_iota(jnp.int32, (chunk, 256), 0) == 0
    total = jnp.zeros((1, 256), F32)
    for k in range(0, HALF, chunk):
        re = spectrum[k : k + chunk]
        im = spectrum[HALF + k : HALF + k + chunk]
        size = jnp.sqrt(re * re + im * im)
        if k == 0:
            size = jnp.where(first_row, jnp.abs(re) + jnp.abs(im), size)
        total = total + jnp.sum(size, axis=0, keepdims=True)
    level = WATER * (total / (HALF + 1) + 1e-06)
    low = lax.broadcasted_iota(jnp.int32, (chunk, 128), 1) < 64
    for k in range(0, HALF, chunk):
        re = spectrum[k : k + chunk]
        im = spectrum[HALF + k : HALF + k + chunk]
        size = jnp.sqrt(re * re + im * im)
        if k == 0:
            re = re / (jnp.where(first_row, jnp.abs(re), size) + level)
            im = im / (jnp.where(first_row, jnp.abs(im), size) + level)
        else:
            scale = 1.0 / (size + level)
            re = re * scale
            im = im * scale
        for pair in range(2):
            a = re[:, 128 * pair : 128 * pair + 128]
            b = im[:, 128 * pair : 128 * pair + 128]
            even = jnp.where(low, a, pltpu.roll(b, 64, 1))
            odd = jnp.where(low, pltpu.roll(a, 64, 1), b)
            outgoing[2 * pair, k : k + chunk] = even.astype(BF16)
            outgoing[2 * pair + 1, k : k + chunk] = odd.astype(BF16)

    def white_copy(to, slot):
        return pltpu.make_async_remote_copy(
            src_ref=outgoing.at[to],
            dst_ref=incoming.at[slot],
            send_sem=white_send.at[to],
            recv_sem=white_recv.at[slot],
            device_id=at_x(to),
            device_id_type=MESH,
        )

    for step in (2, 1, 3):
        white_copy(lax.rem(me_x + step, NX), me_x).start()
    incoming[me_x] = outgoing[me_x]

    @pl.loop(1, plane)
    def _(step):
        reduce_copy(me_plane, lax.rem(me_plane + step, plane)).wait_recv()

    total = reduced[0].astype(F32)
    for i in range(1, plane):
        total = total + reduced[i].astype(F32)
    gathered[me_side] = total.astype(BF16)

    def side_copy(to, slot):
        return pltpu.make_async_remote_copy(
            src_ref=gathered.at[me_side],
            dst_ref=gathered.at[slot],
            send_sem=side_send.at[to],
            recv_sem=side_recv.at[slot],
            device_id=at_side(to),
            device_id_type=MESH,
        )

    @pl.loop(1, side)
    def _(step):
        side_copy(lax.rem(me_side + step, side), me_side).start()

    @pl.loop(1, side)
    def _(step):
        side_copy(me_side, lax.rem(me_side + step, side)).wait_recv()

    for l in range(per):
        for x in range(NX):
            total = gathered[x, l].astype(F32)
            for low_z in range(1, nlow):
                total = total + gathered[low_z * NX + x, l].astype(F32)
            piece_out[l, NSRC * x : NSRC * x + NSRC] = total.astype(BF16)

    def y_copy(to, slot):
        return pltpu.make_async_remote_copy(
            src_ref=piece_out,
            dst_ref=picked.at[me_core, pl.ds(slot * per, per)],
            send_sem=y_send.at[to],
            recv_sem=y_recv.at[slot],
            device_id=at_plane(to * 2 + me_core),
            device_id_type=MESH,
        )

    def core_copy(core, slot):
        at = picked.at[core, pl.ds(slot * per, per)]
        return pltpu.make_async_remote_copy(
            src_ref=at,
            dst_ref=at,
            send_sem=core_send.at[slot],
            recv_sem=core_recv.at[slot],
            device_id=at_plane(me_y * 2 + 1 - me_core),
            device_id_type=MESH,
        )

    @pl.loop(1, ny)
    def _(step):
        y_copy(lax.rem(me_y + step, ny), me_y).start()

    picked[me_core, pl.ds(me_y * per, per)] = piece_out[...]
    core_copy(me_core, me_y).start()

    @pl.loop(1, ny)
    def _(step):
        slot = lax.rem(me_y + step, ny)
        y_copy(me_y, slot).wait_recv()
        core_copy(me_core, slot).start()

    r = lax.broadcasted_iota(jnp.int32, (128, 512), 0)
    c = lax.broadcasted_iota(jnp.int32, (128, 512), 1)
    match = jnp.logical_and(r // BLK == c // 128, r % BLK == c % BLK)
    spread = jnp.where(match, 1.0, 0.0).astype(BF16)
    r = lax.broadcasted_iota(jnp.int32, (16, 512), 0)
    c = lax.broadcasted_iota(jnp.int32, (16, 512), 1)
    mask = jnp.where(r == c // BLK, 1.0, 0.0).astype(BF16)

    def widen(x):
        copies[...] = dot(incoming[x], spread).astype(BF16)

        @pl.loop(0, 8)
        def _(small):
            for big in range(4):
                group = big * 8 + small
                at = pl.ds(pl.multiple_of(group * 16, 16), 16)
                for p in range(2):
                    for w in range(WIN):
                        quarter = p * 2 + w
                        tile = copies[at, quarter * 128 : quarter * 128 + 128]
                        slab = pl.multiple_of((p * 8 + x * 2 + w) * 16, 16)
                        right[group, pl.ds(slab, 16), :] = (
                            jnp.concatenate([tile] * 4, axis=1) * mask
                        )

    widen(me_x)
    for step in (1, 3, 2):
        x = lax.rem(me_x + step, NX)
        white_copy(me_x, x).wait_recv()
        widen(x)

    @pl.loop(0, ny)
    def _(slot):
        core_copy(1 - me_core, slot).wait_recv()

    rows = [
        jnp.concatenate([picked[w, l] for l in range(LANES)], axis=1) for w in range(WIN)
    ]
    rows = jnp.concatenate(rows, axis=0)
    both = dot_t(rows, upper[...]) + dot_t(rows, lower[...])
    re = both[:, :HALF]
    im = both[:, HALF:]
    size = jnp.sqrt(re * re + im * im)
    first = lax.broadcasted_iota(jnp.int32, (ROWS, HALF), 1) == 0
    total = jnp.sum(
        jnp.where(first, jnp.abs(re) + jnp.abs(im), size), axis=1, keepdims=True
    )
    level = WATER * (total / (HALF + 1) + 1e-06)
    re = (re / (jnp.where(first, jnp.abs(re), size) + level)).astype(BF16)
    im = (im / (jnp.where(first, jnp.abs(im), size) + level)).astype(BF16)
    parts = []
    for x in range(NX):
        for w in range(WIN):
            tiles = []
            for half in (re, im):
                for big in range(4):
                    at = NSRC * (w * NX + x)
                    tiles.append(half[at : at + NSRC, 128 * big : 128 * big + 128])
            parts.append(jnp.concatenate(tiles, axis=0))
    parts = block_transpose(parts)
    for small in range(8):
        a_re = parts[small][:64]
        a_im = parts[small][64:]
        re_b0, re_b1, im_b0, im_b1 = a_re, a_im, -a_im, a_re
        if small == 0:
            shape = (64, 128)
            zero_bin = jnp.logical_and(
                lax.broadcasted_iota(jnp.int32, shape, 0) < 16,
                lax.broadcasted_iota(jnp.int32, shape, 1) % 16 == 0,
            )
            zero = jnp.zeros(shape, BF16)
            re_b1 = jnp.where(zero_bin, zero, re_b1)
            im_b0 = jnp.where(zero_bin, zero, im_b0)
            im_b1 = jnp.where(zero_bin, a_im, im_b1)
        left[small, 0, 0] = re_b0
        left[small, 0, 1] = re_b1
        left[small, 1, 0] = im_b0
        left[small, 1, 1] = im_b1

    @pl.loop(0, 8)
    def _(small):
        for big in range(4):
            group = big * 8 + small
            rows_left = jnp.concatenate(
                [
                    jnp.concatenate(
                        [left[small, part, p, big * 16 : big * 16 + 16, :] for p in range(2)],
                        axis=1,
                    )
                    for part in range(2)
                ],
                axis=0,
            )
            result = dot(rows_left, right[group])
            for h in range(4):
                cross[h, pl.ds(group, 32, stride=32), :] = result[:, 128 * h : 128 * h + 128]

    loads[3].wait()

    ahead = lax.rem(me_z + 1, NZ)
    behind = lax.rem(me_z + NZ - 1, NZ)
    lag_rows = HALF // NZ
    top = pl.ds(0, lag_rows // 2)
    bottom = pl.ds(lag_rows // 2, lag_rows // 2)

    def z_copy(chunk, kind, way, to=None):
        source = [
            (lags_out.at[chunk, 1, top], lags_out.at[chunk, 1, bottom]),
            (lags_out.at[chunk, 0, bottom], lags_out.at[chunk, 2, top]),
            (mixed.at[chunk, 0], mixed.at[chunk, 1]),
        ][kind][way]
        return pltpu.make_async_remote_copy(
            src_ref=source,
            dst_ref=lags_in.at[chunk, kind, way],
            send_sem=z_send.at[chunk, kind, way],
            recv_sem=z_recv.at[chunk, kind, way],
            device_id=at_z((ahead, behind)[way]),
            device_id_type=MESH,
        )

    def lag_block(to, chunk):
        at = pl.ds(pl.multiple_of(to * lag_rows, lag_rows), lag_rows)
        return dot(inverse[at, :], stacked[:, WIDE * chunk : WIDE * chunk + WIDE])

    for chunk in range(CHUNKS):
        for part in range(2):
            for quad in range(chunk * 4 // CHUNKS, (chunk + 1) * 4 // CHUNKS):
                for h in range(4):
                    parts = [
                        cross[h, pl.ds((part * 16 + quad * 4 + i) * 32, 32), :].astype(BF16)
                        for i in range(4)
                    ]
                    parts = block_transpose(parts)
                    for j in range(4):
                        at = (part * 16 + h * 4 + j) * 32
                        stacked[at : at + 32, 128 * quad : 128 * quad + 128] = parts[j]
        lags_out[chunk, 1] = lag_block(lax.rem(me_z + 2, NZ), chunk).astype(BF16)
        z_copy(chunk, 0, 0).start()
        z_copy(chunk, 0, 1).start()
        block = lag_block(ahead, chunk)
        lags_out[chunk, 0] = block.astype(BF16)
        kept[chunk, 0] = block[: lag_rows // 2]
        z_copy(chunk, 1, 0).start()
        block = lag_block(behind, chunk)
        lags_out[chunk, 2] = block.astype(BF16)
        kept[chunk, 1] = block[lag_rows // 2 :]
        z_copy(chunk, 1, 1).start()
        block = lag_block(me_z, chunk)
        kept[chunk, 2] = block[: lag_rows // 2]
        kept[chunk, 3] = block[lag_rows // 2 :]

    for chunk in range(CHUNKS):
        for way in range(2):
            z_copy(chunk, 0, way).wait_recv()
            total = kept[chunk, way] + lags_in[chunk, 0, way].astype(F32)
            mixed[chunk, way] = total.astype(BF16)
            z_copy(chunk, 2, way).start()

    own = lag_rows // NX

    def last_copy(chunk, to, slot):
        at = pl.ds(pl.multiple_of(to * own, own), own)
        return pltpu.make_async_remote_copy(
            src_ref=finished.at[chunk, at],
            dst_ref=last.at[chunk, slot],
            send_sem=last_send.at[chunk, to],
            recv_sem=last_recv.at[chunk, slot],
            device_id=at_x(to),
            device_id_type=MESH,
        )

    for chunk in range(CHUNKS):
        for kind in (1, 2):
            for way in range(2):
                z_copy(chunk, kind, way).wait_recv()
        for half in range(2):
            total = (
                kept[chunk, 2 + half]
                + lags_in[chunk, 2, half].astype(F32)
                + lags_in[chunk, 1, 1 - half].astype(F32)
            )
            finished[chunk, pl.ds(half * lag_rows // 2, lag_rows // 2)] = total.astype(BF16)
        for step in (2, 1, 3):
            last_copy(chunk, lax.rem(me_x + step, NX), me_x).start()
        last[chunk, me_x] = finished[chunk, pl.ds(pl.multiple_of(me_x * own, own), own), :]

    for chunk in range(CHUNKS):
        for step in (1, 3, 2):
            last_copy(chunk, me_x, lax.rem(me_x + step, NX)).wait_recv()
        for quad in range(4 // CHUNKS):
            parts = [last[chunk, x, :, 128 * quad : 128 * quad + 128] for x in range(NX)]
            parts = block_transpose(parts)
            for j in range(4):
                s = chunk * NSRC // CHUNKS + quad * 4 + j
                out[:, 128 * s : 128 * s + 128] = parts[j]

    @pl.loop(1, plane)
    def _(step):
        reduce_copy(lax.rem(me_plane + step, plane), me_plane).wait_send()

    @pl.loop(1, side)
    def _(step):
        side_copy(lax.rem(me_side + step, side), me_side).wait_send()

    @pl.loop(1, ny)
    def _(step):
        y_copy(lax.rem(me_y + step, ny), me_y).wait_send()

    @pl.loop(0, ny)
    def _(slot):
        core_copy(me_core, slot).wait_send()

    for step in (1, 2, 3):
        to = lax.rem(me_x + step, NX)
        white_copy(to, me_x).wait_send()
        for chunk in range(CHUNKS):
            last_copy(chunk, to, me_x).wait_send()
    for chunk in range(CHUNKS):
        for kind in range(3):
            for way in range(2):
                z_copy(chunk, kind, way).wait_send()


def local(nchan, record, offsets, sources):
    lag_rows = HALF // NZ
    own = lag_rows // NX
    nlow, ny = split_chan(nchan)
    per = LANES // ny
    upper, lower = forward_tables()
    inverse = inverse_table(NZ * NX * WIN)
    tables = np.concatenate([upper, lower, inverse], axis=0)
    vmem = pl.BlockSpec(memory_space=pltpu.VMEM)
    hbm = pl.BlockSpec(memory_space=pltpu.HBM)
    dma = pltpu.SemaphoreType.DMA
    flat = pl.pallas_call(
        functools.partial(kernel, nchan),
        out_shape=jax.ShapeDtypeStruct((own, NSRC * ROWS), BF16),
        in_specs=[hbm, vmem, hbm],
        out_specs=vmem,
        scratch_shapes=[
            pltpu.SMEM((WIN + NSRC,), jnp.int32),
            pltpu.VMEM((SAMPLES, SAMPLES), BF16),
            pltpu.VMEM((SAMPLES, SAMPLES), BF16),
            pltpu.VMEM((HALF, SAMPLES), BF16),
            pltpu.VMEM((256, SAMPLES), BF16),
            pltpu.VMEM((WIN, LANES, NSRC, 128), BF16),
            pltpu.VMEM((2 * ny, per, NSRC, 128), BF16),
            pltpu.VMEM((nlow * NX, per, NSRC, 128), BF16),
            pltpu.VMEM((per, NX * NSRC, 128), BF16),
            pltpu.VMEM((WIN, LANES, NX * NSRC, 128), BF16),
            pltpu.VMEM((SAMPLES, 256), F32),
            pltpu.VMEM((NX, HALF, 128), BF16),
            pltpu.VMEM((NX, HALF, 128), BF16),
            pltpu.VMEM((8, 2, 2, 64, 128), BF16),
            pltpu.VMEM((HALF, 512), BF16),
            pltpu.VMEM((GROUPS, 256, 512), BF16),
            pltpu.VMEM((4, SAMPLES, 128), F32),
            pltpu.VMEM((SAMPLES, 512), BF16),
            pltpu.VMEM((CHUNKS, 3, lag_rows, WIDE), BF16),
            pltpu.VMEM((CHUNKS, 2, lag_rows // 2, WIDE), BF16),
            pltpu.VMEM((CHUNKS, 4, lag_rows // 2, WIDE), F32),
            pltpu.VMEM((CHUNKS, 3, 2, lag_rows // 2, WIDE), BF16),
            pltpu.VMEM((CHUNKS, lag_rows, WIDE), BF16),
            pltpu.VMEM((CHUNKS, NX, own, WIDE), BF16),
            dma((4,)),
            dma((2 * ny,)),
            dma((2 * ny,)),
            dma((nlow * NX,)),
            dma((nlow * NX,)),
            dma((ny,)),
            dma((ny,)),
            dma((ny,)),
            dma((ny,)),
            dma((NX,)),
            dma((NX,)),
            dma((CHUNKS, 3, 2)),
            dma((CHUNKS, 3, 2)),
            dma((CHUNKS, NX)),
            dma((CHUNKS, NX)),
        ],
        compiler_params=pltpu.CompilerParams(
            collective_id=0, has_side_effects=True, vmem_limit_bytes=60 * 1024 * 1024
        ),
        cost_estimate=pl.CostEstimate(
            flops=3 * 10**9, bytes_accessed=7 * 10**6, transcendentals=10**6
        ),
    )(
        jnp.concatenate([offsets, sources]),
        jnp.transpose(record, (1, 0, 2)),
        jnp.asarray(tables),
    )
    return flat.reshape(own, NSRC, ROWS)


def solution(mesh):
    nchan = mesh.shape["chan"]
    in_specs = (P("chan", "spec", None), P("spec"), P())
    out_specs = P("spec", None, "chan")
    return jax.shard_map(
        functools.partial(local, nchan),
        mesh=mesh,
        in_specs=in_specs,
        out_specs=out_specs,
        check_vma=False,
    )
```

```python
import functools
import math

import jax
import jax.numpy as jnp
import numpy as np
from jax import lax
from jax.experimental import pallas as pl
from jax.experimental.pallas import tpu as pltpu
from jax.sharding import PartitionSpec as P

SAMPLES = 1024
HALF = SAMPLES // 2
PAD = 128
NSRC = 16
WATER = 0.1
NX = 4
ROWS = 128
WIN = 2
BLK = ROWS // NX
GROUPS = 32
NLOW = 2
NZ = 4
CHUNKS = 2
WIDE = NSRC * BLK // CHUNKS
F32 = jnp.float32
BF16 = jnp.bfloat16
MESH = pl.DeviceIdType.MESH


def forward_tables():
    rows = np.arange(SAMPLES)[:, None]
    cols = np.arange(SAMPLES)[None, :]
    freq = rows % HALF
    angle = 2.0 * np.pi / SAMPLES * (freq * cols % SAMPLES)
    alternating = 1.0 - 2.0 * (cols % 2)
    imag = np.where(freq == 0, alternating, -np.sin(angle))
    table = np.where(rows < HALF, np.cos(angle), imag)
    upper = table.astype(jnp.bfloat16)
    lower = (table - upper.astype(np.float64)).astype(jnp.bfloat16)
    return upper, lower


def inverse_table(windows):
    shifted = np.arange(HALF)[:, None] - HALF // 2
    freq = (np.arange(16)[:, None] + 16 * np.arange(GROUPS)[None, :]).reshape(1, -1)
    angle = 2.0 * np.pi / SAMPLES * (freq * shifted % SAMPLES)
    alternating = 1.0 - 2.0 * (shifted % 2)
    first = freq == 0
    real = np.where(first, 1.0, 2.0 * np.cos(angle))
    imag = np.where(first, alternating, -2.0 * np.sin(angle))
    table = np.concatenate([real, imag], axis=1) / math.sqrt(windows * SAMPLES)
    return table.astype(jnp.bfloat16)


def dot_t(left, right):
    return lax.dot_general(left, right, (((1,), (1,)), ((), ())), preferred_element_type=F32)


def dot(left, right):
    return lax.dot_general(left, right, (((1,), (0,)), ((), ())), preferred_element_type=F32)


def block_transpose(parts):
    count = len(parts)
    width = 128 // count
    lane = lax.broadcasted_iota(jnp.int32, parts[0].shape, 1)
    masks = [lane // width == i for i in range(count - 1)]

    def pick(choices):
        result = choices[-1]
        for mask, choice in zip(masks, choices):
            result = jnp.where(mask, choice, result)
        return result

    turned = []
    for d in range(count):
        part = pick([parts[(i - d) % count] for i in range(count)])
        turned.append(pltpu.roll(part, 128 - width * d, 1) if d else part)
    return [pick([turned[(j - i) % count] for i in range(count)]) for j in range(count)]


def kernel(
    ny,
    offsets_hbm,
    sources_hbm,
    record,
    tables_hbm,
    out,
    offsets,
    sources,
    upper,
    lower,
    inverse,
    traces,
    pieces,
    reduced,
    parts_y,
    picked,
    spectrum,
    outgoing,
    incoming,
    left,
    copies,
    right,
    cross,
    stacked,
    lags_out,
    mixed,
    kept,
    lags_in,
    finished,
    last,
    load_sem,
    near_send,
    near_recv,
    y_send,
    y_recv,
    side_send,
    side_recv,
    core_send,
    core_recv,
    white_send,
    white_recv,
    z_send,
    z_recv,
    last_send,
    last_recv,
):
    plane = 2 * ny
    side = NLOW * NX
    near = NLOW * 2
    chan = lax.axis_index("chan")
    spec = lax.axis_index("spec")
    me_x = lax.rem(spec, NX)
    me_z = spec // NX
    me_low = chan // plane
    me_plane = lax.rem(chan, plane)
    me_y = me_plane // 2
    me_core = lax.rem(chan, 2)
    me_side = me_low * NX + me_x
    me_near = me_low * 2 + me_core

    def at_near(other):
        return (other // 2 * plane + me_y * 2 + lax.rem(other, 2), spec)

    def at_y(other):
        return (me_low * plane + other * 2 + me_core, spec)

    def at_side(other):
        return (other // NX * plane + me_plane, me_z * NX + lax.rem(other, NX))

    def at_x(other):
        return (chan, me_z * NX + other)

    def at_z(other):
        return (chan, other * NX + me_x)

    loads = [
        pltpu.make_async_copy(source, target, load_sem.at[i])
        for i, (source, target) in enumerate(
            [
                (offsets_hbm, offsets),
                (sources_hbm, sources),
                (tables_hbm.at[pl.ds(0, SAMPLES)], upper),
                (tables_hbm.at[pl.ds(SAMPLES, SAMPLES)], lower),
                (tables_hbm.at[pl.ds(2 * SAMPLES, HALF)], inverse),
            ]
        )
    ]
    for load in loads:
        load.start()

    barrier = pltpu.get_barrier_semaphore()

    def greet(device):
        pl.semaphore_signal(barrier, inc=1, device_id=device, device_id_type=MESH)

    greet(at_near(me_low * 2 + 1 - me_core))
    greet(at_near((1 - me_low) * 2 + 1 - me_core))

    @pl.loop(1, ny)
    def _(step):
        greet(at_y(lax.rem(me_y + step, ny)))

    @pl.loop(1, side)
    def _(step):
        greet(at_side(lax.rem(me_side + step, side)))

    for step in (1, NZ - 1):
        greet(at_z(lax.rem(me_z + step, NZ)))

    loads[0].wait()
    loads[1].wait()

    lane = lax.broadcasted_iota(jnp.int32, (ROWS, 128), 1)
    for w in range(WIN):
        rows = record[w].astype(F32)
        head = jnp.where(lane < offsets[w], rows[:, SAMPLES:], rows[:, :PAD])
        rows = jnp.concatenate([head, rows[:, PAD:SAMPLES]], axis=1)
        rows = rows - jnp.mean(rows, axis=1, keepdims=True)
        rows = rows * lax.rsqrt(jnp.mean(rows * rows, axis=1, keepdims=True) + 1e-06)
        rows = rows.astype(BF16)
        for x in range(NX):
            traces[pl.ds(x * 64 + w * BLK, BLK), :] = rows[x * BLK : (x + 1) * BLK]

    row = lax.broadcasted_iota(jnp.int32, (32, 256), 0)
    col = lax.broadcasted_iota(jnp.int32, (32, 256), 1)
    wanted = jnp.zeros((32, 256), jnp.int32)
    for s in range(NSRC):
        wanted = jnp.where(row % NSRC == s, sources[s], wanted)
    channel = chan * ROWS + (col // 64) * BLK + col % BLK
    same = jnp.logical_and(wanted == channel, row // NSRC == (col // BLK) % 2)
    chosen = dot(jnp.where(same, 1.0, 0.0).astype(BF16), traces[...])
    for w in range(WIN):
        for low in range(NLOW):
            rows = chosen[16 * w + 8 * low : 16 * w + 8 * low + 8]
            rows = jnp.concatenate([rows[:, :HALF], rows[:, HALF:]], axis=0)
            pieces[low * 2 + w] = rows.astype(BF16)

    pl.semaphore_wait(barrier, 2 + ny - 1 + side - 1 + 2)

    def near_copy(to, slot):
        return pltpu.make_async_remote_copy(
            src_ref=pieces.at[to],
            dst_ref=reduced.at[slot],
            send_sem=near_send.at[to],
            recv_sem=near_recv.at[slot],
            device_id=at_near(to),
            device_id_type=MESH,
        )

    for step in (2, 3, 1):
        near_copy(lax.rem(me_near + step, near), me_near).start()
    reduced[me_near] = pieces[me_near]
    loads[2].wait()
    loads[3].wait()

    spectrum[...] = dot_t(upper[...], traces[...])
    spectrum[...] += dot_t(lower[...], traces[...])

    for step in (1, 2, 3):
        near_copy(me_near, lax.rem(me_near + step, near)).wait_recv()
    total = reduced[0].astype(F32)
    for i in range(1, near):
        total = total + reduced[i].astype(F32)
    parts_y[me_y] = total.astype(BF16)

    def y_copy(to, slot):
        return pltpu.make_async_remote_copy(
            src_ref=parts_y.at[me_y],
            dst_ref=parts_y.at[slot],
            send_sem=y_send.at[to],
            recv_sem=y_recv.at[slot],
            device_id=at_y(to),
            device_id_type=MESH,
        )

    for step in sorted(range(1, ny), key=lambda step: -min(step, ny - step)):
        y_copy(lax.rem(me_y + step, ny), me_y).start()

    chunk = 64
    first_row = lax.broadcasted_iota(jnp.int32, (chunk, 256), 0) == 0
    total = jnp.zeros((1, 256), F32)
    for k in range(0, HALF, chunk):
        re = spectrum[k : k + chunk]
        im = spectrum[HALF + k : HALF + k + chunk]
        size = jnp.sqrt(re * re + im * im)
        if k == 0:
            size = jnp.where(first_row, jnp.abs(re) + jnp.abs(im), size)
        total = total + jnp.sum(size, axis=0, keepdims=True)
    level = WATER * (total / (HALF + 1) + 1e-06)
    low = lax.broadcasted_iota(jnp.int32, (chunk, 128), 1) < 64
    for k in range(0, HALF, chunk):
        re = spectrum[k : k + chunk]
        im = spectrum[HALF + k : HALF + k + chunk]
        size = jnp.sqrt(re * re + im * im)
        if k == 0:
            re = re / (jnp.where(first_row, jnp.abs(re), size) + level)
            im = im / (jnp.where(first_row, jnp.abs(im), size) + level)
        else:
            scale = 1.0 / (size + level)
            re = re * scale
            im = im * scale
        for pair in range(2):
            a = re[:, 128 * pair : 128 * pair + 128]
            b = im[:, 128 * pair : 128 * pair + 128]
            even = jnp.where(low, a, pltpu.roll(b, 64, 1))
            odd = jnp.where(low, pltpu.roll(a, 64, 1), b)
            outgoing[2 * pair, k : k + chunk] = even.astype(BF16)
            outgoing[2 * pair + 1, k : k + chunk] = odd.astype(BF16)

    def white_copy(to, slot):
        return pltpu.make_async_remote_copy(
            src_ref=outgoing.at[to],
            dst_ref=incoming.at[slot],
            send_sem=white_send.at[to],
            recv_sem=white_recv.at[slot],
            device_id=at_x(to),
            device_id_type=MESH,
        )

    for step in (2, 1, 3):
        white_copy(lax.rem(me_x + step, NX), me_x).start()
    incoming[me_x] = outgoing[me_x]

    r = lax.broadcasted_iota(jnp.int32, (128, 512), 0)
    c = lax.broadcasted_iota(jnp.int32, (128, 512), 1)
    match = jnp.logical_and(r // BLK == c // 128, r % BLK == c % BLK)
    spread = jnp.where(match, 1.0, 0.0).astype(BF16)
    r = lax.broadcasted_iota(jnp.int32, (16, 512), 0)
    c = lax.broadcasted_iota(jnp.int32, (16, 512), 1)
    mask = jnp.where(r == c // BLK, 1.0, 0.0).astype(BF16)

    def widen(x):
        copies[...] = dot(incoming[x], spread).astype(BF16)

        @pl.loop(0, 8)
        def _(small):
            for big in range(4):
                group = big * 8 + small
                at = pl.ds(pl.multiple_of(group * 16, 16), 16)
                for p in range(2):
                    for w in range(WIN):
                        quarter = p * 2 + w
                        tile = copies[at, quarter * 128 : quarter * 128 + 128]
                        slab = pl.multiple_of((p * 8 + x * 2 + w) * 16, 16)
                        right[group, pl.ds(slab, 16), :] = (
                            jnp.concatenate([tile] * 4, axis=1) * mask
                        )

    @pl.loop(1, ny)
    def _(step):
        y_copy(me_y, lax.rem(me_y + step, ny)).wait_recv()

    total = parts_y[0].astype(F32)
    for i in range(1, ny):
        total = total + parts_y[i].astype(F32)
    rows = jnp.concatenate([total[:8], total[8:]], axis=1).astype(BF16)
    both = dot_t(rows, upper[...]) + dot_t(rows, lower[...])
    re = both[:, :HALF]
    im = both[:, HALF:]
    size = jnp.sqrt(re * re + im * im)
    first = lax.broadcasted_iota(jnp.int32, (8, HALF), 1) == 0
    total = jnp.sum(
        jnp.where(first, jnp.abs(re) + jnp.abs(im), size), axis=1, keepdims=True
    )
    level = WATER * (total / (HALF + 1) + 1e-06)
    re = re / (jnp.where(first, jnp.abs(re), size) + level)
    im = im / (jnp.where(first, jnp.abs(im), size) + level)
    picked[me_core, me_side] = jnp.concatenate([re, im], axis=0).astype(BF16)

    def side_copy(to, slot):
        return pltpu.make_async_remote_copy(
            src_ref=picked.at[me_core, me_side],
            dst_ref=picked.at[me_core, slot],
            send_sem=side_send.at[to],
            recv_sem=side_recv.at[slot],
            device_id=at_side(to),
            device_id_type=MESH,
        )

    def core_copy(core, slot):
        return pltpu.make_async_remote_copy(
            src_ref=picked.at[core, slot],
            dst_ref=picked.at[core, slot],
            send_sem=core_send.at[slot],
            recv_sem=core_recv.at[slot],
            device_id=at_near(me_low * 2 + 1 - me_core),
            device_id_type=MESH,
        )

    @pl.loop(1, side)
    def _(step):
        side_copy(lax.rem(me_side + step, side), me_side).start()

    core_copy(me_core, me_side).start()

    widen(me_x)
    for step in (1, 3, 2):
        x = lax.rem(me_x + step, NX)
        white_copy(me_x, x).wait_recv()
        widen(x)

    @pl.loop(1, side)
    def _(step):
        slot = lax.rem(me_side + step, side)
        side_copy(me_side, slot).wait_recv()
        core_copy(me_core, slot).start()

    @pl.loop(0, side)
    def _(slot):
        core_copy(1 - me_core, slot).wait_recv()

    parts = []
    for x in range(NX):
        for w in range(WIN):
            tiles = []
            halves = [picked[w, low * NX + x].astype(F32) for low in range(NLOW)]
            for part in range(2):
                for big in range(4):
                    for half in halves:
                        tiles.append(
                            half[8 * part : 8 * part + 8, 128 * big : 128 * big + 128]
                        )
            parts.append(jnp.concatenate(tiles, axis=0))
    parts = block_transpose(parts)
    for small in range(8):
        a_re = parts[small][:64].astype(BF16)
        a_im = parts[small][64:].astype(BF16)
        re_b0, re_b1, im_b0, im_b1 = a_re, a_im, -a_im, a_re
        if small == 0:
            shape = (64, 128)
            zero_bin = jnp.logical_and(
                lax.broadcasted_iota(jnp.int32, shape, 0) < 16,
                lax.broadcasted_iota(jnp.int32, shape, 1) % 16 == 0,
            )
            zero = jnp.zeros(shape, BF16)
            re_b1 = jnp.where(zero_bin, zero, re_b1)
            im_b0 = jnp.where(zero_bin, zero, im_b0)
            im_b1 = jnp.where(zero_bin, a_im, im_b1)
        left[small, 0, 0] = re_b0
        left[small, 0, 1] = re_b1
        left[small, 1, 0] = im_b0
        left[small, 1, 1] = im_b1

    @pl.loop(0, 8)
    def _(small):
        for big in range(4):
            group = big * 8 + small
            rows_left = jnp.concatenate(
                [
                    jnp.concatenate(
                        [left[small, part, p, big * 16 : big * 16 + 16, :] for p in range(2)],
                        axis=1,
                    )
                    for part in range(2)
                ],
                axis=0,
            )
            result = dot(rows_left, right[group])
            for h in range(4):
                cross[h, pl.ds(group, 32, stride=32), :] = result[:, 128 * h : 128 * h + 128]

    loads[4].wait()

    ahead = lax.rem(me_z + 1, NZ)
    behind = lax.rem(me_z + NZ - 1, NZ)
    lag_rows = HALF // NZ
    top = pl.ds(0, lag_rows // 2)
    bottom = pl.ds(lag_rows // 2, lag_rows // 2)

    def z_copy(chunk, kind, way, to=None):
        source = [
            (lags_out.at[chunk, 1, top], lags_out.at[chunk, 1, bottom]),
            (lags_out.at[chunk, 0, bottom], lags_out.at[chunk, 2, top]),
            (mixed.at[chunk, 0], mixed.at[chunk, 1]),
        ][kind][way]
        return pltpu.make_async_remote_copy(
            src_ref=source,
            dst_ref=lags_in.at[chunk, kind, way],
            send_sem=z_send.at[chunk, kind, way],
            recv_sem=z_recv.at[chunk, kind, way],
            device_id=at_z((ahead, behind)[way]),
            device_id_type=MESH,
        )

    def lag_block(to, chunk):
        at = pl.ds(pl.multiple_of(to * lag_rows, lag_rows), lag_rows)
        return dot(inverse[at, :], stacked[:, WIDE * chunk : WIDE * chunk + WIDE])

    for chunk in range(CHUNKS):
        for part in range(2):
            for quad in range(chunk * 4 // CHUNKS, (chunk + 1) * 4 // CHUNKS):
                for h in range(4):
                    parts = [
                        cross[h, pl.ds((part * 16 + quad * 4 + i) * 32, 32), :].astype(BF16)
                        for i in range(4)
                    ]
                    parts = block_transpose(parts)
                    for j in range(4):
                        at = (part * 16 + h * 4 + j) * 32
                        stacked[at : at + 32, 128 * quad : 128 * quad + 128] = parts[j]
        lags_out[chunk, 1] = lag_block(lax.rem(me_z + 2, NZ), chunk).astype(BF16)
        z_copy(chunk, 0, 0).start()
        z_copy(chunk, 0, 1).start()
        block = lag_block(ahead, chunk)
        lags_out[chunk, 0] = block.astype(BF16)
        kept[chunk, 0] = block[: lag_rows // 2]
        z_copy(chunk, 1, 0).start()
        block = lag_block(behind, chunk)
        lags_out[chunk, 2] = block.astype(BF16)
        kept[chunk, 1] = block[lag_rows // 2 :]
        z_copy(chunk, 1, 1).start()
        block = lag_block(me_z, chunk)
        kept[chunk, 2] = block[: lag_rows // 2]
        kept[chunk, 3] = block[lag_rows // 2 :]

    for chunk in range(CHUNKS):
        for way in range(2):
            z_copy(chunk, 0, way).wait_recv()
            total = kept[chunk, way] + lags_in[chunk, 0, way].astype(F32)
            mixed[chunk, way] = total.astype(BF16)
            z_copy(chunk, 2, way).start()

    own = lag_rows // NX

    def last_copy(chunk, to, slot):
        at = pl.ds(pl.multiple_of(to * own, own), own)
        return pltpu.make_async_remote_copy(
            src_ref=finished.at[chunk, at],
            dst_ref=last.at[chunk, slot],
            send_sem=last_send.at[chunk, to],
            recv_sem=last_recv.at[chunk, slot],
            device_id=at_x(to),
            device_id_type=MESH,
        )

    for chunk in range(CHUNKS):
        for kind in (1, 2):
            for way in range(2):
                z_copy(chunk, kind, way).wait_recv()
        for half in range(2):
            total = (
                kept[chunk, 2 + half]
                + lags_in[chunk, 2, half].astype(F32)
                + lags_in[chunk, 1, 1 - half].astype(F32)
            )
            finished[chunk, pl.ds(half * lag_rows // 2, lag_rows // 2)] = total.astype(BF16)
        for step in (2, 1, 3):
            last_copy(chunk, lax.rem(me_x + step, NX), me_x).start()
        last[chunk, me_x] = finished[chunk, pl.ds(pl.multiple_of(me_x * own, own), own), :]

    for chunk in range(CHUNKS):
        for step in (1, 3, 2):
            last_copy(chunk, me_x, lax.rem(me_x + step, NX)).wait_recv()
        for quad in range(4 // CHUNKS):
            parts = [last[chunk, x, :, 128 * quad : 128 * quad + 128] for x in range(NX)]
            parts = block_transpose(parts)
            for j in range(4):
                s = chunk * NSRC // CHUNKS + quad * 4 + j
                out[:, 128 * s : 128 * s + 128] = parts[j]

    for step in (1, 2, 3):
        near_copy(lax.rem(me_near + step, near), me_near).wait_send()

    @pl.loop(1, ny)
    def _(step):
        y_copy(lax.rem(me_y + step, ny), me_y).wait_send()

    @pl.loop(1, side)
    def _(step):
        side_copy(lax.rem(me_side + step, side), me_side).wait_send()

    @pl.loop(0, side)
    def _(slot):
        core_copy(me_core, slot).wait_send()

    for step in (1, 2, 3):
        to = lax.rem(me_x + step, NX)
        white_copy(to, me_x).wait_send()
        for chunk in range(CHUNKS):
            last_copy(chunk, to, me_x).wait_send()
    for chunk in range(CHUNKS):
        for kind in range(3):
            for way in range(2):
                z_copy(chunk, kind, way).wait_send()


def local(ny, record, offsets, sources):
    lag_rows = HALF // NZ
    own = lag_rows // NX
    upper, lower = forward_tables()
    inverse = inverse_table(NZ * NX * WIN)
    tables = np.concatenate([upper, lower, inverse], axis=0)
    vmem = pl.BlockSpec(memory_space=pltpu.VMEM)
    hbm = pl.BlockSpec(memory_space=pltpu.HBM)
    dma = pltpu.SemaphoreType.DMA
    flat = pl.pallas_call(
        functools.partial(kernel, ny),
        out_shape=jax.ShapeDtypeStruct((own, NSRC * ROWS), BF16),
        in_specs=[hbm, hbm, vmem, hbm],
        out_specs=vmem,
        scratch_shapes=[
            pltpu.SMEM((WIN,), jnp.int32),
            pltpu.SMEM((NSRC,), jnp.int32),
            pltpu.VMEM((SAMPLES, SAMPLES), BF16),
            pltpu.VMEM((SAMPLES, SAMPLES), BF16),
            pltpu.VMEM((HALF, SAMPLES), BF16),
            pltpu.VMEM((256, SAMPLES), BF16),
            pltpu.VMEM((2 * NLOW, 16, HALF), BF16),
            pltpu.VMEM((2 * NLOW, 16, HALF), BF16),
            pltpu.VMEM((ny, 16, HALF), BF16),
            pltpu.VMEM((2, NLOW * NX, 16, HALF), BF16),
            pltpu.VMEM((SAMPLES, 256), F32),
            pltpu.VMEM((NX, HALF, 128), BF16),
            pltpu.VMEM((NX, HALF, 128), BF16),
            pltpu.VMEM((8, 2, 2, 64, 128), BF16),
            pltpu.VMEM((HALF, 512), BF16),
            pltpu.VMEM((GROUPS, 256, 512), BF16),
            pltpu.VMEM((4, SAMPLES, 128), F32),
            pltpu.VMEM((SAMPLES, 512), BF16),
            pltpu.VMEM((CHUNKS, 3, lag_rows, WIDE), BF16),
            pltpu.VMEM((CHUNKS, 2, lag_rows // 2, WIDE), BF16),
            pltpu.VMEM((CHUNKS, 4, lag_rows // 2, WIDE), F32),
            pltpu.VMEM((CHUNKS, 3, 2, lag_rows // 2, WIDE), BF16),
            pltpu.VMEM((CHUNKS, lag_rows, WIDE), BF16),
            pltpu.VMEM((CHUNKS, NX, own, WIDE), BF16),
            dma((5,)),
            dma((2 * NLOW,)),
            dma((2 * NLOW,)),
            dma((ny,)),
            dma((ny,)),
            dma((NLOW * NX,)),
            dma((NLOW * NX,)),
            dma((NLOW * NX,)),
            dma((NLOW * NX,)),
            dma((NX,)),
            dma((NX,)),
            dma((CHUNKS, 3, 2)),
            dma((CHUNKS, 3, 2)),
            dma((CHUNKS, NX)),
            dma((CHUNKS, NX)),
        ],
        compiler_params=pltpu.CompilerParams(
            collective_id=0, has_side_effects=True, vmem_limit_bytes=60 * 1024 * 1024
        ),
        cost_estimate=pl.CostEstimate(
            flops=3 * 10**9, bytes_accessed=7 * 10**6, transcendentals=10**6
        ),
    )(
        offsets,
        sources,
        jnp.transpose(record, (1, 0, 2)),
        jnp.asarray(tables),
    )
    return flat.reshape(own, NSRC, ROWS)


def solution(mesh):
    ny = mesh.shape["chan"] // (2 * NLOW)
    in_specs = (P("chan", "spec", None), P("spec"), P())
    out_specs = P("spec", None, "chan")
    return jax.shard_map(
        functools.partial(local, ny),
        mesh=mesh,
        in_specs=in_specs,
        out_specs=out_specs,
        check_vma=False,
    )
```

```python
import functools
import math

import jax
import jax.numpy as jnp
import numpy as np
from jax import lax
from jax.experimental import pallas as pl
from jax.experimental.pallas import tpu as pltpu
from jax.sharding import PartitionSpec as P

SAMPLES = 1024
HALF = SAMPLES // 2
PAD = 128
NSRC = 16
WATER = 0.1
NX = 4
ROWS = 128
WIN = 2
BLK = ROWS // NX
GROUPS = 32
NLOW = 2
NZ = 4
CHUNKS = 2
WIDE = NSRC * BLK // CHUNKS
F32 = jnp.float32
BF16 = jnp.bfloat16
MESH = pl.DeviceIdType.MESH


def forward_tables():
    rows = np.arange(SAMPLES)[:, None]
    cols = np.arange(SAMPLES)[None, :]
    freq = rows % HALF
    angle = 2.0 * np.pi / SAMPLES * (freq * cols % SAMPLES)
    alternating = 1.0 - 2.0 * (cols % 2)
    imag = np.where(freq == 0, alternating, -np.sin(angle))
    table = np.where(rows < HALF, np.cos(angle), imag)
    upper = table.astype(jnp.bfloat16)
    lower = (table - upper.astype(np.float64)).astype(jnp.bfloat16)
    return upper, lower


def inverse_table(windows):
    shifted = np.arange(HALF)[:, None] - HALF // 2
    freq = (np.arange(16)[:, None] + 16 * np.arange(GROUPS)[None, :]).reshape(1, -1)
    angle = 2.0 * np.pi / SAMPLES * (freq * shifted % SAMPLES)
    alternating = 1.0 - 2.0 * (shifted % 2)
    first = freq == 0
    real = np.where(first, 1.0, 2.0 * np.cos(angle))
    imag = np.where(first, alternating, -2.0 * np.sin(angle))
    table = np.concatenate([real, imag], axis=1) / math.sqrt(windows * SAMPLES)
    return table.astype(jnp.bfloat16)


def dot_t(left, right):
    return lax.dot_general(left, right, (((1,), (1,)), ((), ())), preferred_element_type=F32)


def dot(left, right):
    return lax.dot_general(left, right, (((1,), (0,)), ((), ())), preferred_element_type=F32)


def block_transpose(parts):
    count = len(parts)
    width = 128 // count
    lane = lax.broadcasted_iota(jnp.int32, parts[0].shape, 1)
    masks = [lane // width == i for i in range(count - 1)]

    def pick(choices):
        result = choices[-1]
        for mask, choice in zip(masks, choices):
            result = jnp.where(mask, choice, result)
        return result

    turned = []
    for d in range(count):
        part = pick([parts[(i - d) % count] for i in range(count)])
        turned.append(pltpu.roll(part, 128 - width * d, 1) if d else part)
    return [pick([turned[(j - i) % count] for i in range(count)]) for j in range(count)]


def kernel(
    ny,
    offsets_hbm,
    sources_hbm,
    record,
    tables_hbm,
    out,
    offsets,
    sources,
    upper,
    lower,
    inverse,
    traces,
    pieces,
    reduced,
    parts_y,
    picked,
    spectrum,
    outgoing,
    incoming,
    left,
    copies,
    right,
    cross,
    stacked,
    lags_out,
    mixed,
    kept,
    lags_in,
    finished,
    last,
    load_sem,
    near_send,
    near_recv,
    y_send,
    y_recv,
    side_send,
    side_recv,
    core_send,
    core_recv,
    white_send,
    white_recv,
    z_send,
    z_recv,
    last_send,
    last_recv,
):
    plane = 2 * ny
    side = NLOW * NX
    near = NLOW * 2
    chan = lax.axis_index("chan")
    spec = lax.axis_index("spec")
    me_x = lax.rem(spec, NX)
    me_z = spec // NX
    me_low = chan // plane
    me_plane = lax.rem(chan, plane)
    me_y = me_plane // 2
    me_core = lax.rem(chan, 2)
    me_side = me_low * NX + me_x
    me_near = me_low * 2 + me_core

    def at_near(other):
        return (other // 2 * plane + me_y * 2 + lax.rem(other, 2), spec)

    def at_y(other):
        return (me_low * plane + other * 2 + me_core, spec)

    def at_side(other):
        return (other // NX * plane + me_plane, me_z * NX + lax.rem(other, NX))

    def at_x(other):
        return (chan, me_z * NX + other)

    def at_z(other):
        return (chan, other * NX + me_x)

    loads = [
        pltpu.make_async_copy(source, target, load_sem.at[i])
        for i, (source, target) in enumerate(
            [
                (offsets_hbm, offsets),
                (sources_hbm, sources),
                (tables_hbm.at[pl.ds(0, SAMPLES)], upper),
                (tables_hbm.at[pl.ds(SAMPLES, SAMPLES)], lower),
                (tables_hbm.at[pl.ds(2 * SAMPLES, HALF)], inverse),
            ]
        )
    ]
    for load in loads:
        load.start()

    barrier = pltpu.get_barrier_semaphore()

    def greet(device):
        pl.semaphore_signal(barrier, inc=1, device_id=device, device_id_type=MESH)

    greet(at_near(me_low * 2 + 1 - me_core))
    greet(at_near((1 - me_low) * 2 + 1 - me_core))

    @pl.loop(1, ny)
    def _(step):
        greet(at_y(lax.rem(me_y + step, ny)))

    @pl.loop(1, side)
    def _(step):
        greet(at_side(lax.rem(me_side + step, side)))

    for step in (1, NZ - 1):
        greet(at_z(lax.rem(me_z + step, NZ)))

    loads[0].wait()
    loads[1].wait()

    lane = lax.broadcasted_iota(jnp.int32, (ROWS, 128), 1)
    for w in range(WIN):
        rows = record[w].astype(F32)
        head = jnp.where(lane < offsets[w], rows[:, SAMPLES:], rows[:, :PAD])
        rows = jnp.concatenate([head, rows[:, PAD:SAMPLES]], axis=1)
        rows = rows - jnp.mean(rows, axis=1, keepdims=True)
        rows = rows * lax.rsqrt(jnp.mean(rows * rows, axis=1, keepdims=True) + 1e-06)
        rows = rows.astype(BF16)
        for x in range(NX):
            traces[pl.ds(x * 64 + w * BLK, BLK), :] = rows[x * BLK : (x + 1) * BLK]

    row = lax.broadcasted_iota(jnp.int32, (32, 256), 0)
    col = lax.broadcasted_iota(jnp.int32, (32, 256), 1)
    wanted = jnp.zeros((32, 256), jnp.int32)
    for s in range(NSRC):
        wanted = jnp.where(row % NSRC == s, sources[s], wanted)
    channel = chan * ROWS + (col // 64) * BLK + col % BLK
    same = jnp.logical_and(wanted == channel, row // NSRC == (col // BLK) % 2)
    chosen = dot(jnp.where(same, 1.0, 0.0).astype(BF16), traces[...])
    for w in range(WIN):
        for low in range(NLOW):
            rows = chosen[16 * w + 8 * low : 16 * w + 8 * low + 8]
            rows = jnp.concatenate([rows[:, :HALF], rows[:, HALF:]], axis=0)
            pieces[low * 2 + w] = rows.astype(BF16)

    pl.semaphore_wait(barrier, 2 + ny - 1 + side - 1 + 2)

    def near_copy(to, slot):
        return pltpu.make_async_remote_copy(
            src_ref=pieces.at[to],
            dst_ref=reduced.at[slot],
            send_sem=near_send.at[to],
            recv_sem=near_recv.at[slot],
            device_id=at_near(to),
            device_id_type=MESH,
        )

    for step in (2, 3, 1):
        near_copy(lax.rem(me_near + step, near), me_near).start()
    reduced[me_near] = pieces[me_near]
    loads[2].wait()
    loads[3].wait()

    spectrum[...] = dot_t(upper[...], traces[...])
    spectrum[...] += dot_t(lower[...], traces[...])

    for step in (1, 2, 3):
        near_copy(me_near, lax.rem(me_near + step, near)).wait_recv()
    total = reduced[0].astype(F32)
    for i in range(1, near):
        total = total + reduced[i].astype(F32)
    parts_y[me_y] = total.astype(BF16)

    def y_copy(to, slot):
        return pltpu.make_async_remote_copy(
            src_ref=parts_y.at[me_y],
            dst_ref=parts_y.at[slot],
            send_sem=y_send.at[to],
            recv_sem=y_recv.at[slot],
            device_id=at_y(to),
            device_id_type=MESH,
        )

    for step in sorted(range(1, ny), key=lambda step: -min(step, ny - step)):
        y_copy(lax.rem(me_y + step, ny), me_y).start()

    chunk = 64
    first_row = lax.broadcasted_iota(jnp.int32, (chunk, 256), 0) == 0
    total = jnp.zeros((1, 256), F32)
    for k in range(0, HALF, chunk):
        re = spectrum[k : k + chunk]
        im = spectrum[HALF + k : HALF + k + chunk]
        size = jnp.sqrt(re * re + im * im)
        if k == 0:
            size = jnp.where(first_row, jnp.abs(re) + jnp.abs(im), size)
        total = total + jnp.sum(size, axis=0, keepdims=True)
    level = WATER * (total / (HALF + 1) + 1e-06)
    low = lax.broadcasted_iota(jnp.int32, (chunk, 128), 1) < 64
    for k in range(0, HALF, chunk):
        re = spectrum[k : k + chunk]
        im = spectrum[HALF + k : HALF + k + chunk]
        size = jnp.sqrt(re * re + im * im)
        if k == 0:
            re = re / (jnp.where(first_row, jnp.abs(re), size) + level)
            im = im / (jnp.where(first_row, jnp.abs(im), size) + level)
        else:
            scale = 1.0 / (size + level)
            re = re * scale
            im = im * scale
        for pair in range(2):
            a = re[:, 128 * pair : 128 * pair + 128]
            b = im[:, 128 * pair : 128 * pair + 128]
            even = jnp.where(low, a, pltpu.roll(b, 64, 1))
            odd = jnp.where(low, pltpu.roll(a, 64, 1), b)
            outgoing[2 * pair, k : k + chunk] = even.astype(BF16)
            outgoing[2 * pair + 1, k : k + chunk] = odd.astype(BF16)

    def white_copy(to, slot):
        return pltpu.make_async_remote_copy(
            src_ref=outgoing.at[to],
            dst_ref=incoming.at[slot],
            send_sem=white_send.at[to],
            recv_sem=white_recv.at[slot],
            device_id=at_x(to),
            device_id_type=MESH,
        )

    for step in (2, 1, 3):
        white_copy(lax.rem(me_x + step, NX), me_x).start()
    incoming[me_x] = outgoing[me_x]

    r = lax.broadcasted_iota(jnp.int32, (128, 512), 0)
    c = lax.broadcasted_iota(jnp.int32, (128, 512), 1)
    match = jnp.logical_and(r // BLK == c // 128, r % BLK == c % BLK)
    spread = jnp.where(match, 1.0, 0.0).astype(BF16)
    r = lax.broadcasted_iota(jnp.int32, (16, 512), 0)
    c = lax.broadcasted_iota(jnp.int32, (16, 512), 1)
    mask = jnp.where(r == c // BLK, 1.0, 0.0).astype(BF16)

    def widen(x):
        copies[...] = dot(incoming[x], spread).astype(BF16)

        @pl.loop(0, 8)
        def _(small):
            for big in range(4):
                group = big * 8 + small
                at = pl.ds(pl.multiple_of(group * 16, 16), 16)
                for p in range(2):
                    for w in range(WIN):
                        quarter = p * 2 + w
                        tile = copies[at, quarter * 128 : quarter * 128 + 128]
                        slab = pl.multiple_of((p * 8 + x * 2 + w) * 16, 16)
                        right[group, pl.ds(slab, 16), :] = (
                            jnp.concatenate([tile] * 4, axis=1) * mask
                        )

    widen(me_x)

    @pl.loop(1, ny)
    def _(step):
        y_copy(me_y, lax.rem(me_y + step, ny)).wait_recv()

    total = parts_y[0].astype(F32)
    for i in range(1, ny):
        total = total + parts_y[i].astype(F32)
    rows = jnp.concatenate([total[:8], total[8:]], axis=1).astype(BF16)
    both = dot_t(rows, upper[...]) + dot_t(rows, lower[...])
    re = both[:, :HALF]
    im = both[:, HALF:]
    size = jnp.sqrt(re * re + im * im)
    first = lax.broadcasted_iota(jnp.int32, (8, HALF), 1) == 0
    total = jnp.sum(
        jnp.where(first, jnp.abs(re) + jnp.abs(im), size), axis=1, keepdims=True
    )
    level = WATER * (total / (HALF + 1) + 1e-06)
    re = re / (jnp.where(first, jnp.abs(re), size) + level)
    im = im / (jnp.where(first, jnp.abs(im), size) + level)
    picked[me_core, me_side] = jnp.concatenate([re, im], axis=0).astype(BF16)

    def side_copy(to, slot):
        return pltpu.make_async_remote_copy(
            src_ref=picked.at[me_core, me_side],
            dst_ref=picked.at[me_core, slot],
            send_sem=side_send.at[to],
            recv_sem=side_recv.at[slot],
            device_id=at_side(to),
            device_id_type=MESH,
        )

    def core_copy(core, slot):
        return pltpu.make_async_remote_copy(
            src_ref=picked.at[core, slot],
            dst_ref=picked.at[core, slot],
            send_sem=core_send.at[slot],
            recv_sem=core_recv.at[slot],
            device_id=at_near(me_low * 2 + 1 - me_core),
            device_id_type=MESH,
        )

    @pl.loop(1, side)
    def _(step):
        side_copy(lax.rem(me_side + step, side), me_side).start()

    core_copy(me_core, me_side).start()

    def widen_next(step):
        x = lax.rem(me_x + step, NX)
        white_copy(me_x, x).wait_recv()
        widen(x)

    widen_next(1)
    widen_next(3)

    @pl.loop(1, side)
    def _(step):
        slot = lax.rem(me_side + step, side)
        side_copy(me_side, slot).wait_recv()
        core_copy(me_core, slot).start()

    widen_next(2)

    @pl.loop(0, side)
    def _(slot):
        core_copy(1 - me_core, slot).wait_recv()

    parts = []
    for x in range(NX):
        for w in range(WIN):
            tiles = []
            halves = [picked[w, low * NX + x].astype(F32) for low in range(NLOW)]
            for part in range(2):
                for big in range(4):
                    for half in halves:
                        tiles.append(
                            half[8 * part : 8 * part + 8, 128 * big : 128 * big + 128]
                        )
            parts.append(jnp.concatenate(tiles, axis=0))
    parts = block_transpose(parts)
    for small in range(8):
        a_re = parts[small][:64].astype(BF16)
        a_im = parts[small][64:].astype(BF16)
        re_b0, re_b1, im_b0, im_b1 = a_re, a_im, -a_im, a_re
        if small == 0:
            shape = (64, 128)
            zero_bin = jnp.logical_and(
                lax.broadcasted_iota(jnp.int32, shape, 0) < 16,
                lax.broadcasted_iota(jnp.int32, shape, 1) % 16 == 0,
            )
            zero = jnp.zeros(shape, BF16)
            re_b1 = jnp.where(zero_bin, zero, re_b1)
            im_b0 = jnp.where(zero_bin, zero, im_b0)
            im_b1 = jnp.where(zero_bin, a_im, im_b1)
        left[small, 0, 0] = re_b0
        left[small, 0, 1] = re_b1
        left[small, 1, 0] = im_b0
        left[small, 1, 1] = im_b1

    @pl.loop(0, 8)
    def _(small):
        for big in range(4):
            group = big * 8 + small
            rows_left = jnp.concatenate(
                [
                    jnp.concatenate(
                        [left[small, part, p, big * 16 : big * 16 + 16, :] for p in range(2)],
                        axis=1,
                    )
                    for part in range(2)
                ],
                axis=0,
            )
            result = dot(rows_left, right[group])
            for h in range(4):
                cross[h, pl.ds(group, 32, stride=32), :] = result[:, 128 * h : 128 * h + 128]

    loads[4].wait()

    ahead = lax.rem(me_z + 1, NZ)
    behind = lax.rem(me_z + NZ - 1, NZ)
    lag_rows = HALF // NZ
    top = pl.ds(0, lag_rows // 2)
    bottom = pl.ds(lag_rows // 2, lag_rows // 2)

    def z_copy(chunk, kind, way, to=None):
        source = [
            (lags_out.at[chunk, 1, top], lags_out.at[chunk, 1, bottom]),
            (lags_out.at[chunk, 0, bottom], lags_out.at[chunk, 2, top]),
            (mixed.at[chunk, 0], mixed.at[chunk, 1]),
        ][kind][way]
        return pltpu.make_async_remote_copy(
            src_ref=source,
            dst_ref=lags_in.at[chunk, kind, way],
            send_sem=z_send.at[chunk, kind, way],
            recv_sem=z_recv.at[chunk, kind, way],
            device_id=at_z((ahead, behind)[way]),
            device_id_type=MESH,
        )

    def lag_block(to, chunk):
        at = pl.ds(pl.multiple_of(to * lag_rows, lag_rows), lag_rows)
        return dot(inverse[at, :], stacked[:, WIDE * chunk : WIDE * chunk + WIDE])

    for chunk in range(CHUNKS):
        for part in range(2):
            for quad in range(chunk * 4 // CHUNKS, (chunk + 1) * 4 // CHUNKS):
                for h in range(4):
                    parts = [
                        cross[h, pl.ds((part * 16 + quad * 4 + i) * 32, 32), :].astype(BF16)
                        for i in range(4)
                    ]
                    parts = block_transpose(parts)
                    for j in range(4):
                        at = (part * 16 + h * 4 + j) * 32
                        stacked[at : at + 32, 128 * quad : 128 * quad + 128] = parts[j]
        lags_out[chunk, 1] = lag_block(lax.rem(me_z + 2, NZ), chunk).astype(BF16)
        z_copy(chunk, 0, 0).start()
        z_copy(chunk, 0, 1).start()
        block = lag_block(ahead, chunk)
        lags_out[chunk, 0] = block.astype(BF16)
        kept[chunk, 0] = block[: lag_rows // 2]
        z_copy(chunk, 1, 0).start()
        block = lag_block(behind, chunk)
        lags_out[chunk, 2] = block.astype(BF16)
        kept[chunk, 1] = block[lag_rows // 2 :]
        z_copy(chunk, 1, 1).start()
        block = lag_block(me_z, chunk)
        kept[chunk, 2] = block[: lag_rows // 2]
        kept[chunk, 3] = block[lag_rows // 2 :]

    for chunk in range(CHUNKS):
        for way in range(2):
            z_copy(chunk, 0, way).wait_recv()
            total = kept[chunk, way] + lags_in[chunk, 0, way].astype(F32)
            mixed[chunk, way] = total.astype(BF16)
            z_copy(chunk, 2, way).start()

    own = lag_rows // NX

    def last_copy(chunk, to, slot):
        at = pl.ds(pl.multiple_of(to * own, own), own)
        return pltpu.make_async_remote_copy(
            src_ref=finished.at[chunk, at],
            dst_ref=last.at[chunk, slot],
            send_sem=last_send.at[chunk, to],
            recv_sem=last_recv.at[chunk, slot],
            device_id=at_x(to),
            device_id_type=MESH,
        )

    for chunk in range(CHUNKS):
        for kind in (1, 2):
            for way in range(2):
                z_copy(chunk, kind, way).wait_recv()
        for half in range(2):
            total = (
                kept[chunk, 2 + half]
                + lags_in[chunk, 2, half].astype(F32)
                + lags_in[chunk, 1, 1 - half].astype(F32)
            )
            finished[chunk, pl.ds(half * lag_rows // 2, lag_rows // 2)] = total.astype(BF16)
        for step in (2, 1, 3):
            last_copy(chunk, lax.rem(me_x + step, NX), me_x).start()
        last[chunk, me_x] = finished[chunk, pl.ds(pl.multiple_of(me_x * own, own), own), :]

    for chunk in range(CHUNKS):
        for step in (1, 3, 2):
            last_copy(chunk, me_x, lax.rem(me_x + step, NX)).wait_recv()
        for quad in range(4 // CHUNKS):
            parts = [last[chunk, x, :, 128 * quad : 128 * quad + 128] for x in range(NX)]
            parts = block_transpose(parts)
            for j in range(4):
                s = chunk * NSRC // CHUNKS + quad * 4 + j
                out[:, 128 * s : 128 * s + 128] = parts[j]

    for step in (1, 2, 3):
        near_copy(lax.rem(me_near + step, near), me_near).wait_send()

    @pl.loop(1, ny)
    def _(step):
        y_copy(lax.rem(me_y + step, ny), me_y).wait_send()

    @pl.loop(1, side)
    def _(step):
        side_copy(lax.rem(me_side + step, side), me_side).wait_send()

    @pl.loop(0, side)
    def _(slot):
        core_copy(me_core, slot).wait_send()

    for step in (1, 2, 3):
        to = lax.rem(me_x + step, NX)
        white_copy(to, me_x).wait_send()
        for chunk in range(CHUNKS):
            last_copy(chunk, to, me_x).wait_send()
    for chunk in range(CHUNKS):
        for kind in range(3):
            for way in range(2):
                z_copy(chunk, kind, way).wait_send()


def local(ny, record, offsets, sources):
    lag_rows = HALF // NZ
    own = lag_rows // NX
    upper, lower = forward_tables()
    inverse = inverse_table(NZ * NX * WIN)
    tables = np.concatenate([upper, lower, inverse], axis=0)
    vmem = pl.BlockSpec(memory_space=pltpu.VMEM)
    hbm = pl.BlockSpec(memory_space=pltpu.HBM)
    dma = pltpu.SemaphoreType.DMA
    flat = pl.pallas_call(
        functools.partial(kernel, ny),
        out_shape=jax.ShapeDtypeStruct((own, NSRC * ROWS), BF16),
        in_specs=[hbm, hbm, vmem, hbm],
        out_specs=vmem,
        scratch_shapes=[
            pltpu.SMEM((WIN,), jnp.int32),
            pltpu.SMEM((NSRC,), jnp.int32),
            pltpu.VMEM((SAMPLES, SAMPLES), BF16),
            pltpu.VMEM((SAMPLES, SAMPLES), BF16),
            pltpu.VMEM((HALF, SAMPLES), BF16),
            pltpu.VMEM((256, SAMPLES), BF16),
            pltpu.VMEM((2 * NLOW, 16, HALF), BF16),
            pltpu.VMEM((2 * NLOW, 16, HALF), BF16),
            pltpu.VMEM((ny, 16, HALF), BF16),
            pltpu.VMEM((2, NLOW * NX, 16, HALF), BF16),
            pltpu.VMEM((SAMPLES, 256), F32),
            pltpu.VMEM((NX, HALF, 128), BF16),
            pltpu.VMEM((NX, HALF, 128), BF16),
            pltpu.VMEM((8, 2, 2, 64, 128), BF16),
            pltpu.VMEM((HALF, 512), BF16),
            pltpu.VMEM((GROUPS, 256, 512), BF16),
            pltpu.VMEM((4, SAMPLES, 128), F32),
            pltpu.VMEM((SAMPLES, 512), BF16),
            pltpu.VMEM((CHUNKS, 3, lag_rows, WIDE), BF16),
            pltpu.VMEM((CHUNKS, 2, lag_rows // 2, WIDE), BF16),
            pltpu.VMEM((CHUNKS, 4, lag_rows // 2, WIDE), F32),
            pltpu.VMEM((CHUNKS, 3, 2, lag_rows // 2, WIDE), BF16),
            pltpu.VMEM((CHUNKS, lag_rows, WIDE), BF16),
            pltpu.VMEM((CHUNKS, NX, own, WIDE), BF16),
            dma((5,)),
            dma((2 * NLOW,)),
            dma((2 * NLOW,)),
            dma((ny,)),
            dma((ny,)),
            dma((NLOW * NX,)),
            dma((NLOW * NX,)),
            dma((NLOW * NX,)),
            dma((NLOW * NX,)),
            dma((NX,)),
            dma((NX,)),
            dma((CHUNKS, 3, 2)),
            dma((CHUNKS, 3, 2)),
            dma((CHUNKS, NX)),
            dma((CHUNKS, NX)),
        ],
        compiler_params=pltpu.CompilerParams(
            collective_id=0, has_side_effects=True, vmem_limit_bytes=53 * 1024 * 1024
        ),
        cost_estimate=pl.CostEstimate(
            flops=3 * 10**9, bytes_accessed=7 * 10**6, transcendentals=10**6
        ),
    )(
        offsets,
        sources,
        jnp.transpose(record, (1, 0, 2)),
        jnp.asarray(tables),
    )
    return flat.reshape(own, NSRC, ROWS)


def solution(mesh):
    ny = mesh.shape["chan"] // (2 * NLOW)
    in_specs = (P("chan", "spec", None), P("spec"), P())
    out_specs = P("spec", None, "chan")
    return jax.shard_map(
        functools.partial(local, ny),
        mesh=mesh,
        in_specs=in_specs,
        out_specs=out_specs,
        check_vma=False,
    )
```

```python
import functools
import math

import jax
import jax.numpy as jnp
import numpy as np
from jax import lax
from jax.experimental import pallas as pl
from jax.experimental.pallas import tpu as pltpu
from jax.sharding import PartitionSpec as P

SAMPLES = 1024
HALF = SAMPLES // 2
PAD = 128
NSRC = 16
WATER = 0.1
NX = 4
ROWS = 128
WIN = 2
BLK = ROWS // NX
GROUPS = 32
NLOW = 2
NZ = 4
CHUNKS = 2
PART = BLK // CHUNKS
WIDE = NSRC * PART
F32 = jnp.float32
BF16 = jnp.bfloat16
MESH = pl.DeviceIdType.MESH


def forward_tables():
    rows = np.arange(SAMPLES)[:, None]
    cols = np.arange(SAMPLES)[None, :]
    freq = rows % HALF
    angle = 2.0 * np.pi / SAMPLES * (freq * cols % SAMPLES)
    alternating = 1.0 - 2.0 * (cols % 2)
    imag = np.where(freq == 0, alternating, -np.sin(angle))
    table = np.where(rows < HALF, np.cos(angle), imag)
    upper = table.astype(jnp.bfloat16)
    lower = (table - upper.astype(np.float64)).astype(jnp.bfloat16)
    return upper, lower


def inverse_table(windows):
    shifted = np.arange(HALF)[:, None] - HALF // 2
    freq = (np.arange(16)[:, None] + 16 * np.arange(GROUPS)[None, :]).reshape(1, -1)
    angle = 2.0 * np.pi / SAMPLES * (freq * shifted % SAMPLES)
    alternating = 1.0 - 2.0 * (shifted % 2)
    first = freq == 0
    real = np.where(first, 1.0, 2.0 * np.cos(angle))
    imag = np.where(first, alternating, -2.0 * np.sin(angle))
    table = np.concatenate([real, imag], axis=1) / math.sqrt(windows * SAMPLES)
    return table.astype(jnp.bfloat16)


def dot_t(left, right):
    return lax.dot_general(left, right, (((1,), (1,)), ((), ())), preferred_element_type=F32)


def dot(left, right):
    return lax.dot_general(left, right, (((1,), (0,)), ((), ())), preferred_element_type=F32)


def block_transpose(parts):
    count = len(parts)
    width = 128 // count
    lane = lax.broadcasted_iota(jnp.int32, parts[0].shape, 1)
    masks = [lane // width == i for i in range(count - 1)]

    def pick(choices):
        result = choices[-1]
        for mask, choice in zip(masks, choices):
            result = jnp.where(mask, choice, result)
        return result

    turned = []
    for d in range(count):
        part = pick([parts[(i - d) % count] for i in range(count)])
        turned.append(pltpu.roll(part, 128 - width * d, 1) if d else part)
    return [pick([turned[(j - i) % count] for i in range(count)]) for j in range(count)]


def kernel(
    ny,
    offsets_hbm,
    sources_hbm,
    record,
    tables_hbm,
    out,
    offsets,
    sources,
    upper,
    lower,
    inverse,
    traces,
    pieces,
    reduced,
    parts_y,
    picked,
    spectrum,
    outgoing,
    incoming,
    left,
    copies,
    right,
    cross,
    stacked,
    lags_out,
    mixed,
    kept,
    lags_in,
    finished,
    last,
    load_sem,
    near_send,
    near_recv,
    y_send,
    y_recv,
    side_send,
    side_recv,
    white_send,
    white_recv,
    z_send,
    z_recv,
    last_send,
    last_recv,
):
    plane = 2 * ny
    near = NLOW * 2
    chan = lax.axis_index("chan")
    spec = lax.axis_index("spec")
    me_x = lax.rem(spec, NX)
    me_z = spec // NX
    me_low = chan // plane
    me_plane = lax.rem(chan, plane)
    me_y = me_plane // 2
    me_core = lax.rem(chan, 2)
    me_side = me_low * NX + me_x
    me_near = me_low * 2 + me_core

    def at_near(other):
        return (other // 2 * plane + me_y * 2 + lax.rem(other, 2), spec)

    def at_y(other):
        return (me_low * plane + other * 2 + me_core, spec)

    around = sorted(
        (
            (low, x, core)
            for low in range(NLOW)
            for x in range(NX)
            for core in range(2)
            if low + x + core
        ),
        key=lambda step: -(step[0] + 2 * min(step[1], NX - step[1])),
    )

    def moved(step):
        low = lax.rem(me_low + step[0], NLOW)
        x = lax.rem(me_x + step[1], NX)
        core = lax.rem(me_core + step[2], 2)
        device = (low * plane + me_y * 2 + core, me_z * NX + x)
        return device, core, low * NX + x

    def at_x(other):
        return (chan, me_z * NX + other)

    def at_z(other):
        return (chan, other * NX + me_x)

    loads = [
        pltpu.make_async_copy(source, target, load_sem.at[i])
        for i, (source, target) in enumerate(
            [
                (offsets_hbm, offsets),
                (sources_hbm, sources),
                (tables_hbm.at[pl.ds(0, SAMPLES)], upper),
                (tables_hbm.at[pl.ds(SAMPLES, SAMPLES)], lower),
                (tables_hbm.at[pl.ds(2 * SAMPLES, HALF)], inverse),
            ]
        )
    ]
    for load in loads:
        load.start()

    barrier = pltpu.get_barrier_semaphore()

    def greet(device):
        pl.semaphore_signal(barrier, inc=1, device_id=device, device_id_type=MESH)

    @pl.loop(1, ny)
    def _(step):
        greet(at_y(lax.rem(me_y + step, ny)))

    for step in around:
        greet(moved(step)[0])

    for step in (1, NZ - 1):
        greet(at_z(lax.rem(me_z + step, NZ)))

    loads[0].wait()
    loads[1].wait()

    lane = lax.broadcasted_iota(jnp.int32, (ROWS, 128), 1)
    for w in range(WIN):
        rows = record[w].astype(F32)
        head = jnp.where(lane < offsets[w], rows[:, SAMPLES:], rows[:, :PAD])
        rows = jnp.concatenate([head, rows[:, PAD:SAMPLES]], axis=1)
        rows = rows - jnp.mean(rows, axis=1, keepdims=True)
        rows = rows * lax.rsqrt(jnp.mean(rows * rows, axis=1, keepdims=True) + 1e-06)
        rows = rows.astype(BF16)
        for x in range(NX):
            traces[pl.ds(x * 64 + w * BLK, BLK), :] = rows[x * BLK : (x + 1) * BLK]

    row = lax.broadcasted_iota(jnp.int32, (32, 256), 0)
    col = lax.broadcasted_iota(jnp.int32, (32, 256), 1)
    wanted = jnp.zeros((32, 256), jnp.int32)
    for s in range(NSRC):
        wanted = jnp.where(row % NSRC == s, sources[s], wanted)
    channel = chan * ROWS + (col // 64) * BLK + col % BLK
    same = jnp.logical_and(wanted == channel, row // NSRC == (col // BLK) % 2)
    chosen = dot(jnp.where(same, 1.0, 0.0).astype(BF16), traces[...])
    for w in range(WIN):
        for low in range(NLOW):
            rows = chosen[16 * w + 8 * low : 16 * w + 8 * low + 8]
            rows = jnp.concatenate([rows[:, :HALF], rows[:, HALF:]], axis=0)
            pieces[low * 2 + w] = rows.astype(BF16)

    pl.semaphore_wait(barrier, ny - 1 + len(around) + 2)

    def near_copy(to, slot):
        return pltpu.make_async_remote_copy(
            src_ref=pieces.at[to],
            dst_ref=reduced.at[slot],
            send_sem=near_send.at[to],
            recv_sem=near_recv.at[slot],
            device_id=at_near(to),
            device_id_type=MESH,
        )

    for step in (2, 3, 1):
        near_copy(lax.rem(me_near + step, near), me_near).start()
    reduced[me_near] = pieces[me_near]
    loads[2].wait()
    spectrum[...] = dot_t(upper[...], traces[...])

    for step in (1, 2, 3):
        near_copy(me_near, lax.rem(me_near + step, near)).wait_recv()
    total = reduced[0].astype(F32)
    for i in range(1, near):
        total = total + reduced[i].astype(F32)
    parts_y[me_y] = total.astype(BF16)

    def y_copy(to, slot):
        return pltpu.make_async_remote_copy(
            src_ref=parts_y.at[me_y],
            dst_ref=parts_y.at[slot],
            send_sem=y_send.at[to],
            recv_sem=y_recv.at[slot],
            device_id=at_y(to),
            device_id_type=MESH,
        )

    for step in sorted(range(1, ny), key=lambda step: -min(step, ny - step)):
        y_copy(lax.rem(me_y + step, ny), me_y).start()

    loads[3].wait()
    spectrum[...] += dot_t(lower[...], traces[...])

    chunk = 64
    first_row = lax.broadcasted_iota(jnp.int32, (chunk, 256), 0) == 0
    total = jnp.zeros((1, 256), F32)
    for k in range(0, HALF, chunk):
        re = spectrum[k : k + chunk]
        im = spectrum[HALF + k : HALF + k + chunk]
        size = jnp.sqrt(re * re + im * im)
        if k == 0:
            size = jnp.where(first_row, jnp.abs(re) + jnp.abs(im), size)
        total = total + jnp.sum(size, axis=0, keepdims=True)
    level = WATER * (total / (HALF + 1) + 1e-06)
    low = lax.broadcasted_iota(jnp.int32, (chunk, 128), 1) < 64
    for k in range(0, HALF, chunk):
        re = spectrum[k : k + chunk]
        im = spectrum[HALF + k : HALF + k + chunk]
        size = jnp.sqrt(re * re + im * im)
        if k == 0:
            re = re / (jnp.where(first_row, jnp.abs(re), size) + level)
            im = im / (jnp.where(first_row, jnp.abs(im), size) + level)
        else:
            scale = 1.0 / (size + level)
            re = re * scale
            im = im * scale
        for pair in range(2):
            a = re[:, 128 * pair : 128 * pair + 128]
            b = im[:, 128 * pair : 128 * pair + 128]
            even = jnp.where(low, a, pltpu.roll(b, 64, 1))
            odd = jnp.where(low, pltpu.roll(a, 64, 1), b)
            outgoing[2 * pair, k : k + chunk] = even.astype(BF16)
            outgoing[2 * pair + 1, k : k + chunk] = odd.astype(BF16)

    def white_copy(to, slot):
        return pltpu.make_async_remote_copy(
            src_ref=outgoing.at[to],
            dst_ref=incoming.at[slot],
            send_sem=white_send.at[to],
            recv_sem=white_recv.at[slot],
            device_id=at_x(to),
            device_id_type=MESH,
        )

    for step in (2, 1, 3):
        white_copy(lax.rem(me_x + step, NX), me_x).start()
    incoming[me_x] = outgoing[me_x]

    r = lax.broadcasted_iota(jnp.int32, (128, 1024), 0)
    c = lax.broadcasted_iota(jnp.int32, (128, 1024), 1)
    match = jnp.logical_and(r // BLK == c // 256, r % BLK // PART == c // 128 % 2)
    match = jnp.logical_and(match, r % PART == c % PART)
    spread = jnp.where(match, 1.0, 0.0).astype(BF16)
    r = lax.broadcasted_iota(jnp.int32, (16, 256), 0)
    c = lax.broadcasted_iota(jnp.int32, (16, 256), 1)
    mask = jnp.where(r == c // PART, 1.0, 0.0).astype(BF16)

    def widen(x):
        copies[...] = dot(incoming[x], spread).astype(BF16)

        @pl.loop(0, 8)
        def _(small):
            for big in range(4):
                group = big * 8 + small
                at = pl.ds(pl.multiple_of(group * 16, 16), 16)
                for p in range(2):
                    for w in range(WIN):
                        slab = pl.multiple_of((p * 8 + x * 2 + w) * 16, 16)
                        for chunk in range(CHUNKS):
                            lane = (p * 2 + w) * 256 + chunk * 128
                            tile = copies[at, lane : lane + 128]
                            right[chunk, group, pl.ds(slab, 16), :] = (
                                jnp.concatenate([tile] * 2, axis=1) * mask
                            )

    widen(me_x)

    @pl.loop(1, ny)
    def _(step):
        y_copy(me_y, lax.rem(me_y + step, ny)).wait_recv()

    total = parts_y[0].astype(F32)
    for i in range(1, ny):
        total = total + parts_y[i].astype(F32)
    rows = jnp.concatenate([total[:8], total[8:]], axis=1).astype(BF16)
    both = dot_t(rows, upper[...]) + dot_t(rows, lower[...])
    re = both[:, :HALF]
    im = both[:, HALF:]
    size = jnp.sqrt(re * re + im * im)
    first = lax.broadcasted_iota(jnp.int32, (8, HALF), 1) == 0
    total = jnp.sum(
        jnp.where(first, jnp.abs(re) + jnp.abs(im), size), axis=1, keepdims=True
    )
    level = WATER * (total / (HALF + 1) + 1e-06)
    re = re / (jnp.where(first, jnp.abs(re), size) + level)
    im = im / (jnp.where(first, jnp.abs(im), size) + level)
    picked[me_core, me_side] = jnp.concatenate([re, im], axis=0).astype(BF16)

    def side_copy(step, back=False):
        device, core, slot = moved(step)
        at = (core, slot) if back else (me_core, me_side)
        return pltpu.make_async_remote_copy(
            src_ref=picked.at[me_core, me_side],
            dst_ref=picked.at[at],
            send_sem=side_send.at[core, slot],
            recv_sem=side_recv.at[at],
            device_id=device,
            device_id_type=MESH,
        )

    for step in around:
        side_copy(step).start()

    def widen_next(step):
        x = lax.rem(me_x + step, NX)
        white_copy(me_x, x).wait_recv()
        widen(x)

    widen_next(1)
    widen_next(3)

    widen_next(2)

    for step in around[::-1]:
        side_copy(step, True).wait_recv()

    parts = []
    for x in range(NX):
        for w in range(WIN):
            tiles = []
            halves = [picked[w, low * NX + x].astype(F32) for low in range(NLOW)]
            for part in range(2):
                for big in range(4):
                    for half in halves:
                        tiles.append(
                            half[8 * part : 8 * part + 8, 128 * big : 128 * big + 128]
                        )
            parts.append(jnp.concatenate(tiles, axis=0))
    parts = block_transpose(parts)
    for small in range(8):
        a_re = parts[small][:64].astype(BF16)
        a_im = parts[small][64:].astype(BF16)
        re_b0, re_b1, im_b0, im_b1 = a_re, a_im, -a_im, a_re
        if small == 0:
            shape = (64, 128)
            zero_bin = jnp.logical_and(
                lax.broadcasted_iota(jnp.int32, shape, 0) < 16,
                lax.broadcasted_iota(jnp.int32, shape, 1) % 16 == 0,
            )
            zero = jnp.zeros(shape, BF16)
            re_b1 = jnp.where(zero_bin, zero, re_b1)
            im_b0 = jnp.where(zero_bin, zero, im_b0)
            im_b1 = jnp.where(zero_bin, a_im, im_b1)
        left[small, 0, 0] = re_b0
        left[small, 0, 1] = re_b1
        left[small, 1, 0] = im_b0
        left[small, 1, 1] = im_b1

    def cross_spectra(chunk):
        @pl.loop(0, 8)
        def _(small):
            for big in range(4):
                group = big * 8 + small
                rows_left = jnp.concatenate(
                    [
                        jnp.concatenate(
                            [left[small, part, p, big * 16 : big * 16 + 16, :] for p in range(2)],
                            axis=1,
                        )
                        for part in range(2)
                    ],
                    axis=0,
                )
                result = dot(rows_left, right[chunk, group])
                for h in range(2):
                    cross[chunk, h, pl.ds(group, 32, stride=32), :] = result[
                        :, 128 * h : 128 * h + 128
                    ]

    loads[4].wait()

    ahead = lax.rem(me_z + 1, NZ)
    behind = lax.rem(me_z + NZ - 1, NZ)
    lag_rows = HALF // NZ
    top = pl.ds(0, lag_rows // 2)
    bottom = pl.ds(lag_rows // 2, lag_rows // 2)

    def z_copy(chunk, kind, way, to=None):
        source = [
            (lags_out.at[chunk, 1, top], lags_out.at[chunk, 1, bottom]),
            (lags_out.at[chunk, 0, bottom], lags_out.at[chunk, 2, top]),
            (mixed.at[chunk, 0], mixed.at[chunk, 1]),
        ][kind][way]
        return pltpu.make_async_remote_copy(
            src_ref=source,
            dst_ref=lags_in.at[chunk, kind, way],
            send_sem=z_send.at[chunk, kind, way],
            recv_sem=z_recv.at[chunk, kind, way],
            device_id=at_z((ahead, behind)[way]),
            device_id_type=MESH,
        )

    def lag_block(to, chunk):
        at = pl.ds(pl.multiple_of(to * lag_rows, lag_rows), lag_rows)
        return dot(inverse[at, :], stacked[:, WIDE * chunk : WIDE * chunk + WIDE])

    for chunk in range(CHUNKS):
        cross_spectra(chunk)
        for part in range(2):
            for octet in range(2):
                for h in range(2):
                    parts = [
                        cross[chunk, h, pl.ds((part * 16 + octet * 8 + i) * 32, 32), :].astype(BF16)
                        for i in range(8)
                    ]
                    parts = block_transpose(parts)
                    lane = WIDE * chunk + 128 * octet
                    for j in range(8):
                        at = (part * 16 + h * 8 + j) * 32
                        stacked[at : at + 32, lane : lane + 128] = parts[j]
        lags_out[chunk, 1] = lag_block(lax.rem(me_z + 2, NZ), chunk).astype(BF16)
        z_copy(chunk, 0, 0).start()
        z_copy(chunk, 0, 1).start()
        block = lag_block(ahead, chunk)
        lags_out[chunk, 0] = block.astype(BF16)
        kept[chunk, 0] = block[: lag_rows // 2]
        z_copy(chunk, 1, 0).start()
        block = lag_block(behind, chunk)
        lags_out[chunk, 2] = block.astype(BF16)
        kept[chunk, 1] = block[lag_rows // 2 :]
        z_copy(chunk, 1, 1).start()
        block = lag_block(me_z, chunk)
        kept[chunk, 2] = block[: lag_rows // 2]
        kept[chunk, 3] = block[lag_rows // 2 :]

    for chunk in range(CHUNKS):
        for way in range(2):
            z_copy(chunk, 0, way).wait_recv()
            total = kept[chunk, way] + lags_in[chunk, 0, way].astype(F32)
            mixed[chunk, way] = total.astype(BF16)
            z_copy(chunk, 2, way).start()

    own = lag_rows // NX

    def last_copy(chunk, to, slot):
        at = pl.ds(pl.multiple_of(to * own, own), own)
        return pltpu.make_async_remote_copy(
            src_ref=finished.at[chunk, at],
            dst_ref=last.at[chunk, slot],
            send_sem=last_send.at[chunk, to],
            recv_sem=last_recv.at[chunk, slot],
            device_id=at_x(to),
            device_id_type=MESH,
        )

    for chunk in range(CHUNKS):
        for kind in (1, 2):
            for way in range(2):
                z_copy(chunk, kind, way).wait_recv()
        for half in range(2):
            total = (
                kept[chunk, 2 + half]
                + lags_in[chunk, 2, half].astype(F32)
                + lags_in[chunk, 1, 1 - half].astype(F32)
            )
            finished[chunk, pl.ds(half * lag_rows // 2, lag_rows // 2)] = total.astype(BF16)
        for step in (2, 1, 3):
            last_copy(chunk, lax.rem(me_x + step, NX), me_x).start()
        last[chunk, me_x] = finished[chunk, pl.ds(pl.multiple_of(me_x * own, own), own), :]

    for chunk in range(CHUNKS):
        for step in (1, 3, 2):
            last_copy(chunk, me_x, lax.rem(me_x + step, NX)).wait_recv()
    for octet in range(2):
        parts = [
            last[chunk, x, :, 128 * octet : 128 * octet + 128]
            for x in range(NX)
            for chunk in range(CHUNKS)
        ]
        parts = block_transpose(parts)
        for j in range(8):
            s = octet * 8 + j
            out[:, 128 * s : 128 * s + 128] = parts[j]

    for step in (1, 2, 3):
        near_copy(lax.rem(me_near + step, near), me_near).wait_send()

    @pl.loop(1, ny)
    def _(step):
        y_copy(lax.rem(me_y + step, ny), me_y).wait_send()

    for step in around:
        side_copy(step).wait_send()

    for step in (1, 2, 3):
        to = lax.rem(me_x + step, NX)
        white_copy(to, me_x).wait_send()
        for chunk in range(CHUNKS):
            last_copy(chunk, to, me_x).wait_send()
    for chunk in range(CHUNKS):
        for kind in range(3):
            for way in range(2):
                z_copy(chunk, kind, way).wait_send()


def local(ny, record, offsets, sources):
    lag_rows = HALF // NZ
    own = lag_rows // NX
    upper, lower = forward_tables()
    inverse = inverse_table(NZ * NX * WIN)
    tables = np.concatenate([upper, lower, inverse], axis=0)
    vmem = pl.BlockSpec(memory_space=pltpu.VMEM)
    hbm = pl.BlockSpec(memory_space=pltpu.HBM)
    dma = pltpu.SemaphoreType.DMA
    flat = pl.pallas_call(
        functools.partial(kernel, ny),
        out_shape=jax.ShapeDtypeStruct((own, NSRC * ROWS), BF16),
        in_specs=[hbm, hbm, vmem, hbm],
        out_specs=vmem,
        scratch_shapes=[
            pltpu.SMEM((WIN,), jnp.int32),
            pltpu.SMEM((NSRC,), jnp.int32),
            pltpu.VMEM((SAMPLES, SAMPLES), BF16),
            pltpu.VMEM((SAMPLES, SAMPLES), BF16),
            pltpu.VMEM((HALF, SAMPLES), BF16),
            pltpu.VMEM((256, SAMPLES), BF16),
            pltpu.VMEM((2 * NLOW, 16, HALF), BF16),
            pltpu.VMEM((2 * NLOW, 16, HALF), BF16),
            pltpu.VMEM((ny, 16, HALF), BF16),
            pltpu.VMEM((2, NLOW * NX, 16, HALF), BF16),
            pltpu.VMEM((SAMPLES, 256), F32),
            pltpu.VMEM((NX, HALF, 128), BF16),
            pltpu.VMEM((NX, HALF, 128), BF16),
            pltpu.VMEM((8, 2, 2, 64, 128), BF16),
            pltpu.VMEM((HALF, 1024), BF16),
            pltpu.VMEM((CHUNKS, GROUPS, 256, 256), BF16),
            pltpu.VMEM((CHUNKS, 2, SAMPLES, 128), F32),
            pltpu.VMEM((SAMPLES, 512), BF16),
            pltpu.VMEM((CHUNKS, 3, lag_rows, WIDE), BF16),
            pltpu.VMEM((CHUNKS, 2, lag_rows // 2, WIDE), BF16),
            pltpu.VMEM((CHUNKS, 4, lag_rows // 2, WIDE), F32),
            pltpu.VMEM((CHUNKS, 3, 2, lag_rows // 2, WIDE), BF16),
            pltpu.VMEM((CHUNKS, lag_rows, WIDE), BF16),
            pltpu.VMEM((CHUNKS, NX, own, WIDE), BF16),
            dma((5,)),
            dma((2 * NLOW,)),
            dma((2 * NLOW,)),
            dma((ny,)),
            dma((ny,)),
            dma((2, NLOW * NX)),
            dma((2, NLOW * NX)),
            dma((NX,)),
            dma((NX,)),
            dma((CHUNKS, 3, 2)),
            dma((CHUNKS, 3, 2)),
            dma((CHUNKS, NX)),
            dma((CHUNKS, NX)),
        ],
        compiler_params=pltpu.CompilerParams(
            collective_id=0, has_side_effects=True, vmem_limit_bytes=53 * 1024 * 1024
        ),
        cost_estimate=pl.CostEstimate(
            flops=3 * 10**9, bytes_accessed=7 * 10**6, transcendentals=10**6
        ),
    )(
        offsets,
        sources,
        jnp.transpose(record, (1, 0, 2)),
        jnp.asarray(tables),
    )
    return flat.reshape(own, NSRC, ROWS)


def solution(mesh):
    ny = mesh.shape["chan"] // (2 * NLOW)
    in_specs = (P("chan", "spec", None), P("spec"), P())
    out_specs = P("spec", None, "chan")
    return jax.shard_map(
        functools.partial(local, ny),
        mesh=mesh,
        in_specs=in_specs,
        out_specs=out_specs,
        check_vma=False,
    )
```

```python
import functools
import math

import jax
import jax.numpy as jnp
import numpy as np
from jax import lax
from jax.experimental import pallas as pl
from jax.experimental.pallas import tpu as pltpu
from jax.sharding import PartitionSpec as P

SAMPLES = 1024
HALF = SAMPLES // 2
PAD = 128
NSRC = 16
WATER = 0.1
NX = 4
ROWS = 128
WIN = 2
BLK = ROWS // NX
GROUPS = 32
SKIP = 40
NLOW = 2
NZ = 4
CHUNKS = 2
PART = BLK // CHUNKS
WIDE = NSRC * PART
BINS = np.concatenate([np.arange(0, HALF, 2), np.arange(1, HALF, 2)])
F32 = jnp.float32
BF16 = jnp.bfloat16
MESH = pl.DeviceIdType.MESH


def forward_tables():
    rows = np.arange(SAMPLES)[:, None]
    cols = np.arange(SAMPLES)[None, :]
    freq = BINS[rows % HALF]
    angle = 2.0 * np.pi / SAMPLES * (freq * cols % SAMPLES)
    alternating = 1.0 - 2.0 * (cols % 2)
    imag = np.where(freq == 0, alternating, -np.sin(angle))
    table = np.where(rows < HALF, np.cos(angle), imag)
    upper = table.astype(jnp.bfloat16)
    lower = (table - upper.astype(np.float64)).astype(jnp.bfloat16)
    return upper, lower


def inverse_table(windows):
    shifted = np.arange(HALF)[:, None] - HALF // 2
    freq = BINS[(np.arange(16)[:, None] + 16 * np.arange(GROUPS)[None, :]).reshape(1, -1)]
    angle = 2.0 * np.pi / SAMPLES * (freq * shifted % SAMPLES)
    alternating = 1.0 - 2.0 * (shifted % 2)
    first = freq == 0
    real = np.where(first, 1.0, 2.0 * np.cos(angle))
    imag = np.where(first, alternating, -2.0 * np.sin(angle))
    table = np.concatenate([real, imag], axis=1) / math.sqrt(windows * SAMPLES)
    return table.astype(jnp.bfloat16)


def dot_t(left, right):
    return lax.dot_general(left, right, (((1,), (1,)), ((), ())), preferred_element_type=F32)


def dot(left, right):
    return lax.dot_general(left, right, (((1,), (0,)), ((), ())), preferred_element_type=F32)


def block_transpose(parts):
    count = len(parts)
    width = 128 // count
    lane = lax.broadcasted_iota(jnp.int32, parts[0].shape, 1)
    masks = [lane // width == i for i in range(count - 1)]

    def pick(choices):
        result = choices[-1]
        for mask, choice in zip(masks, choices):
            result = jnp.where(mask, choice, result)
        return result

    turned = []
    for d in range(count):
        part = pick([parts[(i - d) % count] for i in range(count)])
        turned.append(pltpu.roll(part, 128 - width * d, 1) if d else part)
    return [pick([turned[(j - i) % count] for i in range(count)]) for j in range(count)]


def kernel(
    ny,
    offsets_hbm,
    sources_hbm,
    record,
    tables_hbm,
    out,
    offsets,
    sources,
    upper,
    lower,
    upper_t,
    lower_t,
    inverse,
    traces,
    pieces,
    reduced,
    parts_y,
    picked,
    spectrum,
    outgoing,
    incoming,
    left,
    copies,
    right,
    cross,
    stacked,
    lags_out,
    mixed,
    kept,
    lags_in,
    finished,
    last,
    load_sem,
    near_send,
    near_recv,
    y_send,
    y_recv,
    side_send,
    side_recv,
    white_send,
    white_recv,
    z_send,
    z_recv,
    last_send,
    last_recv,
):
    plane = 2 * ny
    near = NLOW * 2
    chan = lax.axis_index("chan")
    spec = lax.axis_index("spec")
    me_x = lax.rem(spec, NX)
    me_z = spec // NX
    me_low = chan // plane
    me_plane = lax.rem(chan, plane)
    me_y = me_plane // 2
    me_core = lax.rem(chan, 2)
    me_side = me_low * NX + me_x
    me_near = me_low * 2 + me_core

    def at_near(other):
        return (other // 2 * plane + me_y * 2 + lax.rem(other, 2), spec)

    def at_y(other):
        return (me_low * plane + other * 2 + me_core, spec)

    around = sorted(
        (
            (low, x, core)
            for low in range(NLOW)
            for x in range(NX)
            for core in range(2)
            if low + x + core
        ),
        key=lambda step: -(step[0] + 2 * min(step[1], NX - step[1])),
    )

    def moved(step):
        low = lax.rem(me_low + step[0], NLOW)
        x = lax.rem(me_x + step[1], NX)
        core = lax.rem(me_core + step[2], 2)
        device = (low * plane + me_y * 2 + core, me_z * NX + x)
        return device, core, low * NX + x

    def at_x(other):
        return (chan, me_z * NX + other)

    def at_z(other):
        return (chan, other * NX + me_x)

    loads = [
        pltpu.make_async_copy(source, target, load_sem.at[i])
        for i, (source, target) in enumerate(
            [
                (offsets_hbm, offsets),
                (sources_hbm, sources),
                (tables_hbm.at[pl.ds(0, SAMPLES)], upper),
                (tables_hbm.at[pl.ds(SAMPLES, SAMPLES)], lower),
                (tables_hbm.at[pl.ds(2 * SAMPLES, HALF)], upper_t),
                (tables_hbm.at[pl.ds(2 * SAMPLES + HALF, HALF)], lower_t),
                (tables_hbm.at[pl.ds(3 * SAMPLES, HALF)], inverse),
            ]
        )
    ]
    for load in loads:
        load.start()

    barrier = pltpu.get_barrier_semaphore()

    def greet(device):
        pl.semaphore_signal(barrier, inc=1, device_id=device, device_id_type=MESH)

    @pl.loop(1, ny)
    def _(step):
        greet(at_y(lax.rem(me_y + step, ny)))

    for step in around:
        greet(moved(step)[0])

    for step in (1, NZ - 1):
        greet(at_z(lax.rem(me_z + step, NZ)))

    loads[0].wait()
    loads[1].wait()

    lane = lax.broadcasted_iota(jnp.int32, (ROWS, 128), 1)
    for w in range(WIN):
        rows = record[w].astype(F32)
        head = jnp.where(lane < offsets[w], rows[:, SAMPLES:], rows[:, :PAD])
        rows = jnp.concatenate([head, rows[:, PAD:SAMPLES]], axis=1)
        rows = rows - jnp.mean(rows, axis=1, keepdims=True)
        rows = rows * lax.rsqrt(jnp.mean(rows * rows, axis=1, keepdims=True) + 1e-06)
        rows = rows.astype(BF16)
        for x in range(NX):
            traces[pl.ds(x * 64 + w * BLK, BLK), :] = rows[x * BLK : (x + 1) * BLK]

    row = lax.broadcasted_iota(jnp.int32, (32, 256), 0)
    col = lax.broadcasted_iota(jnp.int32, (32, 256), 1)
    wanted = jnp.zeros((32, 256), jnp.int32)
    for s in range(NSRC):
        wanted = jnp.where(row % NSRC == s, sources[s], wanted)
    channel = chan * ROWS + (col // 64) * BLK + col % BLK
    same = jnp.logical_and(wanted == channel, row // NSRC == (col // BLK) % 2)
    chosen = dot(jnp.where(same, 1.0, 0.0).astype(BF16), traces[...])
    for w in range(WIN):
        for low in range(NLOW):
            rows = chosen[16 * w + 8 * low : 16 * w + 8 * low + 8]
            rows = jnp.concatenate([rows[:, :HALF], rows[:, HALF:]], axis=0)
            pieces[low * 2 + w] = rows.astype(BF16)

    pl.semaphore_wait(barrier, ny - 1 + len(around) + 2)

    def near_copy(to, slot):
        return pltpu.make_async_remote_copy(
            src_ref=pieces.at[to],
            dst_ref=reduced.at[slot],
            send_sem=near_send.at[to],
            recv_sem=near_recv.at[slot],
            device_id=at_near(to),
            device_id_type=MESH,
        )

    for step in (2, 3, 1):
        near_copy(lax.rem(me_near + step, near), me_near).start()
    reduced[me_near] = pieces[me_near]
    loads[2].wait()
    spectrum[...] = dot_t(upper[...], traces[...])

    for step in (1, 2, 3):
        near_copy(me_near, lax.rem(me_near + step, near)).wait_recv()
    total = reduced[0].astype(F32)
    for i in range(1, near):
        total = total + reduced[i].astype(F32)
    parts_y[me_y] = total.astype(BF16)

    def y_copy(to, slot):
        return pltpu.make_async_remote_copy(
            src_ref=parts_y.at[me_y],
            dst_ref=parts_y.at[slot],
            send_sem=y_send.at[to],
            recv_sem=y_recv.at[slot],
            device_id=at_y(to),
            device_id_type=MESH,
        )

    for step in sorted(range(1, ny), key=lambda step: -min(step, ny - step)):
        y_copy(lax.rem(me_y + step, ny), me_y).start()

    loads[3].wait()
    spectrum[...] += dot_t(lower[...], traces[...])

    chunk = 64
    first_row = lax.broadcasted_iota(jnp.int32, (chunk, 256), 0) == 0
    total = jnp.zeros((1, 256), F32)
    for k in range(0, HALF, chunk):
        re = spectrum[k : k + chunk]
        im = spectrum[HALF + k : HALF + k + chunk]
        size = jnp.sqrt(re * re + im * im)
        if k == 0:
            size = jnp.where(first_row, jnp.abs(re) + jnp.abs(im), size)
        total = total + jnp.sum(size, axis=0, keepdims=True)
    level = WATER * (total / (HALF + 1) + 1e-06)
    low = lax.broadcasted_iota(jnp.int32, (chunk, 128), 1) < 64
    for k in range(0, HALF, chunk):
        re = spectrum[k : k + chunk]
        im = spectrum[HALF + k : HALF + k + chunk]
        size = jnp.sqrt(re * re + im * im)
        if k == 0:
            re = re / (jnp.where(first_row, jnp.abs(re), size) + level)
            im = im / (jnp.where(first_row, jnp.abs(im), size) + level)
        else:
            scale = 1.0 / (size + level)
            re = re * scale
            im = im * scale
        for pair in range(2):
            a = re[:, 128 * pair : 128 * pair + 128]
            b = im[:, 128 * pair : 128 * pair + 128]
            even = jnp.where(low, a, pltpu.roll(b, 64, 1))
            odd = jnp.where(low, pltpu.roll(a, 64, 1), b)
            outgoing[2 * pair, k : k + chunk] = even.astype(BF16)
            outgoing[2 * pair + 1, k : k + chunk] = odd.astype(BF16)

    def white_copy(to, slot):
        return pltpu.make_async_remote_copy(
            src_ref=outgoing.at[to],
            dst_ref=incoming.at[slot],
            send_sem=white_send.at[to],
            recv_sem=white_recv.at[slot],
            device_id=at_x(to),
            device_id_type=MESH,
        )

    for step in (2, 1, 3):
        white_copy(lax.rem(me_x + step, NX), me_x).start()
    incoming[me_x] = outgoing[me_x]

    r = lax.broadcasted_iota(jnp.int32, (128, 1024), 0)
    c = lax.broadcasted_iota(jnp.int32, (128, 1024), 1)
    match = jnp.logical_and(r // BLK == c // 256, r % BLK // PART == c // 128 % 2)
    match = jnp.logical_and(match, r % PART == c % PART)
    spread = jnp.where(match, 1.0, 0.0).astype(BF16)
    r = lax.broadcasted_iota(jnp.int32, (16, 256), 0)
    c = lax.broadcasted_iota(jnp.int32, (16, 256), 1)
    mask = jnp.where(r == c // PART, 1.0, 0.0).astype(BF16)

    def widen(x):
        copies[...] = dot(incoming[x], spread).astype(BF16)

        @pl.loop(0, 8)
        def _(small):
            for big in range(4):
                group = big * 8 + small
                at = pl.ds(pl.multiple_of(group * 16, 16), 16)
                for p in range(2):
                    for w in range(WIN):
                        slab = pl.multiple_of((p * 8 + x * 2 + w) * 16, 16)
                        for chunk in range(CHUNKS):
                            lane = (p * 2 + w) * 256 + chunk * 128
                            tile = copies[at, lane : lane + 128]
                            right[chunk, group, pl.ds(slab, 16), :] = (
                                jnp.concatenate([tile] * 2, axis=1) * mask
                            )

    widen(me_x)

    @pl.loop(1, ny)
    def _(step):
        y_copy(me_y, lax.rem(me_y + step, ny)).wait_recv()

    loads[4].wait()
    loads[5].wait()
    total = parts_y[0].astype(F32)
    for i in range(1, ny):
        total = total + parts_y[i].astype(F32)
    folded = []
    for rows in (total[:8] + total[8:], total[:8] - total[8:]):
        high = rows.astype(BF16)
        rest = (rows - high.astype(F32)).astype(BF16)
        folded.append(jnp.concatenate([high, rest], axis=0))

    def quarter(i):
        at = pl.ds(i * HALF // 2, HALF // 2)
        both = dot(folded[i % 2], upper_t[:, at]) + dot(folded[i % 2], lower_t[:, at])
        return both[:8] + both[8:]

    re = jnp.concatenate([quarter(0), quarter(1)], axis=1)
    im = jnp.concatenate([quarter(2), quarter(3)], axis=1)
    size = jnp.sqrt(re * re + im * im)
    first = lax.broadcasted_iota(jnp.int32, (8, HALF), 1) == 0
    total = jnp.sum(
        jnp.where(first, jnp.abs(re) + jnp.abs(im), size), axis=1, keepdims=True
    )
    level = WATER * (total / (HALF + 1) + 1e-06)
    re = re / (jnp.where(first, jnp.abs(re), size) + level)
    im = im / (jnp.where(first, jnp.abs(im), size) + level)
    picked[me_core, me_side] = jnp.concatenate([re, im], axis=0).astype(BF16)

    def side_copy(step, back=False):
        device, core, slot = moved(step)
        at = (core, slot) if back else (me_core, me_side)
        return pltpu.make_async_remote_copy(
            src_ref=picked.at[me_core, me_side],
            dst_ref=picked.at[at],
            send_sem=side_send.at[core, slot],
            recv_sem=side_recv.at[at],
            device_id=device,
            device_id_type=MESH,
        )

    for step in around:
        side_copy(step).start()

    def widen_next(step):
        x = lax.rem(me_x + step, NX)
        white_copy(me_x, x).wait_recv()
        widen(x)

    widen_next(1)
    widen_next(3)

    widen_next(2)

    for step in around[::-1]:
        side_copy(step, True).wait_recv()

    parts = []
    for x in range(NX):
        for w in range(WIN):
            tiles = []
            halves = [picked[w, low * NX + x].astype(F32) for low in range(NLOW)]
            for part in range(2):
                for big in range(4):
                    for half in halves:
                        tiles.append(
                            half[8 * part : 8 * part + 8, 128 * big : 128 * big + 128]
                        )
            parts.append(jnp.concatenate(tiles, axis=0))
    parts = block_transpose(parts)
    for small in range(8):
        a_re = parts[small][:64].astype(BF16)
        a_im = parts[small][64:].astype(BF16)
        re_b0, re_b1, im_b0, im_b1 = a_re, a_im, -a_im, a_re
        if small == 0:
            shape = (64, 128)
            zero_bin = jnp.logical_and(
                lax.broadcasted_iota(jnp.int32, shape, 0) < 16,
                lax.broadcasted_iota(jnp.int32, shape, 1) % 16 == 0,
            )
            zero = jnp.zeros(shape, BF16)
            re_b1 = jnp.where(zero_bin, zero, re_b1)
            im_b0 = jnp.where(zero_bin, zero, im_b0)
            im_b1 = jnp.where(zero_bin, a_im, im_b1)
        left[small, 0, 0] = re_b0
        left[small, 0, 1] = re_b1
        left[small, 1, 0] = im_b0
        left[small, 1, 1] = im_b1

    def cross_spectra(chunk):
        @pl.loop(0, 8)
        def _(small):
            for big in range(4):
                group = big * 8 + small
                rows_left = jnp.concatenate(
                    [
                        jnp.concatenate(
                            [left[small, part, p, big * 16 : big * 16 + 16, :] for p in range(2)],
                            axis=1,
                        )
                        for part in range(2)
                    ],
                    axis=0,
                )
                result = dot(rows_left, right[chunk, group])
                for h in range(2):
                    cross[chunk, h, pl.ds(group, 32, stride=SKIP), :] = result[
                        :, 128 * h : 128 * h + 128
                    ]

    loads[6].wait()

    ahead = lax.rem(me_z + 1, NZ)
    behind = lax.rem(me_z + NZ - 1, NZ)
    lag_rows = HALF // NZ
    top = pl.ds(0, lag_rows // 2)
    bottom = pl.ds(lag_rows // 2, lag_rows // 2)

    def z_copy(chunk, kind, way, to=None):
        source = [
            (lags_out.at[chunk, 1, top], lags_out.at[chunk, 1, bottom]),
            (lags_out.at[chunk, 0, bottom], lags_out.at[chunk, 2, top]),
            (mixed.at[chunk, 0], mixed.at[chunk, 1]),
        ][kind][way]
        return pltpu.make_async_remote_copy(
            src_ref=source,
            dst_ref=lags_in.at[chunk, kind, way],
            send_sem=z_send.at[chunk, kind, way],
            recv_sem=z_recv.at[chunk, kind, way],
            device_id=at_z((ahead, behind)[way]),
            device_id_type=MESH,
        )

    def lag_block(to, chunk):
        at = pl.ds(pl.multiple_of(to * lag_rows, lag_rows), lag_rows)
        return dot(inverse[at, :], stacked[:, WIDE * chunk : WIDE * chunk + WIDE])

    for chunk in range(CHUNKS):
        cross_spectra(chunk)
        for part in range(2):
            for octet in range(2):
                for h in range(2):
                    parts = [
                        cross[chunk, h, pl.ds((part * 16 + octet * 8 + i) * SKIP, 32), :].astype(BF16)
                        for i in range(8)
                    ]
                    parts = block_transpose(parts)
                    lane = WIDE * chunk + 128 * octet
                    for j in range(8):
                        at = (part * 16 + h * 8 + j) * 32
                        stacked[at : at + 32, lane : lane + 128] = parts[j]
        lags_out[chunk, 1] = lag_block(lax.rem(me_z + 2, NZ), chunk).astype(BF16)
        z_copy(chunk, 0, 0).start()
        z_copy(chunk, 0, 1).start()
        block = lag_block(ahead, chunk)
        lags_out[chunk, 0] = block.astype(BF16)
        kept[chunk, 0] = block[: lag_rows // 2]
        z_copy(chunk, 1, 0).start()
        block = lag_block(behind, chunk)
        lags_out[chunk, 2] = block.astype(BF16)
        kept[chunk, 1] = block[lag_rows // 2 :]
        z_copy(chunk, 1, 1).start()
        block = lag_block(me_z, chunk)
        kept[chunk, 2] = block[: lag_rows // 2]
        kept[chunk, 3] = block[lag_rows // 2 :]

    for chunk in range(CHUNKS):
        for way in range(2):
            z_copy(chunk, 0, way).wait_recv()
            total = kept[chunk, way] + lags_in[chunk, 0, way].astype(F32)
            mixed[chunk, way] = total.astype(BF16)
            z_copy(chunk, 2, way).start()

    own = lag_rows // NX

    def last_copy(chunk, to, slot):
        at = pl.ds(pl.multiple_of(to * own, own), own)
        return pltpu.make_async_remote_copy(
            src_ref=finished.at[chunk, at],
            dst_ref=last.at[chunk, slot],
            send_sem=last_send.at[chunk, to],
            recv_sem=last_recv.at[chunk, slot],
            device_id=at_x(to),
            device_id_type=MESH,
        )

    for chunk in range(CHUNKS):
        for kind in (1, 2):
            for way in range(2):
                z_copy(chunk, kind, way).wait_recv()
        for half in range(2):
            total = (
                kept[chunk, 2 + half]
                + lags_in[chunk, 2, half].astype(F32)
                + lags_in[chunk, 1, 1 - half].astype(F32)
            )
            finished[chunk, pl.ds(half * lag_rows // 2, lag_rows // 2)] = total.astype(BF16)
        for step in (2, 1, 3):
            last_copy(chunk, lax.rem(me_x + step, NX), me_x).start()
        last[chunk, me_x] = finished[chunk, pl.ds(pl.multiple_of(me_x * own, own), own), :]

    for chunk in range(CHUNKS):
        for step in (1, 3, 2):
            last_copy(chunk, me_x, lax.rem(me_x + step, NX)).wait_recv()
    for octet in range(2):
        parts = [
            last[chunk, x, :, 128 * octet : 128 * octet + 128]
            for x in range(NX)
            for chunk in range(CHUNKS)
        ]
        parts = block_transpose(parts)
        for j in range(8):
            s = octet * 8 + j
            out[:, 128 * s : 128 * s + 128] = parts[j]

    for step in (1, 2, 3):
        near_copy(lax.rem(me_near + step, near), me_near).wait_send()

    @pl.loop(1, ny)
    def _(step):
        y_copy(lax.rem(me_y + step, ny), me_y).wait_send()

    for step in around:
        side_copy(step).wait_send()

    for step in (1, 2, 3):
        to = lax.rem(me_x + step, NX)
        white_copy(to, me_x).wait_send()
        for chunk in range(CHUNKS):
            last_copy(chunk, to, me_x).wait_send()
    for chunk in range(CHUNKS):
        for kind in range(3):
            for way in range(2):
                z_copy(chunk, kind, way).wait_send()


def local(ny, record, offsets, sources):
    lag_rows = HALF // NZ
    own = lag_rows // NX
    upper, lower = forward_tables()
    inverse = inverse_table(NZ * NX * WIN)
    tables = np.concatenate([upper, lower, upper.T[:HALF], lower.T[:HALF], inverse], axis=0)
    vmem = pl.BlockSpec(memory_space=pltpu.VMEM)
    hbm = pl.BlockSpec(memory_space=pltpu.HBM)
    dma = pltpu.SemaphoreType.DMA
    flat = pl.pallas_call(
        functools.partial(kernel, ny),
        out_shape=jax.ShapeDtypeStruct((own, NSRC * ROWS), BF16),
        in_specs=[hbm, hbm, vmem, hbm],
        out_specs=vmem,
        scratch_shapes=[
            pltpu.SMEM((WIN,), jnp.int32),
            pltpu.SMEM((NSRC,), jnp.int32),
            pltpu.VMEM((SAMPLES, SAMPLES), BF16),
            pltpu.VMEM((SAMPLES, SAMPLES), BF16),
            pltpu.VMEM((HALF, SAMPLES), BF16),
            pltpu.VMEM((HALF, SAMPLES), BF16),
            pltpu.VMEM((HALF, SAMPLES), BF16),
            pltpu.VMEM((256, SAMPLES), BF16),
            pltpu.VMEM((2 * NLOW, 16, HALF), BF16),
            pltpu.VMEM((2 * NLOW, 16, HALF), BF16),
            pltpu.VMEM((ny, 16, HALF), BF16),
            pltpu.VMEM((2, NLOW * NX, 16, HALF), BF16),
            pltpu.VMEM((SAMPLES, 256), F32),
            pltpu.VMEM((NX, HALF, 128), BF16),
            pltpu.VMEM((NX, HALF, 128), BF16),
            pltpu.VMEM((8, 2, 2, 64, 128), BF16),
            pltpu.VMEM((HALF, 1024), BF16),
            pltpu.VMEM((CHUNKS, GROUPS, 256, 256), BF16),
            pltpu.VMEM((CHUNKS, 2, 32 * SKIP, 128), F32),
            pltpu.VMEM((SAMPLES, 512), BF16),
            pltpu.VMEM((CHUNKS, 3, lag_rows, WIDE), BF16),
            pltpu.VMEM((CHUNKS, 2, lag_rows // 2, WIDE), BF16),
            pltpu.VMEM((CHUNKS, 4, lag_rows // 2, WIDE), F32),
            pltpu.VMEM((CHUNKS, 3, 2, lag_rows // 2, WIDE), BF16),
            pltpu.VMEM((CHUNKS, lag_rows, WIDE), BF16),
            pltpu.VMEM((CHUNKS, NX, own, WIDE), BF16),
            dma((7,)),
            dma((2 * NLOW,)),
            dma((2 * NLOW,)),
            dma((ny,)),
            dma((ny,)),
            dma((2, NLOW * NX)),
            dma((2, NLOW * NX)),
            dma((NX,)),
            dma((NX,)),
            dma((CHUNKS, 3, 2)),
            dma((CHUNKS, 3, 2)),
            dma((CHUNKS, NX)),
            dma((CHUNKS, NX)),
        ],
        compiler_params=pltpu.CompilerParams(
            collective_id=0, has_side_effects=True, vmem_limit_bytes=53 * 1024 * 1024
        ),
        cost_estimate=pl.CostEstimate(
            flops=3 * 10**9, bytes_accessed=7 * 10**6, transcendentals=10**6
        ),
    )(
        offsets,
        sources,
        jnp.transpose(record, (1, 0, 2)),
        jnp.asarray(tables),
    )
    return flat.reshape(own, NSRC, ROWS)


def solution(mesh):
    ny = mesh.shape["chan"] // (2 * NLOW)
    in_specs = (P("chan", "spec", None), P("spec"), P())
    out_specs = P("spec", None, "chan")
    return jax.shard_map(
        functools.partial(local, ny),
        mesh=mesh,
        in_specs=in_specs,
        out_specs=out_specs,
        check_vma=False,
    )
```

```python
import functools
import math

import jax
import jax.numpy as jnp
import numpy as np
from jax import lax
from jax.experimental import pallas as pl
from jax.experimental.pallas import tpu as pltpu
from jax.sharding import PartitionSpec as P

SAMPLES = 1024
HALF = SAMPLES // 2
PAD = 128
NSRC = 16
WATER = 0.1
NX = 4
ROWS = 128
WIN = 2
BLK = ROWS // NX
GROUPS = 32
SKIP = 40
NLOW = 2
NZ = 4
CHUNKS = 2
PART = BLK // CHUNKS
WIDE = NSRC * PART
BINS = np.concatenate([np.arange(0, HALF, 2), np.arange(1, HALF, 2)])
F32 = jnp.float32
BF16 = jnp.bfloat16
MESH = pl.DeviceIdType.MESH


def forward_tables():
    rows = np.arange(SAMPLES)[:, None]
    cols = np.arange(SAMPLES)[None, :]
    freq = BINS[rows % HALF]
    angle = 2.0 * np.pi / SAMPLES * (freq * cols % SAMPLES)
    alternating = 1.0 - 2.0 * (cols % 2)
    imag = np.where(freq == 0, alternating, -np.sin(angle))
    table = np.where(rows < HALF, np.cos(angle), imag)
    upper = table.astype(jnp.bfloat16)
    lower = (table - upper.astype(np.float64)).astype(jnp.bfloat16)
    return upper, lower


def inverse_table(windows):
    shifted = np.arange(HALF)[:, None] - HALF // 2
    freq = BINS[(np.arange(16)[:, None] + 16 * np.arange(GROUPS)[None, :]).reshape(1, -1)]
    angle = 2.0 * np.pi / SAMPLES * (freq * shifted % SAMPLES)
    alternating = 1.0 - 2.0 * (shifted % 2)
    first = freq == 0
    real = np.where(first, 1.0, 2.0 * np.cos(angle))
    imag = np.where(first, alternating, -2.0 * np.sin(angle))
    table = np.concatenate([real, imag], axis=1) / math.sqrt(windows * SAMPLES)
    return table.astype(jnp.bfloat16)


def dot_t(left, right):
    return lax.dot_general(left, right, (((1,), (1,)), ((), ())), preferred_element_type=F32)


def dot(left, right):
    return lax.dot_general(left, right, (((1,), (0,)), ((), ())), preferred_element_type=F32)


def block_transpose(parts):
    count = len(parts)
    width = 128 // count
    lane = lax.broadcasted_iota(jnp.int32, parts[0].shape, 1)
    masks = [lane // width == i for i in range(count - 1)]

    def pick(choices):
        result = choices[-1]
        for mask, choice in zip(masks, choices):
            result = jnp.where(mask, choice, result)
        return result

    turned = []
    for d in range(count):
        part = pick([parts[(i - d) % count] for i in range(count)])
        turned.append(pltpu.roll(part, 128 - width * d, 1) if d else part)
    return [pick([turned[(j - i) % count] for i in range(count)]) for j in range(count)]


def kernel(
    ny,
    offsets_hbm,
    sources_hbm,
    record,
    tables_hbm,
    out,
    offsets,
    sources,
    upper,
    lower,
    upper_t,
    lower_t,
    inverse,
    traces,
    pieces,
    reduced,
    parts_y,
    picked,
    spectrum,
    outgoing,
    incoming,
    left,
    copies,
    right,
    cross,
    stacked,
    lags_out,
    mixed,
    kept,
    lags_in,
    finished,
    last,
    load_sem,
    near_send,
    near_recv,
    y_send,
    y_recv,
    side_send,
    side_recv,
    white_send,
    white_recv,
    z_send,
    z_recv,
    last_send,
    last_recv,
):
    plane = 2 * ny
    near = NLOW * 2
    chan = lax.axis_index("chan")
    spec = lax.axis_index("spec")
    me_x = lax.rem(spec, NX)
    me_z = spec // NX
    me_low = chan // plane
    me_plane = lax.rem(chan, plane)
    me_y = me_plane // 2
    me_core = lax.rem(chan, 2)
    me_side = me_low * NX + me_x
    me_near = me_low * 2 + me_core

    def at_near(other):
        return (other // 2 * plane + me_y * 2 + lax.rem(other, 2), spec)

    def at_y(other):
        return (me_low * plane + other * 2 + me_core, spec)

    around = sorted(
        (
            (low, x, core)
            for low in range(NLOW)
            for x in range(NX)
            for core in range(2)
            if low + x + core
        ),
        key=lambda step: -(step[0] + 2 * min(step[1], NX - step[1])),
    )

    def moved(step):
        low = lax.rem(me_low + step[0], NLOW)
        x = lax.rem(me_x + step[1], NX)
        core = lax.rem(me_core + step[2], 2)
        device = (low * plane + me_y * 2 + core, me_z * NX + x)
        return device, core, low * NX + x

    def at_x(other):
        return (chan, me_z * NX + other)

    def at_z(other):
        return (chan, other * NX + me_x)

    loads = [
        pltpu.make_async_copy(source, target, load_sem.at[i])
        for i, (source, target) in enumerate(
            [
                (offsets_hbm, offsets),
                (sources_hbm, sources),
                (tables_hbm.at[pl.ds(0, SAMPLES)], upper),
                (tables_hbm.at[pl.ds(SAMPLES, SAMPLES)], lower),
                (tables_hbm.at[pl.ds(2 * SAMPLES, HALF)], upper_t),
                (tables_hbm.at[pl.ds(2 * SAMPLES + HALF, HALF)], lower_t),
                (tables_hbm.at[pl.ds(3 * SAMPLES, HALF)], inverse),
            ]
        )
    ]
    for load in loads:
        load.start()

    barrier = pltpu.get_barrier_semaphore()

    def greet(device):
        pl.semaphore_signal(barrier, inc=1, device_id=device, device_id_type=MESH)

    @pl.loop(1, ny)
    def _(step):
        greet(at_y(lax.rem(me_y + step, ny)))

    for step in around:
        greet(moved(step)[0])

    for step in (1, NZ - 1):
        greet(at_z(lax.rem(me_z + step, NZ)))

    loads[0].wait()
    loads[1].wait()

    lane = lax.broadcasted_iota(jnp.int32, (ROWS, 128), 1)
    for w in range(WIN):
        rows = record[w].astype(F32)
        head = jnp.where(lane < offsets[w], rows[:, SAMPLES:], rows[:, :PAD])
        rows = jnp.concatenate([head, rows[:, PAD:SAMPLES]], axis=1)
        rows = rows - jnp.mean(rows, axis=1, keepdims=True)
        rows = rows * lax.rsqrt(jnp.mean(rows * rows, axis=1, keepdims=True) + 1e-06)
        rows = rows.astype(BF16)
        for x in range(NX):
            traces[pl.ds(x * 64 + w * BLK, BLK), :] = rows[x * BLK : (x + 1) * BLK]

    row = lax.broadcasted_iota(jnp.int32, (32, 256), 0)
    col = lax.broadcasted_iota(jnp.int32, (32, 256), 1)
    wanted = jnp.zeros((32, 256), jnp.int32)
    for s in range(NSRC):
        wanted = jnp.where(row % NSRC == s, sources[s], wanted)
    channel = chan * ROWS + (col // 64) * BLK + col % BLK
    same = jnp.logical_and(wanted == channel, row // NSRC == (col // BLK) % 2)
    chosen = dot(jnp.where(same, 1.0, 0.0).astype(BF16), traces[...])
    for w in range(WIN):
        for low in range(NLOW):
            rows = chosen[16 * w + 8 * low : 16 * w + 8 * low + 8]
            rows = jnp.concatenate([rows[:, :HALF], rows[:, HALF:]], axis=0)
            pieces[low * 2 + w] = rows.astype(BF16)

    pl.semaphore_wait(barrier, ny - 1 + len(around) + 2)

    def near_copy(to, slot):
        return pltpu.make_async_remote_copy(
            src_ref=pieces.at[to],
            dst_ref=reduced.at[slot],
            send_sem=near_send.at[to],
            recv_sem=near_recv.at[slot],
            device_id=at_near(to),
            device_id_type=MESH,
        )

    for step in (2, 3, 1):
        near_copy(lax.rem(me_near + step, near), me_near).start()
    reduced[me_near] = pieces[me_near]
    loads[2].wait()
    spectrum[...] = dot_t(upper[...], traces[...])

    loads[3].wait()
    spectrum[...] += dot_t(lower[...], traces[...])

    chunk = 64
    first_row = lax.broadcasted_iota(jnp.int32, (chunk, 256), 0) == 0
    total = jnp.zeros((1, 256), F32)
    for k in range(0, HALF, chunk):
        re = spectrum[k : k + chunk]
        im = spectrum[HALF + k : HALF + k + chunk]
        size = jnp.sqrt(re * re + im * im)
        if k == 0:
            size = jnp.where(first_row, jnp.abs(re) + jnp.abs(im), size)
        total = total + jnp.sum(size, axis=0, keepdims=True)
    level = WATER * (total / (HALF + 1) + 1e-06)
    low = lax.broadcasted_iota(jnp.int32, (chunk, 128), 1) < 64
    for k in range(0, HALF, chunk):
        re = spectrum[k : k + chunk]
        im = spectrum[HALF + k : HALF + k + chunk]
        size = jnp.sqrt(re * re + im * im)
        if k == 0:
            re = re / (jnp.where(first_row, jnp.abs(re), size) + level)
            im = im / (jnp.where(first_row, jnp.abs(im), size) + level)
        else:
            scale = 1.0 / (size + level)
            re = re * scale
            im = im * scale
        for pair in range(2):
            a = re[:, 128 * pair : 128 * pair + 128]
            b = im[:, 128 * pair : 128 * pair + 128]
            even = jnp.where(low, a, pltpu.roll(b, 64, 1))
            odd = jnp.where(low, pltpu.roll(a, 64, 1), b)
            outgoing[2 * pair, k : k + chunk] = even.astype(BF16)
            outgoing[2 * pair + 1, k : k + chunk] = odd.astype(BF16)

    def white_copy(to, slot):
        return pltpu.make_async_remote_copy(
            src_ref=outgoing.at[to],
            dst_ref=incoming.at[slot],
            send_sem=white_send.at[to],
            recv_sem=white_recv.at[slot],
            device_id=at_x(to),
            device_id_type=MESH,
        )

    for step in (2, 1, 3):
        white_copy(lax.rem(me_x + step, NX), me_x).start()
    for step in (1, 2, 3):
        near_copy(me_near, lax.rem(me_near + step, near)).wait_recv()
    total = reduced[0].astype(F32)
    for i in range(1, near):
        total = total + reduced[i].astype(F32)
    parts_y[me_y] = total.astype(BF16)

    def y_copy(to, slot):
        return pltpu.make_async_remote_copy(
            src_ref=parts_y.at[me_y],
            dst_ref=parts_y.at[slot],
            send_sem=y_send.at[to],
            recv_sem=y_recv.at[slot],
            device_id=at_y(to),
            device_id_type=MESH,
        )

    for step in sorted(range(1, ny), key=lambda step: -min(step, ny - step)):
        y_copy(lax.rem(me_y + step, ny), me_y).start()

    incoming[me_x] = outgoing[me_x]

    r = lax.broadcasted_iota(jnp.int32, (128, 1024), 0)
    c = lax.broadcasted_iota(jnp.int32, (128, 1024), 1)
    match = jnp.logical_and(r // BLK == c // 256, r % BLK // PART == c // 128 % 2)
    match = jnp.logical_and(match, r % PART == c % PART)
    spread = jnp.where(match, 1.0, 0.0).astype(BF16)
    r = lax.broadcasted_iota(jnp.int32, (16, 256), 0)
    c = lax.broadcasted_iota(jnp.int32, (16, 256), 1)
    mask = jnp.where(r == c // PART, 1.0, 0.0).astype(BF16)

    def widen(x):
        copies[...] = dot(incoming[x], spread).astype(BF16)

        @pl.loop(0, 8)
        def _(small):
            for big in range(4):
                group = big * 8 + small
                at = pl.ds(pl.multiple_of(group * 16, 16), 16)
                for p in range(2):
                    for w in range(WIN):
                        slab = pl.multiple_of((p * 8 + x * 2 + w) * 16, 16)
                        for chunk in range(CHUNKS):
                            lane = (p * 2 + w) * 256 + chunk * 128
                            tile = copies[at, lane : lane + 128]
                            right[chunk, group, pl.ds(slab, 16), :] = (
                                jnp.concatenate([tile] * 2, axis=1) * mask
                            )

    widen(me_x)

    @pl.loop(1, ny)
    def _(step):
        y_copy(me_y, lax.rem(me_y + step, ny)).wait_recv()

    loads[4].wait()
    loads[5].wait()
    total = parts_y[0].astype(F32)
    for i in range(1, ny):
        total = total + parts_y[i].astype(F32)
    folded = []
    for rows in (total[:8] + total[8:], total[:8] - total[8:]):
        high = rows.astype(BF16)
        rest = (rows - high.astype(F32)).astype(BF16)
        folded.append(jnp.concatenate([high, rest], axis=0))

    def quarter(i):
        at = pl.ds(i * HALF // 2, HALF // 2)
        both = dot(folded[i % 2], upper_t[:, at]) + dot(folded[i % 2], lower_t[:, at])
        return both[:8] + both[8:]

    re = jnp.concatenate([quarter(0), quarter(1)], axis=1)
    im = jnp.concatenate([quarter(2), quarter(3)], axis=1)
    size = jnp.sqrt(re * re + im * im)
    first = lax.broadcasted_iota(jnp.int32, (8, HALF), 1) == 0
    total = jnp.sum(
        jnp.where(first, jnp.abs(re) + jnp.abs(im), size), axis=1, keepdims=True
    )
    level = WATER * (total / (HALF + 1) + 1e-06)
    re = re / (jnp.where(first, jnp.abs(re), size) + level)
    im = im / (jnp.where(first, jnp.abs(im), size) + level)
    picked[me_core, me_side] = jnp.concatenate([re, im], axis=0).astype(BF16)

    def side_copy(step, back=False):
        device, core, slot = moved(step)
        at = (core, slot) if back else (me_core, me_side)
        return pltpu.make_async_remote_copy(
            src_ref=picked.at[me_core, me_side],
            dst_ref=picked.at[at],
            send_sem=side_send.at[core, slot],
            recv_sem=side_recv.at[at],
            device_id=device,
            device_id_type=MESH,
        )

    for step in around:
        side_copy(step).start()

    def widen_next(step):
        x = lax.rem(me_x + step, NX)
        white_copy(me_x, x).wait_recv()
        widen(x)

    widen_next(1)
    widen_next(3)

    widen_next(2)

    for step in around[::-1]:
        side_copy(step, True).wait_recv()

    parts = []
    for x in range(NX):
        for w in range(WIN):
            tiles = []
            halves = [picked[w, low * NX + x].astype(F32) for low in range(NLOW)]
            for part in range(2):
                for big in range(4):
                    for half in halves:
                        tiles.append(
                            half[8 * part : 8 * part + 8, 128 * big : 128 * big + 128]
                        )
            parts.append(jnp.concatenate(tiles, axis=0))
    parts = block_transpose(parts)
    for small in range(8):
        a_re = parts[small][:64].astype(BF16)
        a_im = parts[small][64:].astype(BF16)
        re_b0, re_b1, im_b0, im_b1 = a_re, a_im, -a_im, a_re
        if small == 0:
            shape = (64, 128)
            zero_bin = jnp.logical_and(
                lax.broadcasted_iota(jnp.int32, shape, 0) < 16,
                lax.broadcasted_iota(jnp.int32, shape, 1) % 16 == 0,
            )
            zero = jnp.zeros(shape, BF16)
            re_b1 = jnp.where(zero_bin, zero, re_b1)
            im_b0 = jnp.where(zero_bin, zero, im_b0)
            im_b1 = jnp.where(zero_bin, a_im, im_b1)
        left[small, 0, 0] = re_b0
        left[small, 0, 1] = re_b1
        left[small, 1, 0] = im_b0
        left[small, 1, 1] = im_b1

    def cross_spectra(chunk):
        @pl.loop(0, 8)
        def _(small):
            for big in range(4):
                group = big * 8 + small
                rows_left = jnp.concatenate(
                    [
                        jnp.concatenate(
                            [left[small, part, p, big * 16 : big * 16 + 16, :] for p in range(2)],
                            axis=1,
                        )
                        for part in range(2)
                    ],
                    axis=0,
                )
                result = dot(rows_left, right[chunk, group])
                for h in range(2):
                    cross[chunk, h, pl.ds(group, 32, stride=SKIP), :] = result[
                        :, 128 * h : 128 * h + 128
                    ]

    loads[6].wait()

    ahead = lax.rem(me_z + 1, NZ)
    behind = lax.rem(me_z + NZ - 1, NZ)
    lag_rows = HALF // NZ
    top = pl.ds(0, lag_rows // 2)
    bottom = pl.ds(lag_rows // 2, lag_rows // 2)

    def z_copy(chunk, kind, way, to=None):
        source = [
            (lags_out.at[chunk, 1, top], lags_out.at[chunk, 1, bottom]),
            (lags_out.at[chunk, 0, bottom], lags_out.at[chunk, 2, top]),
            (mixed.at[chunk, 0], mixed.at[chunk, 1]),
        ][kind][way]
        return pltpu.make_async_remote_copy(
            src_ref=source,
            dst_ref=lags_in.at[chunk, kind, way],
            send_sem=z_send.at[chunk, kind, way],
            recv_sem=z_recv.at[chunk, kind, way],
            device_id=at_z((ahead, behind)[way]),
            device_id_type=MESH,
        )

    def lag_block(to, chunk):
        at = pl.ds(pl.multiple_of(to * lag_rows, lag_rows), lag_rows)
        return dot(inverse[at, :], stacked[:, WIDE * chunk : WIDE * chunk + WIDE])

    for chunk in range(CHUNKS):
        cross_spectra(chunk)
        for part in range(2):
            for octet in range(2):
                for h in range(2):
                    parts = [
                        cross[chunk, h, pl.ds((part * 16 + octet * 8 + i) * SKIP, 32), :].astype(BF16)
                        for i in range(8)
                    ]
                    parts = block_transpose(parts)
                    lane = WIDE * chunk + 128 * octet
                    for j in range(8):
                        at = (part * 16 + h * 8 + j) * 32
                        stacked[at : at + 32, lane : lane + 128] = parts[j]
        lags_out[chunk, 1] = lag_block(lax.rem(me_z + 2, NZ), chunk).astype(BF16)
        z_copy(chunk, 0, 0).start()
        z_copy(chunk, 0, 1).start()
        block = lag_block(ahead, chunk)
        lags_out[chunk, 0] = block.astype(BF16)
        kept[chunk, 0] = block[: lag_rows // 2]
        z_copy(chunk, 1, 0).start()
        block = lag_block(behind, chunk)
        lags_out[chunk, 2] = block.astype(BF16)
        kept[chunk, 1] = block[lag_rows // 2 :]
        z_copy(chunk, 1, 1).start()
        block = lag_block(me_z, chunk)
        kept[chunk, 2] = block[: lag_rows // 2]
        kept[chunk, 3] = block[lag_rows // 2 :]

    for chunk in range(CHUNKS):
        for way in range(2):
            z_copy(chunk, 0, way).wait_recv()
            total = kept[chunk, way] + lags_in[chunk, 0, way].astype(F32)
            mixed[chunk, way] = total.astype(BF16)
            z_copy(chunk, 2, way).start()

    own = lag_rows // NX

    def last_copy(chunk, to, slot):
        at = pl.ds(pl.multiple_of(to * own, own), own)
        return pltpu.make_async_remote_copy(
            src_ref=finished.at[chunk, at],
            dst_ref=last.at[chunk, slot],
            send_sem=last_send.at[chunk, to],
            recv_sem=last_recv.at[chunk, slot],
            device_id=at_x(to),
            device_id_type=MESH,
        )

    for chunk in range(CHUNKS):
        for kind in (1, 2):
            for way in range(2):
                z_copy(chunk, kind, way).wait_recv()
        for half in range(2):
            total = (
                kept[chunk, 2 + half]
                + lags_in[chunk, 2, half].astype(F32)
                + lags_in[chunk, 1, 1 - half].astype(F32)
            )
            finished[chunk, pl.ds(half * lag_rows // 2, lag_rows // 2)] = total.astype(BF16)
        for step in (2, 1, 3):
            last_copy(chunk, lax.rem(me_x + step, NX), me_x).start()
        last[chunk, me_x] = finished[chunk, pl.ds(pl.multiple_of(me_x * own, own), own), :]

    for chunk in range(CHUNKS):
        for step in (1, 3, 2):
            last_copy(chunk, me_x, lax.rem(me_x + step, NX)).wait_recv()
    for octet in range(2):
        parts = [
            last[chunk, x, :, 128 * octet : 128 * octet + 128]
            for x in range(NX)
            for chunk in range(CHUNKS)
        ]
        parts = block_transpose(parts)
        for j in range(8):
            s = octet * 8 + j
            out[:, 128 * s : 128 * s + 128] = parts[j]

    for step in (1, 2, 3):
        near_copy(lax.rem(me_near + step, near), me_near).wait_send()

    @pl.loop(1, ny)
    def _(step):
        y_copy(lax.rem(me_y + step, ny), me_y).wait_send()

    for step in around:
        side_copy(step).wait_send()

    for step in (1, 2, 3):
        to = lax.rem(me_x + step, NX)
        white_copy(to, me_x).wait_send()
        for chunk in range(CHUNKS):
            last_copy(chunk, to, me_x).wait_send()
    for chunk in range(CHUNKS):
        for kind in range(3):
            for way in range(2):
                z_copy(chunk, kind, way).wait_send()


def local(ny, record, offsets, sources):
    lag_rows = HALF // NZ
    own = lag_rows // NX
    upper, lower = forward_tables()
    inverse = inverse_table(NZ * NX * WIN)
    tables = np.concatenate([upper, lower, upper.T[:HALF], lower.T[:HALF], inverse], axis=0)
    vmem = pl.BlockSpec(memory_space=pltpu.VMEM)
    hbm = pl.BlockSpec(memory_space=pltpu.HBM)
    dma = pltpu.SemaphoreType.DMA
    flat = pl.pallas_call(
        functools.partial(kernel, ny),
        out_shape=jax.ShapeDtypeStruct((own, NSRC * ROWS), BF16),
        in_specs=[hbm, hbm, vmem, hbm],
        out_specs=vmem,
        scratch_shapes=[
            pltpu.SMEM((WIN,), jnp.int32),
            pltpu.SMEM((NSRC,), jnp.int32),
            pltpu.VMEM((SAMPLES, SAMPLES), BF16),
            pltpu.VMEM((SAMPLES, SAMPLES), BF16),
            pltpu.VMEM((HALF, SAMPLES), BF16),
            pltpu.VMEM((HALF, SAMPLES), BF16),
            pltpu.VMEM((HALF, SAMPLES), BF16),
            pltpu.VMEM((256, SAMPLES), BF16),
            pltpu.VMEM((2 * NLOW, 16, HALF), BF16),
            pltpu.VMEM((2 * NLOW, 16, HALF), BF16),
            pltpu.VMEM((ny, 16, HALF), BF16),
            pltpu.VMEM((2, NLOW * NX, 16, HALF), BF16),
            pltpu.VMEM((SAMPLES, 256), F32),
            pltpu.VMEM((NX, HALF, 128), BF16),
            pltpu.VMEM((NX, HALF, 128), BF16),
            pltpu.VMEM((8, 2, 2, 64, 128), BF16),
            pltpu.VMEM((HALF, 1024), BF16),
            pltpu.VMEM((CHUNKS, GROUPS, 256, 256), BF16),
            pltpu.VMEM((CHUNKS, 2, 32 * SKIP, 128), F32),
            pltpu.VMEM((SAMPLES, 512), BF16),
            pltpu.VMEM((CHUNKS, 3, lag_rows, WIDE), BF16),
            pltpu.VMEM((CHUNKS, 2, lag_rows // 2, WIDE), BF16),
            pltpu.VMEM((CHUNKS, 4, lag_rows // 2, WIDE), F32),
            pltpu.VMEM((CHUNKS, 3, 2, lag_rows // 2, WIDE), BF16),
            pltpu.VMEM((CHUNKS, lag_rows, WIDE), BF16),
            pltpu.VMEM((CHUNKS, NX, own, WIDE), BF16),
            dma((7,)),
            dma((2 * NLOW,)),
            dma((2 * NLOW,)),
            dma((ny,)),
            dma((ny,)),
            dma((2, NLOW * NX)),
            dma((2, NLOW * NX)),
            dma((NX,)),
            dma((NX,)),
            dma((CHUNKS, 3, 2)),
            dma((CHUNKS, 3, 2)),
            dma((CHUNKS, NX)),
            dma((CHUNKS, NX)),
        ],
        compiler_params=pltpu.CompilerParams(
            collective_id=0, has_side_effects=True, vmem_limit_bytes=53 * 1024 * 1024
        ),
        cost_estimate=pl.CostEstimate(
            flops=3 * 10**9, bytes_accessed=7 * 10**6, transcendentals=10**6
        ),
    )(
        offsets,
        sources,
        jnp.transpose(record, (1, 0, 2)),
        jnp.asarray(tables),
    )
    return flat.reshape(own, NSRC, ROWS)


def solution(mesh):
    ny = mesh.shape["chan"] // (2 * NLOW)
    in_specs = (P("chan", "spec", None), P("spec"), P())
    out_specs = P("spec", None, "chan")
    return jax.shard_map(
        functools.partial(local, ny),
        mesh=mesh,
        in_specs=in_specs,
        out_specs=out_specs,
        check_vma=False,
    )
```

```python
import functools
import math

import jax
import jax.numpy as jnp
import numpy as np
from jax import lax
from jax.experimental import pallas as pl
from jax.experimental.pallas import tpu as pltpu
from jax.sharding import PartitionSpec as P

SAMPLES = 1024
HALF = SAMPLES // 2
PAD = 128
NSRC = 16
WATER = 0.1
NX = 4
ROWS = 128
WIN = 2
BLK = ROWS // NX
GROUPS = 32
SKIP = 40
NLOW = 2
NZ = 4
CHUNKS = 2
PART = BLK // CHUNKS
WIDE = NSRC * PART
BINS = np.concatenate([np.arange(0, HALF, 2), np.arange(1, HALF, 2)])
F32 = jnp.float32
BF16 = jnp.bfloat16
MESH = pl.DeviceIdType.MESH


def forward_tables():
    rows = np.arange(SAMPLES)[:, None]
    cols = np.arange(SAMPLES)[None, :]
    freq = BINS[rows % HALF]
    angle = 2.0 * np.pi / SAMPLES * (freq * cols % SAMPLES)
    alternating = 1.0 - 2.0 * (cols % 2)
    imag = np.where(freq == 0, alternating, -np.sin(angle))
    table = np.where(rows < HALF, np.cos(angle), imag)
    upper = table.astype(jnp.bfloat16)
    lower = (table - upper.astype(np.float64)).astype(jnp.bfloat16)
    return upper, lower


def inverse_table(windows):
    shifted = np.arange(HALF)[:, None] - HALF // 2
    freq = BINS[(np.arange(16)[:, None] + 16 * np.arange(GROUPS)[None, :]).reshape(1, -1)]
    angle = 2.0 * np.pi / SAMPLES * (freq * shifted % SAMPLES)
    alternating = 1.0 - 2.0 * (shifted % 2)
    first = freq == 0
    real = np.where(first, 1.0, 2.0 * np.cos(angle))
    imag = np.where(first, alternating, -2.0 * np.sin(angle))
    table = np.concatenate([real, imag], axis=1) / math.sqrt(windows * SAMPLES)
    return table.astype(jnp.bfloat16)


def dot_t(left, right):
    return lax.dot_general(left, right, (((1,), (1,)), ((), ())), preferred_element_type=F32)


def dot(left, right):
    return lax.dot_general(left, right, (((1,), (0,)), ((), ())), preferred_element_type=F32)


def block_transpose(parts):
    count = len(parts)
    width = 128 // count
    lane = lax.broadcasted_iota(jnp.int32, parts[0].shape, 1)
    masks = [lane // width == i for i in range(count - 1)]

    def pick(choices):
        result = choices[-1]
        for mask, choice in zip(masks, choices):
            result = jnp.where(mask, choice, result)
        return result

    turned = []
    for d in range(count):
        part = pick([parts[(i - d) % count] for i in range(count)])
        turned.append(pltpu.roll(part, 128 - width * d, 1) if d else part)
    return [pick([turned[(j - i) % count] for i in range(count)]) for j in range(count)]


def kernel(
    ny,
    offsets_hbm,
    sources_hbm,
    record,
    tables_hbm,
    out,
    offsets,
    sources,
    upper,
    lower,
    upper_t,
    lower_t,
    inverse,
    traces,
    pieces,
    reduced,
    parts_y,
    picked,
    spectrum,
    outgoing,
    incoming,
    left,
    copies,
    right,
    cross,
    stacked,
    lags_out,
    mixed,
    kept,
    lags_in,
    finished,
    last,
    load_sem,
    near_send,
    near_recv,
    y_send,
    y_recv,
    side_send,
    side_recv,
    white_send,
    white_recv,
    z_send,
    z_recv,
    last_send,
    last_recv,
):
    plane = 2 * ny
    near = NLOW * 2
    chan = lax.axis_index("chan")
    spec = lax.axis_index("spec")
    me_x = lax.rem(spec, NX)
    me_z = spec // NX
    me_low = chan // plane
    me_plane = lax.rem(chan, plane)
    me_y = me_plane // 2
    me_core = lax.rem(chan, 2)
    me_side = me_low * NX + me_x
    me_near = me_low * 2 + me_core

    def at_near(other):
        return (other // 2 * plane + me_y * 2 + lax.rem(other, 2), spec)

    def at_y(other):
        return (me_low * plane + other * 2 + me_core, spec)

    around = sorted(
        (
            (low, x, core)
            for low in range(NLOW)
            for x in range(NX)
            for core in range(2)
            if low + x + core
        ),
        key=lambda step: -(step[0] + 2 * min(step[1], NX - step[1])),
    )

    def moved(step):
        low = lax.rem(me_low + step[0], NLOW)
        x = lax.rem(me_x + step[1], NX)
        core = lax.rem(me_core + step[2], 2)
        device = (low * plane + me_y * 2 + core, me_z * NX + x)
        return device, core, low * NX + x

    def at_x(other):
        return (chan, me_z * NX + other)

    def at_z(other):
        return (chan, other * NX + me_x)

    loads = [
        pltpu.make_async_copy(source, target, load_sem.at[i])
        for i, (source, target) in enumerate(
            [
                (offsets_hbm, offsets),
                (sources_hbm, sources),
                (tables_hbm.at[pl.ds(0, SAMPLES)], upper),
                (tables_hbm.at[pl.ds(SAMPLES, SAMPLES)], lower),
                (tables_hbm.at[pl.ds(2 * SAMPLES, HALF)], upper_t),
                (tables_hbm.at[pl.ds(2 * SAMPLES + HALF, HALF)], lower_t),
                (tables_hbm.at[pl.ds(3 * SAMPLES, HALF)], inverse),
            ]
        )
    ]
    for load in loads[:3]:
        load.start()

    barrier = pltpu.get_barrier_semaphore()

    def greet(device):
        pl.semaphore_signal(barrier, inc=1, device_id=device, device_id_type=MESH)

    @pl.loop(1, ny)
    def _(step):
        greet(at_y(lax.rem(me_y + step, ny)))

    for step in around:
        greet(moved(step)[0])

    for step in (1, NZ - 1):
        greet(at_z(lax.rem(me_z + step, NZ)))

    loads[0].wait()
    loads[1].wait()
    loads[3].start()

    lane = lax.broadcasted_iota(jnp.int32, (ROWS, 128), 1)
    for w in range(WIN):
        rows = record[w].astype(F32)
        head = jnp.where(lane < offsets[w], rows[:, SAMPLES:], rows[:, :PAD])
        rows = jnp.concatenate([head, rows[:, PAD:SAMPLES]], axis=1)
        rows = rows - jnp.mean(rows, axis=1, keepdims=True)
        rows = rows * lax.rsqrt(jnp.mean(rows * rows, axis=1, keepdims=True) + 1e-06)
        rows = rows.astype(BF16)
        for x in range(NX):
            traces[pl.ds(x * 64 + w * BLK, BLK), :] = rows[x * BLK : (x + 1) * BLK]

    row = lax.broadcasted_iota(jnp.int32, (32, 256), 0)
    col = lax.broadcasted_iota(jnp.int32, (32, 256), 1)
    wanted = jnp.zeros((32, 256), jnp.int32)
    for s in range(NSRC):
        wanted = jnp.where(row % NSRC == s, sources[s], wanted)
    channel = chan * ROWS + (col // 64) * BLK + col % BLK
    same = jnp.logical_and(wanted == channel, row // NSRC == (col // BLK) % 2)
    chosen = dot(jnp.where(same, 1.0, 0.0).astype(BF16), traces[...])
    for w in range(WIN):
        for low in range(NLOW):
            rows = chosen[16 * w + 8 * low : 16 * w + 8 * low + 8]
            rows = jnp.concatenate([rows[:, :HALF], rows[:, HALF:]], axis=0)
            pieces[low * 2 + w] = rows.astype(BF16)

    pl.semaphore_wait(barrier, ny - 1 + len(around) + 2)

    def near_copy(to, slot):
        return pltpu.make_async_remote_copy(
            src_ref=pieces.at[to],
            dst_ref=reduced.at[slot],
            send_sem=near_send.at[to],
            recv_sem=near_recv.at[slot],
            device_id=at_near(to),
            device_id_type=MESH,
        )

    for step in (2, 3, 1):
        near_copy(lax.rem(me_near + step, near), me_near).start()
    reduced[me_near] = pieces[me_near]
    loads[2].wait()
    for load in loads[4:]:
        load.start()
    spectrum[...] = dot_t(upper[...], traces[...])

    loads[3].wait()
    spectrum[...] += dot_t(lower[...], traces[...])

    chunk = 64
    first_row = lax.broadcasted_iota(jnp.int32, (chunk, 256), 0) == 0
    total = jnp.zeros((1, 256), F32)
    for k in range(0, HALF, chunk):
        re = spectrum[k : k + chunk]
        im = spectrum[HALF + k : HALF + k + chunk]
        size = jnp.sqrt(re * re + im * im)
        if k == 0:
            size = jnp.where(first_row, jnp.abs(re) + jnp.abs(im), size)
        total = total + jnp.sum(size, axis=0, keepdims=True)
    level = WATER * (total / (HALF + 1) + 1e-06)
    low = lax.broadcasted_iota(jnp.int32, (chunk, 128), 1) < 64
    for k in range(0, HALF, chunk):
        re = spectrum[k : k + chunk]
        im = spectrum[HALF + k : HALF + k + chunk]
        size = jnp.sqrt(re * re + im * im)
        if k == 0:
            re = re / (jnp.where(first_row, jnp.abs(re), size) + level)
            im = im / (jnp.where(first_row, jnp.abs(im), size) + level)
        else:
            scale = 1.0 / (size + level)
            re = re * scale
            im = im * scale
        for pair in range(2):
            a = re[:, 128 * pair : 128 * pair + 128]
            b = im[:, 128 * pair : 128 * pair + 128]
            even = jnp.where(low, a, pltpu.roll(b, 64, 1))
            odd = jnp.where(low, pltpu.roll(a, 64, 1), b)
            outgoing[2 * pair, k : k + chunk] = even.astype(BF16)
            outgoing[2 * pair + 1, k : k + chunk] = odd.astype(BF16)

    def white_copy(to, slot):
        return pltpu.make_async_remote_copy(
            src_ref=outgoing.at[to],
            dst_ref=incoming.at[slot],
            send_sem=white_send.at[to],
            recv_sem=white_recv.at[slot],
            device_id=at_x(to),
            device_id_type=MESH,
        )

    for step in (2, 1, 3):
        white_copy(lax.rem(me_x + step, NX), me_x).start()
    for step in (1, 2, 3):
        near_copy(me_near, lax.rem(me_near + step, near)).wait_recv()
    total = reduced[0].astype(F32)
    for i in range(1, near):
        total = total + reduced[i].astype(F32)
    parts_y[me_y] = total.astype(BF16)

    def y_copy(to, slot):
        return pltpu.make_async_remote_copy(
            src_ref=parts_y.at[me_y],
            dst_ref=parts_y.at[slot],
            send_sem=y_send.at[to],
            recv_sem=y_recv.at[slot],
            device_id=at_y(to),
            device_id_type=MESH,
        )

    for step in sorted(range(1, ny), key=lambda step: -min(step, ny - step)):
        y_copy(lax.rem(me_y + step, ny), me_y).start()

    incoming[me_x] = outgoing[me_x]

    r = lax.broadcasted_iota(jnp.int32, (128, 1024), 0)
    c = lax.broadcasted_iota(jnp.int32, (128, 1024), 1)
    match = jnp.logical_and(r // BLK == c // 256, r % BLK // PART == c // 128 % 2)
    match = jnp.logical_and(match, r % PART == c % PART)
    spread = jnp.where(match, 1.0, 0.0).astype(BF16)
    r = lax.broadcasted_iota(jnp.int32, (16, 256), 0)
    c = lax.broadcasted_iota(jnp.int32, (16, 256), 1)
    mask = jnp.where(r == c // PART, 1.0, 0.0).astype(BF16)

    def widen(x):
        copies[...] = dot(incoming[x], spread).astype(BF16)

        @pl.loop(0, 8)
        def _(small):
            for big in range(4):
                group = big * 8 + small
                at = pl.ds(pl.multiple_of(group * 16, 16), 16)
                for p in range(2):
                    for w in range(WIN):
                        slab = pl.multiple_of((p * 8 + x * 2 + w) * 16, 16)
                        for chunk in range(CHUNKS):
                            lane = (p * 2 + w) * 256 + chunk * 128
                            tile = copies[at, lane : lane + 128]
                            right[chunk, group, pl.ds(slab, 16), :] = (
                                jnp.concatenate([tile] * 2, axis=1) * mask
                            )

    widen(me_x)

    @pl.loop(1, ny)
    def _(step):
        y_copy(me_y, lax.rem(me_y + step, ny)).wait_recv()

    loads[4].wait()
    loads[5].wait()
    total = parts_y[0].astype(F32)
    for i in range(1, ny):
        total = total + parts_y[i].astype(F32)
    folded = []
    for rows in (total[:8] + total[8:], total[:8] - total[8:]):
        high = rows.astype(BF16)
        rest = (rows - high.astype(F32)).astype(BF16)
        folded.append(jnp.concatenate([high, rest], axis=0))

    def quarter(i):
        at = pl.ds(i * HALF // 2, HALF // 2)
        both = dot(folded[i % 2], upper_t[:, at]) + dot(folded[i % 2], lower_t[:, at])
        return both[:8] + both[8:]

    re = jnp.concatenate([quarter(0), quarter(1)], axis=1)
    im = jnp.concatenate([quarter(2), quarter(3)], axis=1)
    size = jnp.sqrt(re * re + im * im)
    first = lax.broadcasted_iota(jnp.int32, (8, HALF), 1) == 0
    total = jnp.sum(
        jnp.where(first, jnp.abs(re) + jnp.abs(im), size), axis=1, keepdims=True
    )
    level = WATER * (total / (HALF + 1) + 1e-06)
    re = re / (jnp.where(first, jnp.abs(re), size) + level)
    im = im / (jnp.where(first, jnp.abs(im), size) + level)
    picked[me_core, me_side] = jnp.concatenate([re, im], axis=0).astype(BF16)

    def side_copy(step, back=False):
        device, core, slot = moved(step)
        at = (core, slot) if back else (me_core, me_side)
        return pltpu.make_async_remote_copy(
            src_ref=picked.at[me_core, me_side],
            dst_ref=picked.at[at],
            send_sem=side_send.at[core, slot],
            recv_sem=side_recv.at[at],
            device_id=device,
            device_id_type=MESH,
        )

    for step in around:
        side_copy(step).start()

    def widen_next(step):
        x = lax.rem(me_x + step, NX)
        white_copy(me_x, x).wait_recv()
        widen(x)

    widen_next(1)
    widen_next(3)

    widen_next(2)

    for step in around[::-1]:
        side_copy(step, True).wait_recv()

    parts = []
    for x in range(NX):
        for w in range(WIN):
            tiles = []
            halves = [picked[w, low * NX + x].astype(F32) for low in range(NLOW)]
            for part in range(2):
                for big in range(4):
                    for half in halves:
                        tiles.append(
                            half[8 * part : 8 * part + 8, 128 * big : 128 * big + 128]
                        )
            parts.append(jnp.concatenate(tiles, axis=0).astype(BF16))
    parts = block_transpose(parts)
    for small in range(8):
        a_re = parts[small][:64]
        a_im = parts[small][64:]
        re_b0, re_b1, im_b0, im_b1 = a_re, a_im, -a_im, a_re
        if small == 0:
            shape = (64, 128)
            zero_bin = jnp.logical_and(
                lax.broadcasted_iota(jnp.int32, shape, 0) < 16,
                lax.broadcasted_iota(jnp.int32, shape, 1) % 16 == 0,
            )
            zero = jnp.zeros(shape, BF16)
            re_b1 = jnp.where(zero_bin, zero, re_b1)
            im_b0 = jnp.where(zero_bin, zero, im_b0)
            im_b1 = jnp.where(zero_bin, a_im, im_b1)
        left[small, 0, 0] = re_b0
        left[small, 0, 1] = re_b1
        left[small, 1, 0] = im_b0
        left[small, 1, 1] = im_b1

    def cross_spectra(chunk):
        @pl.loop(0, 8)
        def _(small):
            for big in range(4):
                group = big * 8 + small
                rows_left = jnp.concatenate(
                    [
                        jnp.concatenate(
                            [left[small, part, p, big * 16 : big * 16 + 16, :] for p in range(2)],
                            axis=1,
                        )
                        for part in range(2)
                    ],
                    axis=0,
                )
                result = dot(rows_left, right[chunk, group])
                for h in range(2):
                    cross[chunk, h, pl.ds(group, 32, stride=SKIP), :] = result[
                        :, 128 * h : 128 * h + 128
                    ]

    loads[6].wait()

    ahead = lax.rem(me_z + 1, NZ)
    behind = lax.rem(me_z + NZ - 1, NZ)
    lag_rows = HALF // NZ
    top = pl.ds(0, lag_rows // 2)
    bottom = pl.ds(lag_rows // 2, lag_rows // 2)

    def z_copy(chunk, kind, way, to=None):
        source = [
            (lags_out.at[chunk, 1, top], lags_out.at[chunk, 1, bottom]),
            (lags_out.at[chunk, 0, bottom], lags_out.at[chunk, 2, top]),
            (mixed.at[chunk, 0], mixed.at[chunk, 1]),
        ][kind][way]
        return pltpu.make_async_remote_copy(
            src_ref=source,
            dst_ref=lags_in.at[chunk, kind, way],
            send_sem=z_send.at[chunk, kind, way],
            recv_sem=z_recv.at[chunk, kind, way],
            device_id=at_z((ahead, behind)[way]),
            device_id_type=MESH,
        )

    def lag_block(to, chunk):
        at = pl.ds(pl.multiple_of(to * lag_rows, lag_rows), lag_rows)
        return dot(inverse[at, :], stacked[:, WIDE * chunk : WIDE * chunk + WIDE])

    for chunk in range(CHUNKS):
        cross_spectra(chunk)
        for part in range(2):
            for octet in range(2):
                for h in range(2):
                    parts = [
                        cross[chunk, h, pl.ds((part * 16 + octet * 8 + i) * SKIP, 32), :].astype(BF16)
                        for i in range(8)
                    ]
                    parts = block_transpose(parts)
                    lane = WIDE * chunk + 128 * octet
                    for j in range(8):
                        at = (part * 16 + h * 8 + j) * 32
                        stacked[at : at + 32, lane : lane + 128] = parts[j]
        lags_out[chunk, 1] = lag_block(lax.rem(me_z + 2, NZ), chunk).astype(BF16)
        z_copy(chunk, 0, 0).start()
        z_copy(chunk, 0, 1).start()
        block = lag_block(ahead, chunk)
        lags_out[chunk, 0] = block.astype(BF16)
        kept[chunk, 0] = block[: lag_rows // 2]
        z_copy(chunk, 1, 0).start()
        block = lag_block(behind, chunk)
        lags_out[chunk, 2] = block.astype(BF16)
        kept[chunk, 1] = block[lag_rows // 2 :]
        z_copy(chunk, 1, 1).start()
        block = lag_block(me_z, chunk)
        kept[chunk, 2] = block[: lag_rows // 2]
        kept[chunk, 3] = block[lag_rows // 2 :]

    for chunk in range(CHUNKS):
        for way in range(2):
            z_copy(chunk, 0, way).wait_recv()
            total = kept[chunk, way] + lags_in[chunk, 0, way].astype(F32)
            mixed[chunk, way] = total.astype(BF16)
            z_copy(chunk, 2, way).start()

    own = lag_rows // NX

    def last_copy(chunk, to, slot):
        at = pl.ds(pl.multiple_of(to * own, own), own)
        return pltpu.make_async_remote_copy(
            src_ref=finished.at[chunk, at],
            dst_ref=last.at[chunk, slot],
            send_sem=last_send.at[chunk, to],
            recv_sem=last_recv.at[chunk, slot],
            device_id=at_x(to),
            device_id_type=MESH,
        )

    for chunk in range(CHUNKS):
        for kind in (1, 2):
            for way in range(2):
                z_copy(chunk, kind, way).wait_recv()
        for half in range(2):
            total = (
                kept[chunk, 2 + half]
                + lags_in[chunk, 2, half].astype(F32)
                + lags_in[chunk, 1, 1 - half].astype(F32)
            )
            finished[chunk, pl.ds(half * lag_rows // 2, lag_rows // 2)] = total.astype(BF16)
        for step in (2, 1, 3):
            last_copy(chunk, lax.rem(me_x + step, NX), me_x).start()
        last[chunk, me_x] = finished[chunk, pl.ds(pl.multiple_of(me_x * own, own), own), :]

    for chunk in range(CHUNKS):
        for step in (1, 3, 2):
            last_copy(chunk, me_x, lax.rem(me_x + step, NX)).wait_recv()
    for octet in range(2):
        parts = [
            last[chunk, x, :, 128 * octet : 128 * octet + 128]
            for x in range(NX)
            for chunk in range(CHUNKS)
        ]
        parts = block_transpose(parts)
        for j in range(8):
            s = octet * 8 + j
            out[:, 128 * s : 128 * s + 128] = parts[j]

    for step in (1, 2, 3):
        near_copy(lax.rem(me_near + step, near), me_near).wait_send()

    @pl.loop(1, ny)
    def _(step):
        y_copy(lax.rem(me_y + step, ny), me_y).wait_send()

    for step in around:
        side_copy(step).wait_send()

    for step in (1, 2, 3):
        to = lax.rem(me_x + step, NX)
        white_copy(to, me_x).wait_send()
        for chunk in range(CHUNKS):
            last_copy(chunk, to, me_x).wait_send()
    for chunk in range(CHUNKS):
        for kind in range(3):
            for way in range(2):
                z_copy(chunk, kind, way).wait_send()


def local(ny, record, offsets, sources):
    lag_rows = HALF // NZ
    own = lag_rows // NX
    upper, lower = forward_tables()
    inverse = inverse_table(NZ * NX * WIN)
    tables = np.concatenate([upper, lower, upper.T[:HALF], lower.T[:HALF], inverse], axis=0)
    vmem = pl.BlockSpec(memory_space=pltpu.VMEM)
    hbm = pl.BlockSpec(memory_space=pltpu.HBM)
    dma = pltpu.SemaphoreType.DMA
    flat = pl.pallas_call(
        functools.partial(kernel, ny),
        out_shape=jax.ShapeDtypeStruct((own, NSRC * ROWS), BF16),
        in_specs=[hbm, hbm, vmem, hbm],
        out_specs=vmem,
        scratch_shapes=[
            pltpu.SMEM((WIN,), jnp.int32),
            pltpu.SMEM((NSRC,), jnp.int32),
            pltpu.VMEM((SAMPLES, SAMPLES), BF16),
            pltpu.VMEM((SAMPLES, SAMPLES), BF16),
            pltpu.VMEM((HALF, SAMPLES), BF16),
            pltpu.VMEM((HALF, SAMPLES), BF16),
            pltpu.VMEM((HALF, SAMPLES), BF16),
            pltpu.VMEM((256, SAMPLES), BF16),
            pltpu.VMEM((2 * NLOW, 16, HALF), BF16),
            pltpu.VMEM((2 * NLOW, 16, HALF), BF16),
            pltpu.VMEM((ny, 16, HALF), BF16),
            pltpu.VMEM((2, NLOW * NX, 16, HALF), BF16),
            pltpu.VMEM((SAMPLES, 256), F32),
            pltpu.VMEM((NX, HALF, 128), BF16),
            pltpu.VMEM((NX, HALF, 128), BF16),
            pltpu.VMEM((8, 2, 2, 64, 128), BF16),
            pltpu.VMEM((HALF, 1024), BF16),
            pltpu.VMEM((CHUNKS, GROUPS, 256, 256), BF16),
            pltpu.VMEM((CHUNKS, 2, 32 * SKIP, 128), F32),
            pltpu.VMEM((SAMPLES, 512), BF16),
            pltpu.VMEM((CHUNKS, 3, lag_rows, WIDE), BF16),
            pltpu.VMEM((CHUNKS, 2, lag_rows // 2, WIDE), BF16),
            pltpu.VMEM((CHUNKS, 4, lag_rows // 2, WIDE), F32),
            pltpu.VMEM((CHUNKS, 3, 2, lag_rows // 2, WIDE), BF16),
            pltpu.VMEM((CHUNKS, lag_rows, WIDE), BF16),
            pltpu.VMEM((CHUNKS, NX, own, WIDE), BF16),
            dma((7,)),
            dma((2 * NLOW,)),
            dma((2 * NLOW,)),
            dma((ny,)),
            dma((ny,)),
            dma((2, NLOW * NX)),
            dma((2, NLOW * NX)),
            dma((NX,)),
            dma((NX,)),
            dma((CHUNKS, 3, 2)),
            dma((CHUNKS, 3, 2)),
            dma((CHUNKS, NX)),
            dma((CHUNKS, NX)),
        ],
        compiler_params=pltpu.CompilerParams(
            collective_id=0, has_side_effects=True, vmem_limit_bytes=53 * 1024 * 1024
        ),
        cost_estimate=pl.CostEstimate(
            flops=3 * 10**9, bytes_accessed=7 * 10**6, transcendentals=10**6
        ),
    )(
        offsets,
        sources,
        jnp.transpose(record, (1, 0, 2)),
        jnp.asarray(tables),
    )
    return flat.reshape(own, NSRC, ROWS)


def solution(mesh):
    ny = mesh.shape["chan"] // (2 * NLOW)
    in_specs = (P("chan", "spec", None), P("spec"), P())
    out_specs = P("spec", None, "chan")
    return jax.shard_map(
        functools.partial(local, ny),
        mesh=mesh,
        in_specs=in_specs,
        out_specs=out_specs,
        check_vma=False,
    )
```

```python
import functools
import math

import jax
import jax.numpy as jnp
import numpy as np
from jax import lax
from jax.experimental import pallas as pl
from jax.experimental.pallas import tpu as pltpu
from jax.sharding import PartitionSpec as P

SAMPLES = 1024
HALF = SAMPLES // 2
PAD = 128
NSRC = 16
WATER = 0.1
NX = 4
ROWS = 128
WIN = 2
BLK = ROWS // NX
GROUPS = 32
SKIP = 40
NLOW = 2
NZ = 4
CHUNKS = 2
PART = BLK // CHUNKS
WIDE = NSRC * PART
BINS = np.concatenate([np.arange(0, HALF, 2), np.arange(1, HALF, 2)])
F32 = jnp.float32
BF16 = jnp.bfloat16
MESH = pl.DeviceIdType.MESH


def forward_tables():
    rows = np.arange(SAMPLES)[:, None]
    cols = np.arange(SAMPLES)[None, :]
    freq = BINS[rows % HALF]
    angle = 2.0 * np.pi / SAMPLES * (freq * cols % SAMPLES)
    alternating = 1.0 - 2.0 * (cols % 2)
    imag = np.where(freq == 0, alternating, -np.sin(angle))
    table = np.where(rows < HALF, np.cos(angle), imag)
    upper = table.astype(jnp.bfloat16)
    lower = (table - upper.astype(np.float64)).astype(jnp.bfloat16)
    return upper, lower


def inverse_table(windows):
    shifted = np.arange(HALF)[:, None] - HALF // 2
    freq = BINS[(np.arange(16)[:, None] + 16 * np.arange(GROUPS)[None, :]).reshape(1, -1)]
    angle = 2.0 * np.pi / SAMPLES * (freq * shifted % SAMPLES)
    alternating = 1.0 - 2.0 * (shifted % 2)
    first = freq == 0
    real = np.where(first, 1.0, 2.0 * np.cos(angle))
    imag = np.where(first, alternating, -2.0 * np.sin(angle))
    table = np.concatenate([real, imag], axis=1) / math.sqrt(windows * SAMPLES)
    return table.astype(jnp.bfloat16)


def dot_t(left, right):
    return lax.dot_general(left, right, (((1,), (1,)), ((), ())), preferred_element_type=F32)


def dot(left, right):
    return lax.dot_general(left, right, (((1,), (0,)), ((), ())), preferred_element_type=F32)


def block_transpose(parts):
    count = len(parts)
    width = 128 // count
    lane = lax.broadcasted_iota(jnp.int32, parts[0].shape, 1)
    masks = [lane // width == i for i in range(count - 1)]

    def pick(choices):
        result = choices[-1]
        for mask, choice in zip(masks, choices):
            result = jnp.where(mask, choice, result)
        return result

    turned = []
    for d in range(count):
        part = pick([parts[(i - d) % count] for i in range(count)])
        turned.append(pltpu.roll(part, 128 - width * d, 1) if d else part)
    return [pick([turned[(j - i) % count] for i in range(count)]) for j in range(count)]


def kernel(
    ny,
    offsets_hbm,
    sources_hbm,
    record,
    tables_hbm,
    out,
    offsets,
    sources,
    upper,
    lower,
    upper_t,
    lower_t,
    inverse,
    traces,
    pieces,
    reduced,
    parts_y,
    picked,
    spectrum,
    outgoing,
    incoming,
    left,
    copies,
    right,
    cross,
    stacked,
    lags_out,
    mixed,
    kept,
    lags_in,
    finished,
    last,
    load_sem,
    near_send,
    near_recv,
    y_send,
    y_recv,
    side_send,
    side_recv,
    white_send,
    white_recv,
    z_send,
    z_recv,
    last_send,
    last_recv,
):
    plane = 2 * ny
    near = NLOW * 2
    chan = lax.axis_index("chan")
    spec = lax.axis_index("spec")
    me_x = lax.rem(spec, NX)
    me_z = spec // NX
    me_low = chan // plane
    me_plane = lax.rem(chan, plane)
    me_y = me_plane // 2
    me_core = lax.rem(chan, 2)
    me_side = me_low * NX + me_x
    me_near = me_low * 2 + me_core

    def at_near(other):
        return (other // 2 * plane + me_y * 2 + lax.rem(other, 2), spec)

    def at_y(other):
        return (me_low * plane + other * 2 + me_core, spec)

    around = sorted(
        (
            (low, x, core)
            for low in range(NLOW)
            for x in range(NX)
            for core in range(2)
            if low + x + core
        ),
        key=lambda step: -(step[0] + 2 * min(step[1], NX - step[1])),
    )

    def moved(step):
        low = lax.rem(me_low + step[0], NLOW)
        x = lax.rem(me_x + step[1], NX)
        core = lax.rem(me_core + step[2], 2)
        device = (low * plane + me_y * 2 + core, me_z * NX + x)
        return device, core, low * NX + x

    def at_x(other):
        return (chan, me_z * NX + other)

    def at_z(other):
        return (chan, other * NX + me_x)

    loads = [
        pltpu.make_async_copy(source, target, load_sem.at[i])
        for i, (source, target) in enumerate(
            [
                (offsets_hbm, offsets),
                (sources_hbm, sources),
                (tables_hbm.at[pl.ds(0, SAMPLES)], upper),
                (tables_hbm.at[pl.ds(SAMPLES, SAMPLES)], lower),
                (tables_hbm.at[pl.ds(2 * SAMPLES, HALF)], upper_t),
                (tables_hbm.at[pl.ds(2 * SAMPLES + HALF, HALF)], lower_t),
                (tables_hbm.at[pl.ds(3 * SAMPLES, HALF)], inverse),
            ]
        )
    ]
    for load in loads[:3]:
        load.start()

    barrier = pltpu.get_barrier_semaphore()

    def greet(device):
        pl.semaphore_signal(barrier, inc=1, device_id=device, device_id_type=MESH)

    @pl.loop(1, ny)
    def _(step):
        greet(at_y(lax.rem(me_y + step, ny)))

    for step in around:
        greet(moved(step)[0])

    for step in (1, NZ - 1):
        greet(at_z(lax.rem(me_z + step, NZ)))

    loads[0].wait()
    loads[1].wait()
    loads[3].start()

    lane = lax.broadcasted_iota(jnp.int32, (ROWS, 128), 1)
    for w in range(WIN):
        rows = record[w].astype(F32)
        head = jnp.where(lane < offsets[w], rows[:, SAMPLES:], rows[:, :PAD])
        rows = jnp.concatenate([head, rows[:, PAD:SAMPLES]], axis=1)
        rows = rows - jnp.mean(rows, axis=1, keepdims=True)
        rows = rows * lax.rsqrt(jnp.mean(rows * rows, axis=1, keepdims=True) + 1e-06)
        rows = rows.astype(BF16)
        for x in range(NX):
            traces[pl.ds(x * 64 + w * BLK, BLK), :] = rows[x * BLK : (x + 1) * BLK]

    row = lax.broadcasted_iota(jnp.int32, (32, 256), 0)
    col = lax.broadcasted_iota(jnp.int32, (32, 256), 1)
    wanted = jnp.zeros((32, 256), jnp.int32)
    for s in range(NSRC):
        wanted = jnp.where(row % NSRC == s, sources[s], wanted)
    channel = chan * ROWS + (col // 64) * BLK + col % BLK
    same = jnp.logical_and(wanted == channel, row // NSRC == (col // BLK) % 2)
    chosen = dot(jnp.where(same, 1.0, 0.0).astype(BF16), traces[...])
    for w in range(WIN):
        for low in range(NLOW):
            rows = chosen[16 * w + 8 * low : 16 * w + 8 * low + 8]
            rows = jnp.concatenate([rows[:, :HALF], rows[:, HALF:]], axis=0)
            pieces[low * 2 + w] = rows.astype(BF16)

    pl.semaphore_wait(barrier, ny - 1 + len(around) + 2)

    def near_copy(to, slot):
        return pltpu.make_async_remote_copy(
            src_ref=pieces.at[to],
            dst_ref=reduced.at[slot],
            send_sem=near_send.at[to],
            recv_sem=near_recv.at[slot],
            device_id=at_near(to),
            device_id_type=MESH,
        )

    for step in (2, 3, 1):
        near_copy(lax.rem(me_near + step, near), me_near).start()
    reduced[me_near] = pieces[me_near]
    loads[2].wait()
    for load in loads[4:]:
        load.start()
    spectrum[...] = dot_t(upper[...], traces[...])

    loads[3].wait()
    spectrum[...] += dot_t(lower[...], traces[...])

    chunk = 64
    first_row = lax.broadcasted_iota(jnp.int32, (chunk, 256), 0) == 0
    total = jnp.zeros((1, 256), F32)
    for k in range(0, HALF, chunk):
        re = spectrum[k : k + chunk]
        im = spectrum[HALF + k : HALF + k + chunk]
        size = jnp.sqrt(re * re + im * im)
        if k == 0:
            size = jnp.where(first_row, jnp.abs(re) + jnp.abs(im), size)
        total = total + jnp.sum(size, axis=0, keepdims=True)
    level = WATER * (total / (HALF + 1) + 1e-06)
    low = lax.broadcasted_iota(jnp.int32, (chunk, 128), 1) < 64
    for k in range(0, HALF, chunk):
        re = spectrum[k : k + chunk]
        im = spectrum[HALF + k : HALF + k + chunk]
        size = jnp.sqrt(re * re + im * im)
        if k == 0:
            re = re / (jnp.where(first_row, jnp.abs(re), size) + level)
            im = im / (jnp.where(first_row, jnp.abs(im), size) + level)
        else:
            scale = 1.0 / (size + level)
            re = re * scale
            im = im * scale
        for pair in range(2):
            a = re[:, 128 * pair : 128 * pair + 128]
            b = im[:, 128 * pair : 128 * pair + 128]
            even = jnp.where(low, a, pltpu.roll(b, 64, 1))
            odd = jnp.where(low, pltpu.roll(a, 64, 1), b)
            outgoing[2 * pair, k : k + chunk] = even.astype(BF16)
            outgoing[2 * pair + 1, k : k + chunk] = odd.astype(BF16)

    def white_copy(to, slot):
        return pltpu.make_async_remote_copy(
            src_ref=outgoing.at[to],
            dst_ref=incoming.at[slot],
            send_sem=white_send.at[to],
            recv_sem=white_recv.at[slot],
            device_id=at_x(to),
            device_id_type=MESH,
        )

    for step in (2, 1, 3):
        white_copy(lax.rem(me_x + step, NX), me_x).start()
    for step in (1, 2, 3):
        near_copy(me_near, lax.rem(me_near + step, near)).wait_recv()
    total = reduced[0].astype(F32)
    for i in range(1, near):
        total = total + reduced[i].astype(F32)
    parts_y[me_y] = total.astype(BF16)

    def y_copy(to, slot):
        return pltpu.make_async_remote_copy(
            src_ref=parts_y.at[me_y],
            dst_ref=parts_y.at[slot],
            send_sem=y_send.at[to],
            recv_sem=y_recv.at[slot],
            device_id=at_y(to),
            device_id_type=MESH,
        )

    for step in sorted(range(1, ny), key=lambda step: -min(step, ny - step)):
        y_copy(lax.rem(me_y + step, ny), me_y).start()

    incoming[me_x] = outgoing[me_x]

    r = lax.broadcasted_iota(jnp.int32, (128, 1024), 0)
    c = lax.broadcasted_iota(jnp.int32, (128, 1024), 1)
    match = jnp.logical_and(r // BLK == c // 256, r % BLK // PART == c // 128 % 2)
    match = jnp.logical_and(match, r % PART == c % PART)
    spread = jnp.where(match, 1.0, 0.0).astype(BF16)
    r = lax.broadcasted_iota(jnp.int32, (16, 256), 0)
    c = lax.broadcasted_iota(jnp.int32, (16, 256), 1)
    mask = jnp.where(r == c // PART, 1.0, 0.0).astype(BF16)

    def widen(x):
        copies[...] = dot(incoming[x], spread).astype(BF16)

        @pl.loop(0, 8)
        def _(small):
            for big in range(4):
                group = big * 8 + small
                at = pl.ds(pl.multiple_of(group * 16, 16), 16)
                for p in range(2):
                    for w in range(WIN):
                        slab = pl.multiple_of((p * 8 + x * 2 + w) * 16, 16)
                        for chunk in range(CHUNKS):
                            lane = (p * 2 + w) * 256 + chunk * 128
                            tile = copies[at, lane : lane + 128]
                            right[chunk, group, pl.ds(slab, 16), :] = (
                                jnp.concatenate([tile] * 2, axis=1) * mask
                            )

    widen(me_x)

    @pl.loop(1, ny)
    def _(step):
        y_copy(me_y, lax.rem(me_y + step, ny)).wait_recv()

    loads[4].wait()
    loads[5].wait()
    total = parts_y[0].astype(F32)
    for i in range(1, ny):
        total = total + parts_y[i].astype(F32)
    folded = []
    for rows in (total[:8] + total[8:], total[:8] - total[8:]):
        high = rows.astype(BF16)
        rest = (rows - high.astype(F32)).astype(BF16)
        folded.append(jnp.concatenate([high, rest], axis=0))

    def quarter(i):
        at = pl.ds(i * HALF // 2, HALF // 2)
        both = dot(folded[i % 2], upper_t[:, at]) + dot(folded[i % 2], lower_t[:, at])
        return both[:8] + both[8:]

    re = jnp.concatenate([quarter(0), quarter(1)], axis=1)
    im = jnp.concatenate([quarter(2), quarter(3)], axis=1)
    size = jnp.sqrt(re * re + im * im)
    first = lax.broadcasted_iota(jnp.int32, (8, HALF), 1) == 0
    total = jnp.sum(
        jnp.where(first, jnp.abs(re) + jnp.abs(im), size), axis=1, keepdims=True
    )
    level = WATER * (total / (HALF + 1) + 1e-06)
    re = re / (jnp.where(first, jnp.abs(re), size) + level)
    im = im / (jnp.where(first, jnp.abs(im), size) + level)
    picked[me_core, me_side] = jnp.concatenate([re, im], axis=0).astype(BF16)

    def side_copy(step, back=False):
        device, core, slot = moved(step)
        at = (core, slot) if back else (me_core, me_side)
        return pltpu.make_async_remote_copy(
            src_ref=picked.at[me_core, me_side],
            dst_ref=picked.at[at],
            send_sem=side_send.at[core, slot],
            recv_sem=side_recv.at[at],
            device_id=device,
            device_id_type=MESH,
        )

    for step in around:
        side_copy(step).start()

    def widen_next(step):
        x = lax.rem(me_x + step, NX)
        white_copy(me_x, x).wait_recv()
        widen(x)

    widen_next(1)
    widen_next(3)

    widen_next(2)

    for step in around[::-1]:
        side_copy(step, True).wait_recv()

    parts = []
    for x in range(NX):
        for w in range(WIN):
            tiles = []
            halves = [picked[w, low * NX + x].astype(F32) for low in range(NLOW)]
            for part in range(2):
                for big in range(4):
                    for half in halves:
                        tiles.append(
                            half[8 * part : 8 * part + 8, 128 * big : 128 * big + 128]
                        )
            parts.append(jnp.concatenate(tiles, axis=0).astype(BF16))
    parts = block_transpose(parts)
    for small in range(8):
        a_re = parts[small][:64]
        a_im = parts[small][64:]
        re_b0, re_b1, im_b0, im_b1 = a_re, a_im, -a_im, a_re
        if small == 0:
            shape = (64, 128)
            zero_bin = jnp.logical_and(
                lax.broadcasted_iota(jnp.int32, shape, 0) < 16,
                lax.broadcasted_iota(jnp.int32, shape, 1) % 16 == 0,
            )
            zero = jnp.zeros(shape, BF16)
            re_b1 = jnp.where(zero_bin, zero, re_b1)
            im_b0 = jnp.where(zero_bin, zero, im_b0)
            im_b1 = jnp.where(zero_bin, a_im, im_b1)
        left[small, 0, 0] = re_b0
        left[small, 0, 1] = re_b1
        left[small, 1, 0] = im_b0
        left[small, 1, 1] = im_b1

    def cross_spectra(chunk):
        @pl.loop(0, 8)
        def _(small):
            for big in range(4):
                group = big * 8 + small
                rows_left = jnp.concatenate(
                    [
                        jnp.concatenate(
                            [left[small, part, p, big * 16 : big * 16 + 16, :] for p in range(2)],
                            axis=1,
                        )
                        for part in range(2)
                    ],
                    axis=0,
                )
                result = dot(rows_left, right[chunk, group])
                for h in range(2):
                    cross[chunk, h, pl.ds(group, 32, stride=SKIP), :] = result[
                        :, 128 * h : 128 * h + 128
                    ]

    loads[6].wait()

    ahead = lax.rem(me_z + 1, NZ)
    behind = lax.rem(me_z + NZ - 1, NZ)
    lag_rows = HALF // NZ
    top = pl.ds(0, lag_rows // 2)
    bottom = pl.ds(lag_rows // 2, lag_rows // 2)

    def z_copy(chunk, kind, way, to=None):
        source = [
            (lags_out.at[chunk, 1, top], lags_out.at[chunk, 1, bottom]),
            (lags_out.at[chunk, 0, bottom], lags_out.at[chunk, 2, top]),
            (mixed.at[chunk, 0], mixed.at[chunk, 1]),
        ][kind][way]
        return pltpu.make_async_remote_copy(
            src_ref=source,
            dst_ref=lags_in.at[chunk, kind, way],
            send_sem=z_send.at[chunk, kind, way],
            recv_sem=z_recv.at[chunk, kind, way],
            device_id=at_z((ahead, behind)[way]),
            device_id_type=MESH,
        )

    def lag_block(to, chunk):
        at = pl.ds(pl.multiple_of(to * lag_rows, lag_rows), lag_rows)
        return dot(inverse[at, :], stacked[:, WIDE * chunk : WIDE * chunk + WIDE])

    for chunk in range(CHUNKS):
        cross_spectra(chunk)
        for part in range(2):
            for octet in range(2):
                for h in range(2):
                    parts = [
                        cross[chunk, h, pl.ds((part * 16 + octet * 8 + i) * SKIP, 32), :].astype(BF16)
                        for i in range(8)
                    ]
                    parts = block_transpose(parts)
                    lane = WIDE * chunk + 128 * octet
                    for j in range(8):
                        at = (part * 16 + h * 8 + j) * 32
                        stacked[at : at + 32, lane : lane + 128] = parts[j]
        lags_out[chunk, 1] = lag_block(lax.rem(me_z + 2, NZ), chunk).astype(BF16)
        z_copy(chunk, 0, 0).start()
        z_copy(chunk, 0, 1).start()
        block = lag_block(ahead, chunk)
        lags_out[chunk, 0] = block.astype(BF16)
        kept[chunk, 0] = block[: lag_rows // 2]
        z_copy(chunk, 1, 0).start()
        block = lag_block(behind, chunk)
        lags_out[chunk, 2] = block.astype(BF16)
        kept[chunk, 1] = block[lag_rows // 2 :]
        z_copy(chunk, 1, 1).start()
        block = lag_block(me_z, chunk)
        kept[chunk, 2] = block[: lag_rows // 2]
        kept[chunk, 3] = block[lag_rows // 2 :]

    for chunk in range(CHUNKS):
        for way in range(2):
            z_copy(chunk, 0, way).wait_recv()
            total = kept[chunk, way] + lags_in[chunk, 0, way].astype(F32)
            mixed[chunk, way] = total.astype(BF16)
            z_copy(chunk, 2, way).start()

    own = lag_rows // NX

    def last_copy(chunk, to, slot):
        at = pl.ds(pl.multiple_of(to * own, own), own)
        return pltpu.make_async_remote_copy(
            src_ref=finished.at[chunk, at],
            dst_ref=last.at[chunk, slot],
            send_sem=last_send.at[chunk, to],
            recv_sem=last_recv.at[chunk, slot],
            device_id=at_x(to),
            device_id_type=MESH,
        )

    for chunk in range(CHUNKS):
        for kind in (1, 2):
            for way in range(2):
                z_copy(chunk, kind, way).wait_recv()
        for half in range(2):
            total = (
                kept[chunk, 2 + half]
                + lags_in[chunk, 2, half].astype(F32)
                + lags_in[chunk, 1, 1 - half].astype(F32)
            )
            finished[chunk, pl.ds(half * lag_rows // 2, lag_rows // 2)] = total.astype(BF16)
        for step in (2, 1, 3):
            last_copy(chunk, lax.rem(me_x + step, NX), me_x).start()
        last[chunk, me_x] = finished[chunk, pl.ds(pl.multiple_of(me_x * own, own), own), :]

    for chunk in range(CHUNKS):
        for step in (1, 3, 2):
            last_copy(chunk, me_x, lax.rem(me_x + step, NX)).wait_recv()
    for octet in range(2):
        parts = [
            last[chunk, x, :, 128 * octet : 128 * octet + 128]
            for x in range(NX)
            for chunk in range(CHUNKS)
        ]
        parts = block_transpose(parts)
        for j in range(8):
            s = octet * 8 + j
            out[:, 128 * s : 128 * s + 128] = parts[j]

    for step in (1, 2, 3):
        near_copy(lax.rem(me_near + step, near), me_near).wait_send()

    @pl.loop(1, ny)
    def _(step):
        y_copy(lax.rem(me_y + step, ny), me_y).wait_send()

    for step in around:
        side_copy(step).wait_send()

    for step in (1, 2, 3):
        to = lax.rem(me_x + step, NX)
        white_copy(to, me_x).wait_send()
        for chunk in range(CHUNKS):
            last_copy(chunk, to, me_x).wait_send()
    for chunk in range(CHUNKS):
        for kind in range(3):
            for way in range(2):
                z_copy(chunk, kind, way).wait_send()


def local(ny, record, offsets, sources):
    lag_rows = HALF // NZ
    own = lag_rows // NX
    upper, lower = forward_tables()
    inverse = inverse_table(NZ * NX * WIN)
    tables = np.concatenate([upper, lower, upper.T[:HALF], lower.T[:HALF], inverse], axis=0)
    vmem = pl.BlockSpec(memory_space=pltpu.VMEM)
    hbm = pl.BlockSpec(memory_space=pltpu.HBM)
    dma = pltpu.SemaphoreType.DMA
    flat = pl.pallas_call(
        functools.partial(kernel, ny),
        out_shape=jax.ShapeDtypeStruct((own, NSRC * ROWS), BF16),
        in_specs=[hbm, hbm, vmem, hbm],
        out_specs=vmem,
        scratch_shapes=[
            pltpu.SMEM((WIN,), jnp.int32),
            pltpu.SMEM((NSRC,), jnp.int32),
            pltpu.VMEM((SAMPLES, SAMPLES), BF16),
            pltpu.VMEM((SAMPLES, SAMPLES), BF16),
            pltpu.VMEM((HALF, SAMPLES), BF16),
            pltpu.VMEM((HALF, SAMPLES), BF16),
            pltpu.VMEM((HALF, SAMPLES), BF16),
            pltpu.VMEM((256, SAMPLES), BF16),
            pltpu.VMEM((2 * NLOW, 16, HALF), BF16),
            pltpu.VMEM((2 * NLOW, 16, HALF), BF16),
            pltpu.VMEM((ny, 16, HALF), BF16),
            pltpu.VMEM((2, NLOW * NX, 16, HALF), BF16),
            pltpu.VMEM((SAMPLES, 256), F32),
            pltpu.VMEM((NX, HALF, 128), BF16),
            pltpu.VMEM((NX, HALF, 128), BF16),
            pltpu.VMEM((8, 2, 2, 64, 128), BF16),
            pltpu.VMEM((HALF, 1024), BF16),
            pltpu.VMEM((CHUNKS, GROUPS, 256, 256), BF16),
            pltpu.VMEM((CHUNKS, 2, 33 * SKIP, 128), F32),
            pltpu.VMEM((SAMPLES, 512), BF16),
            pltpu.VMEM((CHUNKS, 3, lag_rows, WIDE), BF16),
            pltpu.VMEM((CHUNKS, 2, lag_rows // 2, WIDE), BF16),
            pltpu.VMEM((CHUNKS, 4, lag_rows // 2, WIDE), F32),
            pltpu.VMEM((CHUNKS, 3, 2, lag_rows // 2, WIDE), BF16),
            pltpu.VMEM((CHUNKS, lag_rows, WIDE), BF16),
            pltpu.VMEM((CHUNKS, NX, own, WIDE), BF16),
            dma((7,)),
            dma((2 * NLOW,)),
            dma((2 * NLOW,)),
            dma((ny,)),
            dma((ny,)),
            dma((2, NLOW * NX)),
            dma((2, NLOW * NX)),
            dma((NX,)),
            dma((NX,)),
            dma((CHUNKS, 3, 2)),
            dma((CHUNKS, 3, 2)),
            dma((CHUNKS, NX)),
            dma((CHUNKS, NX)),
        ],
        compiler_params=pltpu.CompilerParams(
            collective_id=0, has_side_effects=True, vmem_limit_bytes=53 * 1024 * 1024
        ),
        cost_estimate=pl.CostEstimate(
            flops=3 * 10**9, bytes_accessed=7 * 10**6, transcendentals=10**6
        ),
    )(
        offsets,
        sources,
        jnp.transpose(record, (1, 0, 2)),
        jnp.asarray(tables),
    )
    return flat.reshape(own, NSRC, ROWS)


def solution(mesh):
    ny = mesh.shape["chan"] // (2 * NLOW)
    in_specs = (P("chan", "spec", None), P("spec"), P())
    out_specs = P("spec", None, "chan")
    return jax.shard_map(
        functools.partial(local, ny),
        mesh=mesh,
        in_specs=in_specs,
        out_specs=out_specs,
        check_vma=False,
    )
```
